32 devices in a mesh: tm: 8 (over z, y), state: 4 (over x, core).
Axes of the slice: x: 2, y: 2, z: 4, core: 2. Of those that a mesh axis runs over, the one named last changes fastest.
Arguments:
- filtered_covariance: float32 [32, 512, 512], P('tm', 'state'), may hold values from -1 to 2.5, as said below
- pred_prec: float32 [32, 512, 512], P('tm', 'state'), may hold values from -1 to 3, as said below
- transition: float32 [512, 512], P('state'), may hold values from -1 to 1.5
- filt_means: float32 [32, 512], P('tm'), may hold values from -6 to 6
- terminal_mean: float32 [512], replicated, may hold values from -6 to 6
Outputs:
- smoothed: float32 [32, 512], P('tm', 'state')
The draws below stay inside these ranges and needn't reach their ends.
Inputs may be any that keep to these rules, and one draw needn't show every extreme that they name: `filtered_covariance`: each step's matrix is symmetric and positive definite. `pred_prec`: each step's matrix is symmetric and positive definite.
All inputs are finite; a program needn't handle non-finite values.
Results may differ from the reference program's by a relative error of at most 0.0003.
Values sent between devices are 32-bit elements; how exact they have to be, the bound alone decides.
No kernel may reach another device: no remote copies, remote signals or barrier semaphores. Data moves between devices by JAX's collectives and lax.ppermute only.
A program may use at most 128 MiB of HBM per device.

```python
import math
import jax
import jax.numpy as jnp
from jax import lax

D = 512
HORIZON_LENGTH = 32


coupling = 0.15


def shared_rates(key, slow_count):
    sampler_seeds = jax.random.split(key, 5)
    diag_trans = jax.random.uniform(sampler_seeds[0], (D,), jnp.float32, 0.9, 1.0)
    diag_cov = jax.random.uniform(sampler_seeds[1], (HORIZON_LENGTH, D), jnp.float32, 0.56, 1.75)
    slow_flags = jax.random.randint(sampler_seeds[2], (D,), 0, 8) < slow_count
    fast_rate = jax.random.uniform(sampler_seeds[3], (D,), jnp.float32, 0.94, 0.97)
    nominal_intensity = jnp.where(slow_flags, jnp.float32(0.1) ** (1.0 / HORIZON_LENGTH), fast_rate)
    spike_occurrences = jax.random.randint(sampler_seeds[4], (HORIZON_LENGTH, 1), 0, 64) == 0
    desired_quantity = nominal_intensity[None, :] * jnp.where(spike_occurrences, 0.6, 1.0)
    step_rate = jnp.sqrt(jnp.maximum(desired_quantity * desired_quantity - 0.1, 0.04))
    return (diag_trans, diag_cov, step_rate)


def symmetric_noise(key, scales):
    noise = jax.random.normal(key, (HORIZON_LENGTH, D, D), jnp.float32)
    paired = (noise + jnp.swapaxes(noise, 1, 2)) * jnp.float32(0.70710678)
    roots = jnp.sqrt(scales)
    factor = jnp.float32(coupling / math.sqrt(D))
    return factor * roots[:, :, None] * roots[:, None, :] * paired


def draw_filtered_covariance(key, part):
    diag_trans, diag_cov, step_rate = shared_rates(key, 4)
    key = jax.random.fold_in(key, 11)
    return diag_cov[:, :, None] * jnp.eye(D, dtype=jnp.float32) + symmetric_noise(key, diag_cov)


def draw_pred_prec(key, part):
    diag_trans, diag_cov, step_rate = shared_rates(key, 4)
    key = jax.random.fold_in(key, 12)
    diag_prec = step_rate / (diag_trans[None, :] * diag_cov)
    return diag_prec[:, :, None] * jnp.eye(D, dtype=jnp.float32) + symmetric_noise(key, diag_prec)


def draw_transition(key, part):
    diag_trans, diag_cov, step_rate = shared_rates(key, 4)
    key = jax.random.fold_in(key, 13)
    noise = jax.random.normal(key, (D, D), jnp.float32)
    return jnp.diag(diag_trans) + jnp.float32(coupling / math.sqrt(D)) * noise


def shard_levels(own_key, dims, pieces, smallest, top_value):
    loudness, own = 1.0, jax.random.fold_in(own_key, 6)
    for dim, shards_of in pieces:
        heights = jnp.exp(jax.random.uniform(jax.random.fold_in(own, dim), (shards_of,), jnp.float32, smallest / len(pieces), top_value / len(pieces)))
        loudness = loudness * jnp.repeat(heights, dims[dim] // shards_of).reshape([-1 if axis == dim else 1 for axis in range(len(dims))])
    return loudness


def centred(own_key, extent, deviation, reach, cuts=(), kind=jnp.bfloat16):
    result = deviation * jax.random.normal(own_key, extent, jnp.float32)
    if cuts:
        result = result * shard_levels(own_key, extent, cuts, -0.22, 0.18)
    return jnp.clip(result, -reach, reach).astype(kind)


def setup_inputs(seed: int = 0) -> dict:
    splits = jax.random.split(jax.random.key(seed), 6)
    return {
        "filtered_covariance": draw_filtered_covariance(jax.random.fold_in(splits[5], 71), 0),
        "pred_prec": draw_pred_prec(jax.random.fold_in(splits[5], 71), 0),
        "transition": draw_transition(jax.random.fold_in(splits[5], 71), 0),
        "filt_means": centred(splits[3], (HORIZON_LENGTH, D), 1.0, 6.0, ((0, 8),), jnp.float32),
        "terminal_mean": centred(splits[4], (D,), 1.0, 6.0, (), jnp.float32),
    }


HIGHEST = lax.Precision.HIGHEST


def reference(filtered_covariance, pred_prec, transition, filt_means, terminal_mean):
    pred_means = jnp.dot(filt_means, transition.T, precision=HIGHEST)

    def smooth_step(state_mean, element):
        covariance, precision, mean_now, mean_pred = element
        matrix_product = jnp.dot(covariance, transition.T, precision=HIGHEST)
        step_gain = jnp.dot(matrix_product, precision, precision=HIGHEST)
        offset = mean_now - jnp.dot(step_gain, mean_pred, precision=HIGHEST)
        updated = jnp.dot(step_gain, state_mean, precision=HIGHEST) + offset
        return updated, updated

    _, smoothed = lax.scan(smooth_step, terminal_mean.astype(jnp.float32),
                           (filtered_covariance, pred_prec, filt_means, pred_means), reverse=True)
    return smoothed
```

```python
import functools

import jax
import jax.numpy as jnp
from jax import lax
from jax.experimental import pallas as pl
from jax.experimental.pallas import tpu as pltpu
from jax.sharding import PartitionSpec as P

F32, BF16 = jnp.float32, jnp.bfloat16
NN = (((1,), (0,)), ((), ()))
NT = (((1,), (1,)), ((), ()))
ANY = pl.BlockSpec(memory_space=pl.ANY)
VMEM = pl.BlockSpec(memory_space=pltpu.VMEM)
LIMIT = 40 * 1024 * 1024


def split(x):
    high = x.astype(BF16)
    return high, (x - high.astype(F32)).astype(BF16)


def dot3(a, b, dims):
    (ah, al), (bh, bl) = split(a), split(b)
    dot = functools.partial(lax.dot_general, dimension_numbers=dims, preferred_element_type=F32)
    return dot(ah, bh) + (dot(ah, bl) + dot(al, bh))


def matvec(matrix, row):
    order = matrix.shape[1]
    total = matrix[:, :128] * row[:, :128]
    for j in range(128, order, 128):
        total += matrix[:, j : j + 128] * row[:, j : j + 128]
    return jnp.sum(total.T, axis=0, keepdims=True)


def gain_kernel(devices, repeat, *refs):
    half = devices // 2
    cov, prec, means, trans = refs[:4]
    arrived = refs[4 : 4 + devices - 1]
    gain, pred, pf, lf, af, sems = refs[4 + devices - 1 :]
    panel, order = cov.shape[1:]
    wide = order // 2
    s = lax.axis_index("state")
    side = s // half
    step = s // repeat

    copies = []

    def start(source, target):
        copy = pltpu.make_async_copy(source, target, sems.at[len(copies)])
        copy.start()
        copies.append(copy)

    def rows(i):
        return pl.ds(pl.multiple_of(i * panel, panel), panel)

    other = pl.multiple_of((1 - side) * wide, wide)
    own = pl.multiple_of(side * wide, wide)
    start(trans, af)
    start(cov.at[step], pf.at[rows(s), :])
    start(prec.at[step], lf.at[rows(s), :])
    for off in range(1, devices):
        i = s ^ off
        for which, full in enumerate((pf, lf)):
            place = full.at[rows(i), :] if off < half else full.at[rows(i), pl.ds(other, wide)]
            start(arrived[off - 1].at[which], place)
    steps = means.shape[0]
    pf[order:, :] = jnp.concatenate([means[...], jnp.zeros((16 - steps, order), F32)], axis=0)
    for copy in copies:
        copy.wait()
    for full in (pf, lf):
        full[pl.ds(other, wide), pl.ds(own, wide)] = full[pl.ds(own, wide), pl.ds(other, wide)].T
    cov_trans = dot3(pf[...], af[...], NT)
    pred[...] = cov_trans[order : order + 8]
    gain[...] = dot3(cov_trans[:order], lf[...], NN)


def pair_kernel(repeat, own, partner, means, pred, c_ref, late_ref, vec_ref, slots, sems):
    step = lax.axis_index("state") // repeat
    bit = step % 2
    first = pltpu.make_async_copy(own, slots.at[bit], sems.at[0])
    second = pltpu.make_async_copy(partner, slots.at[1 - bit], sems.at[1])
    first.start()
    second.start()
    a = step - bit
    mean_a, mean_b = means[pl.ds(a, 1), :], means[pl.ds(a + 1, 1), :]
    pred_a, pred_b = pred[pl.ds(a, 1), :], pred[pl.ds(a + 1, 1), :]
    first.wait()
    second.wait()
    ga, gb = slots[0], slots[1]
    vec_ref[...] = jnp.concatenate(
        [mean_a + matvec(ga, mean_b - pred_a), mean_b, pred_b, jnp.zeros((5, ga.shape[1]), F32)], axis=0
    )
    c_ref[...] = dot3(ga, gb, NN)
    late_ref[...] = gb


def hop_kernel(x_ref, c_ref, vec_ref, out_ref):
    vec = vec_ref[...]
    out_ref[...] = vec[0:1] + matvec(c_ref[...], x_ref[...] - vec[2:3])


def last_kernel(x_ref, c_ref, late_ref, vec_ref, out_ref):
    vec = vec_ref[...]
    gap = x_ref[...] - vec[2:3]
    out_ref[0:1, :] = vec[0:1] + matvec(c_ref[...], gap)
    out_ref[1:2, :] = vec[1:2] + matvec(late_ref[...], gap)


def params():
    return pltpu.CompilerParams(vmem_limit_bytes=LIMIT)


def local(filtered_covariance, pred_prec, transition, filt_means, terminal_mean):
    steps, panel, order = filtered_covariance.shape
    devices, blocks = lax.axis_size("state"), lax.axis_size("tm")
    repeat, half, wide = devices // steps, devices // 2, order // 2
    s, b = lax.axis_index("state"), lax.axis_index("tm")
    side = s // half

    def swap(x, off):
        return lax.ppermute(x, "state", [(i, i ^ off) for i in range(devices)])

    across = swap(transition, half)
    both = jnp.stack([transition, across])
    parts = [both] + [swap(both, off) for off in range(1, half)]
    parts = jnp.concatenate(parts, axis=0).reshape(half, 2, panel, order)
    full = jnp.zeros((devices, panel, order), F32)
    for o in range(half):
        for h in range(2):
            full = lax.dynamic_update_slice_in_dim(full, parts[o, h][None], s ^ o ^ (h * half), 0)
    trans = full.reshape(order, order)

    arrived = []
    for off in range(1, devices):
        target = (s ^ off) // repeat
        piece = [lax.dynamic_index_in_dim(m, target, 0, False) for m in (filtered_covariance, pred_prec)]
        if off >= half:
            piece = [lax.dynamic_slice_in_dim(m, side * wide, wide, 1) for m in piece]
        arrived.append(swap(jnp.stack(piece), off))

    count = 3 + 2 * (devices - 1)
    gain, pred = pl.pallas_call(
        functools.partial(gain_kernel, devices, repeat),
        out_shape=(jax.ShapeDtypeStruct((order, order), F32), jax.ShapeDtypeStruct((8, order), F32)),
        in_specs=[ANY, ANY, VMEM, ANY] + [ANY] * (devices - 1),
        out_specs=(VMEM, VMEM),
        scratch_shapes=[
            pltpu.VMEM((order + 16, order), F32),
            pltpu.VMEM((order, order), F32),
            pltpu.VMEM((order, order), F32),
            pltpu.SemaphoreType.DMA((count,)),
        ],
        compiler_params=params(),
        name="gain",
    )(filtered_covariance, pred_prec, filt_means, trans, *arrived)

    partner = swap(gain, repeat)
    c, late, vec = pl.pallas_call(
        functools.partial(pair_kernel, repeat),
        out_shape=(
            jax.ShapeDtypeStruct((order, order), F32),
            jax.ShapeDtypeStruct((order, order), F32),
            jax.ShapeDtypeStruct((8, order), F32),
        ),
        in_specs=[ANY, ANY, VMEM, VMEM],
        out_specs=(VMEM, VMEM, VMEM),
        scratch_shapes=[pltpu.VMEM((2, order, order), F32), pltpu.SemaphoreType.DMA((2,))],
        compiler_params=params(),
        name="pair",
    )(gain, partner, filt_means, pred)

    hop = pl.pallas_call(
        hop_kernel,
        out_shape=jax.ShapeDtypeStruct((1, order), F32),
        in_specs=[VMEM] * 3,
        out_specs=VMEM,
        compiler_params=params(),
        name="hop",
    )

    def flat(tm, state):
        return tm * devices + state

    lower, upper = range(half), range(half, devices)
    start = jnp.where((b == blocks - 1) & (side == 1), terminal_mean, 0.0)[None]
    incoming, total = start, start
    for tm in range(blocks - 1, -1, -1):
        for to, members in ((tm, upper), (tm - 1, lower)):
            if to < 0:
                break
            pairs = [(flat(tm, i), flat(to, i ^ half)) for i in members]
            incoming = lax.ppermute(hop(incoming, c, vec), ("tm", "state"), pairs)
            total = total + incoming

    both = pl.pallas_call(
        last_kernel,
        out_shape=jax.ShapeDtypeStruct((2, order), F32),
        in_specs=[VMEM] * 4,
        out_specs=VMEM,
        compiler_params=params(),
        name="last",
    )(total, c, late, vec)
    theirs = swap(lax.dynamic_slice_in_dim(both, (s ^ half) * panel, panel, 1), half)
    mine = lax.dynamic_slice_in_dim(both, s * panel, panel, 1)
    return jnp.where(
        side == 0, jnp.concatenate([mine, theirs], axis=0), jnp.concatenate([theirs, mine], axis=0)
    )


def solution(mesh):
    return jax.shard_map(
        local,
        mesh=mesh,
        in_specs=(
            P("tm", "state", None),
            P("tm", "state", None),
            P("state", None),
            P("tm", None),
            P(),
        ),
        out_specs=P("tm", "state"),
        check_vma=False,
    )
```

```python
import functools

import jax
import jax.numpy as jnp
from jax import lax
from jax.experimental import pallas as pl
from jax.experimental.pallas import tpu as pltpu
from jax.sharding import PartitionSpec as P

F32, BF16 = jnp.float32, jnp.bfloat16
NN = (((1,), (0,)), ((), ()))
NT = (((1,), (1,)), ((), ()))
ANY = pl.BlockSpec(memory_space=pl.ANY)
HBM = pl.BlockSpec(memory_space=pltpu.HBM)
VMEM = pl.BlockSpec(memory_space=pltpu.VMEM)


def split(x):
    high = x.astype(BF16)
    return high, (x - high.astype(F32)).astype(BF16)


def dot3(a, b, dims):
    (ah, al), (bh, bl) = split(a), split(b)
    dot = functools.partial(lax.dot_general, dimension_numbers=dims, preferred_element_type=F32)
    return dot(ah, bh) + (dot(ah, bl) + dot(al, bh))


def matvec(matrix, row):
    order = matrix.shape[1]
    total = matrix[:, :128] * row[:, :128]
    for j in range(128, order, 128):
        total += matrix[:, j : j + 128] * row[:, j : j + 128]
    return jnp.sum(total.T, axis=0, keepdims=True)


def rows(i, panel):
    return pl.ds(pl.multiple_of(i * panel, panel), panel)


def starter(sems):
    copies = []

    def start(source, target):
        copy = pltpu.make_async_copy(source, target, sems.at[len(copies)])
        copy.start()
        copies.append(copy)

    return start, copies


def width(devices, panel, order, off):
    if off < devices // 2:
        return order
    return panel if off == devices - 1 and panel % 128 == 0 else order // 2


def pack_kernel(devices, repeat, cov, prec, *refs):
    outs, sems = refs[:-1], refs[-1]
    panel, order = cov.shape[1:]
    half, wide = devices // 2, order // 2
    s = lax.axis_index("state")
    start, copies = starter(sems)
    for off in list(range(half, devices)) + list(range(1, half)):
        step = (s ^ off) // repeat
        w = width(devices, panel, order, off)
        for which, matrix in enumerate((cov, prec)):
            if w == order:
                source = matrix.at[step]
            else:
                first = pl.multiple_of((s // half) * wide if w == wide else s * panel, w)
                source = matrix.at[step, :, pl.ds(first, w)]
            start(source, outs[off - 1].at[which])
    for copy in copies:
        copy.wait()


def gain_kernel(devices, repeat, *refs):
    half = devices // 2
    cov, prec, means, trans, across = refs[:5]
    near, far = refs[5 : 5 + half - 1], refs[4 + half : 4 + half + half - 1]
    arrived = refs[3 + 2 * half : 3 + 2 * half + devices - 1]
    gain, pred, pf, lf, af, sems = refs[3 + 2 * half + devices - 1 :]
    panel, order = cov.shape[1:]
    wide = order // 2
    s = lax.axis_index("state")
    side = s // half
    step = s // repeat
    start, copies = starter(sems)
    other = pl.multiple_of((1 - side) * wide, wide)
    own = pl.multiple_of(side * wide, wide)
    start(trans, af.at[rows(s, panel), :])
    start(across, af.at[rows(s ^ half, panel), :])
    for off in range(1, half):
        start(near[off - 1], af.at[rows(s ^ off, panel), :])
        start(far[off - 1], af.at[rows(s ^ off ^ half, panel), :])
    start(cov.at[step], pf.at[rows(s, panel), :])
    start(prec.at[step], lf.at[rows(s, panel), :])
    for off in range(1, devices):
        i = s ^ off
        w = width(devices, panel, order, off)
        for which, full in enumerate((pf, lf)):
            place = full.at[rows(i, panel), :]
            if w < order:
                first = other if w == wide else pl.multiple_of(i * panel, panel)
                place = full.at[rows(i, panel), pl.ds(first, w)]
            start(arrived[off - 1].at[which], place)
    steps = means.shape[0]
    pf[order:, :] = jnp.concatenate([means[...], jnp.zeros((16 - steps, order), F32)], axis=0)
    for copy in copies:
        copy.wait()
    for full in (pf, lf):
        full[pl.ds(other, wide), pl.ds(own, wide)] = full[pl.ds(own, wide), pl.ds(other, wide)].T
        if width(devices, panel, order, devices - 1) < wide:
            i = s ^ (devices - 1)
            for off in range(half, devices - 1):
                j = s ^ off
                full[rows(i, panel), rows(j, panel)] = full[rows(j, panel), rows(i, panel)].T
    cov_trans = dot3(pf[...], af[...], NT)
    pred[...] = cov_trans[order : order + 8]
    gain[...] = dot3(cov_trans[:order], lf[...], NN)


def pair_kernel(repeat, own, partner, means, pred, c_ref, late_ref, vec_ref, slots, sems):
    step = lax.axis_index("state") // repeat
    bit = step % 2
    first = pltpu.make_async_copy(own, slots.at[bit], sems.at[0])
    second = pltpu.make_async_copy(partner, slots.at[1 - bit], sems.at[1])
    first.start()
    second.start()
    a = step - bit
    mean_a, mean_b = means[pl.ds(a, 1), :], means[pl.ds(a + 1, 1), :]
    pred_a, pred_b = pred[pl.ds(a, 1), :], pred[pl.ds(a + 1, 1), :]
    first.wait()
    second.wait()
    ga, gb = slots[0], slots[1]
    vec_ref[...] = jnp.concatenate(
        [mean_a + matvec(ga, mean_b - pred_a), mean_b, pred_b, jnp.zeros((5, ga.shape[1]), F32)], axis=0
    )
    c_ref[...] = dot3(ga, gb, NN)
    late_ref[...] = gb


def hop_kernel(x_ref, c_ref, vec_ref, out_ref):
    vec = vec_ref[...]
    out_ref[...] = vec[0:1] + matvec(c_ref[...], x_ref[...] - vec[2:3])


def last_kernel(x_ref, c_ref, late_ref, vec_ref, out_ref):
    vec = vec_ref[...]
    gap = x_ref[...] - vec[2:3]
    out_ref[0:1, :] = vec[0:1] + matvec(c_ref[...], gap)
    out_ref[1:2, :] = vec[1:2] + matvec(late_ref[...], gap)


def params(mebibytes):
    return pltpu.CompilerParams(vmem_limit_bytes=mebibytes * 2**20)


def local(filtered_covariance, pred_prec, transition, filt_means, terminal_mean):
    steps, panel, order = filtered_covariance.shape
    devices, blocks = lax.axis_size("state"), lax.axis_size("tm")
    repeat, half, wide = devices // steps, devices // 2, order // 2
    s, b = lax.axis_index("state"), lax.axis_index("tm")
    side = s // half

    def swap(x, off):
        return lax.ppermute(x, "state", [(i, i ^ off) for i in range(devices)])

    across = swap(transition, half)
    near = [swap(transition, off) for off in range(1, half)]

    widths = [width(devices, panel, order, off) for off in range(1, devices)]
    pieces = pl.pallas_call(
        functools.partial(pack_kernel, devices, repeat),
        out_shape=[jax.ShapeDtypeStruct((2, panel, w), F32) for w in widths],
        in_specs=[HBM, HBM],
        out_specs=[VMEM] * (devices - 1),
        scratch_shapes=[pltpu.SemaphoreType.DMA((2 * devices - 2,))],
        compiler_params=params(4),
        name="pack",
    )(filtered_covariance, pred_prec)
    arrived = [swap(piece, off) for off, piece in enumerate(pieces, 1)]
    far = [swap(across, off) for off in range(1, half)]

    gain, pred = pl.pallas_call(
        functools.partial(gain_kernel, devices, repeat),
        out_shape=(jax.ShapeDtypeStruct((order, order), F32), jax.ShapeDtypeStruct((8, order), F32)),
        in_specs=[HBM, HBM, VMEM, HBM] + [ANY] * (2 * half + devices - 2),
        out_specs=(VMEM, VMEM),
        scratch_shapes=[
            pltpu.VMEM((order + 16, order), F32),
            pltpu.VMEM((order, order), F32),
            pltpu.VMEM((order, order), F32),
            pltpu.SemaphoreType.DMA((2 * half + 2 * devices,)),
        ],
        compiler_params=params(16),
        name="gain",
    )(filtered_covariance, pred_prec, filt_means, transition, across, *near, *far, *arrived)

    partner = swap(gain, repeat)
    c, late, vec = pl.pallas_call(
        functools.partial(pair_kernel, repeat),
        out_shape=(
            jax.ShapeDtypeStruct((order, order), F32),
            jax.ShapeDtypeStruct((order, order), F32),
            jax.ShapeDtypeStruct((8, order), F32),
        ),
        in_specs=[ANY, ANY, VMEM, VMEM],
        out_specs=(VMEM, VMEM, VMEM),
        scratch_shapes=[pltpu.VMEM((2, order, order), F32), pltpu.SemaphoreType.DMA((2,))],
        compiler_params=params(12),
        name="pair",
    )(gain, partner, filt_means, pred)

    hop = pl.pallas_call(
        hop_kernel,
        out_shape=jax.ShapeDtypeStruct((1, order), F32),
        in_specs=[VMEM] * 3,
        out_specs=VMEM,
        compiler_params=params(6),
        name="hop",
    )

    everyone = range(blocks * devices)
    lead = (half - 1, devices - 1)
    start = jnp.where((b == blocks - 1) & (s == lead[1]), terminal_mean, 0.0)[None]
    arrives = [(tm, h) for tm in range(blocks - 1, -1, -1) for h in (1, 0)]
    incoming, total = start, start
    for (tm, h), (to, g) in zip(arrives, arrives[1:]):
        u, v = tm * devices + lead[h], to * devices + lead[g]
        change = {u: v, v: u}
        swapped = lax.ppermute(hop(incoming, c, vec), ("tm", "state"), [(i, change.get(i, i)) for i in everyone])
        incoming = swapped
        total = jnp.where((b == to) & (s == lead[g]), swapped, total)

    both = pl.pallas_call(
        last_kernel,
        out_shape=jax.ShapeDtypeStruct((2, order), F32),
        in_specs=[VMEM] * 4,
        out_specs=VMEM,
        compiler_params=params(6),
        name="last",
    )(total, c, late, vec)

    def columns(i):
        return lax.dynamic_slice_in_dim(both, i * panel, panel, 1)

    theirs = [columns(s)] + [swap(columns(s ^ off), off) for off in range(1, devices)]
    away = [s ^ lead[h] for h in range(2)]
    return jnp.concatenate([sum(jnp.where(a == off, x, 0.0) for off, x in enumerate(theirs)) for a in away], axis=0)


def solution(mesh):
    return jax.shard_map(
        local,
        mesh=mesh,
        in_specs=(
            P("tm", "state", None),
            P("tm", "state", None),
            P("state", None),
            P("tm", None),
            P(),
        ),
        out_specs=P("tm", "state"),
        check_vma=False,
    )
```

```python
import functools

import jax
import jax.numpy as jnp
from jax import lax
from jax.experimental import pallas as pl
from jax.experimental.pallas import tpu as pltpu
from jax.sharding import PartitionSpec as P

F32, BF16 = jnp.float32, jnp.bfloat16
NN = (((1,), (0,)), ((), ()))
NT = (((1,), (1,)), ((), ()))
ANY = pl.BlockSpec(memory_space=pl.ANY)
HBM = pl.BlockSpec(memory_space=pltpu.HBM)
VMEM = pl.BlockSpec(memory_space=pltpu.VMEM)


def split(x):
    high = x.astype(BF16)
    return high, (x - high.astype(F32)).astype(BF16)


def dot3(a, b, dims):
    (ah, al), (bh, bl) = split(a), split(b)
    dot = functools.partial(lax.dot_general, dimension_numbers=dims, preferred_element_type=F32)
    return dot(ah, bh) + (dot(ah, bl) + dot(al, bh))


def matvec(matrix, row):
    order = matrix.shape[1]
    total = matrix[:, :128] * row[:, :128]
    for j in range(128, order, 128):
        total += matrix[:, j : j + 128] * row[:, j : j + 128]
    return jnp.sum(total.T, axis=0, keepdims=True)


def rows(i, panel):
    return pl.ds(pl.multiple_of(i * panel, panel), panel)


def starter(sems):
    copies = []

    def start(source, target):
        copy = pltpu.make_async_copy(source, target, sems.at[len(copies)])
        copy.start()
        copies.append(copy)

    return start, copies


def width(devices, panel, order, off):
    if off < devices // 2:
        return order
    return panel if off == devices - 1 and panel % 128 == 0 else order // 2


def place():
    b, s, half = lax.axis_index("tm"), lax.axis_index("state"), lax.axis_size("state") // 2
    return b, s, s ^ ((b % 2) * half)


def owned(b, s, repeat):
    return (s ^ ((b % 2) * (lax.axis_size("state") // 2))) // repeat


def pack_kernel(devices, repeat, cov, prec, trans, terminal, *refs):
    pieces, trans_half, first, sems = refs[: devices - 1], *refs[devices - 1 :]
    panel, order = cov.shape[1:]
    half, wide = devices // 2, order // 2
    b, s, _ = place()
    start, copies = starter(sems)
    start(trans.at[pl.ds(pl.multiple_of((b % 2) * (panel // 2), panel // 2), panel // 2), :], trans_half)
    for off in list(range(half, devices)) + list(range(1, half)):
        step = owned(b, s ^ off, repeat)
        w = width(devices, panel, order, off)
        for which, matrix in enumerate((cov, prec)):
            if w == order:
                source = matrix.at[step]
            else:
                column = pl.multiple_of((s // half) * wide if w == wide else s * panel, w)
                source = matrix.at[step, :, pl.ds(column, w)]
            start(source, pieces[off - 1].at[which])
    first[...] = jnp.where(b == lax.axis_size("tm") - 1, terminal[...], 0.0)
    for copy in copies:
        copy.wait()


def gain_kernel(devices, repeat, *refs):
    half = devices // 2
    cov, prec, means, trans, across, around = refs[:6]
    near = refs[6 : 6 + 3 * (half - 1)]
    arrived = refs[6 + 3 * (half - 1) : 5 + 3 * (half - 1) + devices]
    gain, info, pf, lf, af, sems = refs[5 + 3 * (half - 1) + devices :]
    steps, panel, order = cov.shape
    wide = order // 2
    b, s, _ = place()
    side = s // half
    step = owned(b, s, repeat)
    start, copies = starter(sems)
    other = pl.multiple_of((1 - side) * wide, wide)
    own = pl.multiple_of(side * wide, wide)

    def halves(i):
        first = i * panel + (b % 2) * (panel // 2)
        second = i * panel + (1 - b % 2) * (panel // 2)
        return [af.at[pl.ds(pl.multiple_of(at, panel // 2), panel // 2), :] for at in (first, second)]

    start(trans, af.at[rows(s, panel), :])
    for piece, target in zip((across, around), halves(s ^ half)):
        start(piece, target)
    for off in range(1, half):
        mine, one, two = near[3 * off - 3 : 3 * off]
        start(mine, af.at[rows(s ^ off, panel), :])
        for piece, target in zip((one, two), halves(s ^ off ^ half)):
            start(piece, target)
    start(means, pf.at[pl.ds(order, steps), :])
    start(cov.at[step], pf.at[rows(s, panel), :])
    start(prec.at[step], lf.at[rows(s, panel), :])
    for off in range(1, devices):
        i = s ^ off
        w = width(devices, panel, order, off)
        for which, full in enumerate((pf, lf)):
            target = full.at[rows(i, panel), :]
            if w < order:
                column = other if w == wide else pl.multiple_of(i * panel, panel)
                target = full.at[rows(i, panel), pl.ds(column, w)]
            start(arrived[off - 1].at[which], target)
    pf[order + 8 :, :] = jnp.zeros((8, order), F32)
    for copy in copies:
        copy.wait()
    pf[order + steps : order + 8, :] = jnp.zeros((8 - steps, order), F32)
    for full in (pf, lf):
        full[pl.ds(other, wide), pl.ds(own, wide)] = full[pl.ds(own, wide), pl.ds(other, wide)].T
        if width(devices, panel, order, devices - 1) < wide:
            i = s ^ (devices - 1)
            for off in range(half, devices - 1):
                j = s ^ off
                full[rows(i, panel), rows(j, panel)] = full[rows(j, panel), rows(i, panel)].T
    cov_trans = dot3(pf[...], af[...], NT)
    info[:8] = pf[order : order + 8, :]
    info[8:] = cov_trans[order : order + 8]
    gain[...] = dot3(cov_trans[:order], lf[...], NN)


def pair_kernel(repeat, own, partner, info, c_ref, late_ref, vec_ref, slots, sems):
    b, s, _ = place()
    step = owned(b, s, repeat)
    bit = step % 2
    first = pltpu.make_async_copy(own, slots.at[bit], sems.at[0])
    second = pltpu.make_async_copy(partner, slots.at[1 - bit], sems.at[1])
    first.start()
    second.start()
    a = step - bit
    mean_a, mean_b = info[pl.ds(a, 1), :], info[pl.ds(a + 1, 1), :]
    pred_a, pred_b = info[pl.ds(a + 8, 1), :], info[pl.ds(a + 9, 1), :]
    first.wait()
    second.wait()
    ga, gb = slots[0], slots[1]
    vec_ref[...] = jnp.concatenate(
        [mean_a + matvec(ga, mean_b - pred_a), mean_b, pred_b, jnp.zeros((5, ga.shape[1]), F32)], axis=0
    )
    c_ref[...] = dot3(ga, gb, NN)
    late_ref[...] = gb


def hop_kernel(x_ref, c_ref, vec_ref, out_ref):
    vec = vec_ref[...]
    out_ref[...] = vec[0:1] + matvec(c_ref[...], x_ref[...] - vec[2:3])


def last_kernel(devices, *refs):
    incoming, (c_ref, late_ref, vec_ref, mine_ref, theirs_ref, both) = refs[:-6], refs[-6:]
    panel = mine_ref.shape[1]
    half = devices // 2
    b, s, t = place()
    arrival = 2 * (lax.axis_size("tm") - 1 - b) + 1 - t // half
    x = incoming[0][...]
    for k, ref in enumerate(incoming[1:], 1):
        x = jnp.where(arrival == k, ref[...], x)
    vec = vec_ref[...]
    gap = x - vec[2:3]
    full = jnp.concatenate(
        [vec[0:1] + matvec(c_ref[...], gap), vec[1:2] + matvec(late_ref[...], gap)], axis=0
    )
    for i in range(devices):
        both[i] = full[:, i * panel : (i + 1) * panel]
    mine_ref[...] = both[s]
    theirs_ref[...] = both[s ^ half ^ 1]


def out_kernel(devices, mine_ref, theirs_ref, out_ref):
    _, _, t = place()
    low = t < devices // 2
    mine, theirs = mine_ref[...], theirs_ref[...]
    out_ref[...] = jnp.concatenate([jnp.where(low, mine, theirs), jnp.where(low, theirs, mine)], axis=0)


def params(mebibytes):
    return pltpu.CompilerParams(vmem_limit_bytes=mebibytes * 2**20)


def local(filtered_covariance, pred_prec, transition, filt_means, terminal_mean):
    steps, panel, order = filtered_covariance.shape
    devices, blocks = lax.axis_size("state"), lax.axis_size("tm")
    repeat, half = devices // steps, devices // 2

    def swap(x, off):
        return lax.ppermute(x, "state", [(i, i ^ off) for i in range(devices)])

    def swap_blocks(x, off):
        return lax.ppermute(x, "tm", [(i, i ^ off) for i in range(blocks)])

    def shape(*dims):
        return jax.ShapeDtypeStruct(dims, F32)

    cov, prec, trans, means = (
        pltpu.with_memory_space_constraint(x, pltpu.HBM)
        for x in (filtered_covariance, pred_prec, transition, filt_means)
    )
    widths = [width(devices, panel, order, off) for off in range(1, devices)]
    *pieces, trans_half, first = pl.pallas_call(
        functools.partial(pack_kernel, devices, repeat),
        out_shape=[shape(2, panel, w) for w in widths] + [shape(panel // 2, order), shape(1, order)],
        in_specs=[HBM, HBM, HBM, VMEM],
        out_specs=[VMEM] * (devices + 1),
        scratch_shapes=[pltpu.SemaphoreType.DMA((2 * devices,))],
        compiler_params=params(4),
        name="pack",
    )(cov, prec, trans, terminal_mean[None])

    across = swap(trans_half, half)
    arrived = [swap(piece, off) for off, piece in enumerate(pieces, 1)]
    around = swap_blocks(across, 1)
    near = [swap(x, off) for off in range(1, half) for x in (transition, across, around)]

    gain, info = pl.pallas_call(
        functools.partial(gain_kernel, devices, repeat),
        out_shape=(shape(order, order), shape(16, order)),
        in_specs=[HBM] * 4 + [ANY] * (2 + len(near) + len(arrived)),
        out_specs=(VMEM, VMEM),
        scratch_shapes=[
            pltpu.VMEM((order + 16, order), F32),
            pltpu.VMEM((order, order), F32),
            pltpu.VMEM((order, order), F32),
            pltpu.SemaphoreType.DMA((6 + len(near) + 2 * len(arrived),)),
        ],
        compiler_params=params(16),
        name="gain",
    )(cov, prec, means, trans, across, around, *near, *arrived)

    partner = swap(gain, repeat)
    c, late, vec = pl.pallas_call(
        functools.partial(pair_kernel, repeat),
        out_shape=(shape(order, order), shape(order, order), shape(8, order)),
        in_specs=[ANY, ANY, VMEM],
        out_specs=(VMEM, VMEM, VMEM),
        scratch_shapes=[pltpu.VMEM((2, order, order), F32), pltpu.SemaphoreType.DMA((2,))],
        compiler_params=params(12),
        name="pair",
    )(gain, partner, info)

    hop = pl.pallas_call(
        hop_kernel,
        out_shape=shape(1, order),
        in_specs=[VMEM] * 3,
        out_specs=VMEM,
        compiler_params=params(4),
        name="hop",
    )
    incoming = [first]
    for block in range(blocks - 1, -1, -1):
        incoming.append(swap(hop(incoming[-1], c, vec), half ^ 1))
        if block:
            incoming.append(swap_blocks(hop(incoming[-1], c, vec), block ^ (block - 1)))

    mine, theirs = pl.pallas_call(
        functools.partial(last_kernel, devices),
        out_shape=(shape(2, panel), shape(2, panel)),
        in_specs=[VMEM] * (len(incoming) + 3),
        out_specs=(VMEM, VMEM),
        scratch_shapes=[pltpu.VMEM((devices, 2, panel), F32)],
        compiler_params=params(6),
        name="last",
    )(*incoming, c, late, vec)
    return pl.pallas_call(
        functools.partial(out_kernel, devices),
        out_shape=shape(steps, panel),
        in_specs=[VMEM, VMEM],
        out_specs=VMEM,
        compiler_params=params(4),
        name="out",
    )(mine, swap(theirs, half ^ 1))


def solution(mesh):
    return jax.shard_map(
        local,
        mesh=mesh,
        in_specs=(
            P("tm", "state", None),
            P("tm", "state", None),
            P("state", None),
            P("tm", None),
            P(),
        ),
        out_specs=P("tm", "state"),
        check_vma=False,
    )
```

```python
import functools

import jax
import jax.numpy as jnp
from jax import lax
from jax.experimental import pallas as pl
from jax.experimental.pallas import tpu as pltpu
from jax.sharding import PartitionSpec as P

F32, BF16 = jnp.float32, jnp.bfloat16
NN = (((1,), (0,)), ((), ()))
NT = (((1,), (1,)), ((), ()))
ANY = pl.BlockSpec(memory_space=pl.ANY)
HBM = pl.BlockSpec(memory_space=pltpu.HBM)
VMEM = pl.BlockSpec(memory_space=pltpu.VMEM)


def split(x):
    high = x.astype(BF16)
    return high, (x - high.astype(F32)).astype(BF16)


def dot3(a, b, dims):
    (ah, al), (bh, bl) = split(a), split(b)
    dot = functools.partial(lax.dot_general, dimension_numbers=dims, preferred_element_type=F32)
    return dot(ah, bh) + (dot(ah, bl) + dot(al, bh))


def matvec(matrix, row):
    order = matrix.shape[1]
    total = matrix[:, :128] * row[:, :128]
    for j in range(128, order, 128):
        total += matrix[:, j : j + 128] * row[:, j : j + 128]
    return jnp.sum(total.T, axis=0, keepdims=True)


def rows(i, panel):
    return pl.ds(pl.multiple_of(i * panel, panel), panel)


def starter(sems):
    copies = []

    def start(source, target):
        copy = pltpu.make_async_copy(source, target, sems.at[len(copies)])
        copy.start()
        copies.append(copy)

    return start, copies


def width(devices, panel, order, off):
    if off < 2:
        return order
    return panel if devices == 4 and off == 3 and panel % 128 == 0 else order - 2 * panel


def pack_kernel(devices, cov, prec, trans, terminal, *refs):
    pieces, trans_half, first, vector, sems = refs[: 2 * devices - 4], *refs[2 * devices - 4 :]
    steps, panel, order = cov.shape
    b, s = lax.axis_index("tm"), lax.axis_index("state")
    start, copies = starter(sems)
    start(terminal, vector)
    start(trans.at[pl.ds(pl.multiple_of((b % 2) * (panel // 2), panel // 2), panel // 2), :], trans_half)
    for which, matrix in enumerate((cov, prec)):
        for off in range(2, devices):
            mine = pl.ds(((s ^ off) % 2) * (steps // 2), steps // 2)
            w = width(devices, panel, order, off)
            column = 2 * panel if w == order - 2 * panel else pl.multiple_of(s * panel, panel)
            start(matrix.at[mine, :, pl.ds(column, w)], pieces[which * (devices - 2) + off - 2])
    copies[0].wait()
    first[...] = jnp.where(b == lax.axis_size("tm") - 1, vector[...], 0.0)
    for copy in copies[1:]:
        copy.wait()


def load_kernel(cov, prec, trans, means, after, near_cov, near_prec, own_cov, own_prec, own_trans, own_means, sems):
    count = cov.shape[0] // 2
    s = lax.axis_index("state")
    start, copies = starter(sems)
    for matrix, near, own in ((cov, near_cov, own_cov), (prec, near_prec, own_prec)):
        start(matrix.at[pl.ds((1 - s % 2) * count, count)], near)
        start(matrix.at[pl.ds((s % 2) * count, count)], own)
    start(trans, own_trans)
    start(means, own_means)
    for copy in copies:
        copy.wait()


def assemble(devices, start, full, k, own, arrived):
    panel, order = own.shape[1:]
    s = lax.axis_index("state")
    start(own.at[k], full.at[rows(s, panel), :])
    for off, piece in enumerate(arrived, 1):
        i = s ^ off
        w = width(devices, panel, order, off)
        target = full.at[rows(i, panel), :]
        if w < order:
            column = 2 * panel if w == order - 2 * panel else pl.multiple_of(i * panel, panel)
            target = full.at[rows(i, panel), pl.ds(column, w)]
        start(piece.at[k], target)


def mirror(devices, full, panel, order):
    s, known = lax.axis_index("state"), 2 * panel
    full[known:order, :known] = full[:known, known:order].T
    if width(devices, panel, order, 3) < order - known:
        i, j = s ^ 3, s ^ 2
        full[rows(i, panel), rows(j, panel)] = full[rows(j, panel), rows(i, panel)].T


def cov_kernel(devices, *refs):
    own, means, trans, *arrived = refs[: 2 + devices]
    moved = refs[2 + devices : -5]
    out, info, pf, af, sems = refs[-5:]
    count, panel, order = own.shape
    steps = means.shape[0]
    b, s = lax.axis_index("tm"), lax.axis_index("state")
    start, copies = starter(sems)
    for k in range(count):
        assemble(devices, start, pf.at[pl.ds(k * order, order), :], k, own, arrived)
    start(trans, af.at[rows(s, panel), :])
    start(moved[0], af.at[rows(s ^ 1, panel), :])
    spots = [(off ^ near, half) for off in range(2, devices, 2) for near in range(2) for half in range(2)]
    for piece, (off, half) in zip(moved[1:], spots):
        at = (s ^ off) * panel + (b % 2 if half == 0 else 1 - b % 2) * (panel // 2)
        start(piece, af.at[pl.ds(pl.multiple_of(at, panel // 2), panel // 2), :])
    pf[count * order :, :] = jnp.concatenate([means[...], jnp.zeros((16 - steps, order), F32)], axis=0)
    for copy in copies:
        copy.wait()
    for k in range(count):
        mirror(devices, pf.at[pl.ds(k * order, order), :], panel, order)
    product = dot3(pf[...], af[...], NT)
    out[...] = product[: count * order]
    info[:8] = pf[count * order : count * order + 8, :]
    info[8:] = product[count * order : count * order + 8]


def gain_kernel(devices, *refs):
    cov_trans, info, own, *arrived = refs[: 2 + devices]
    map_ref, late_ref, lf, sems = refs[2 + devices :]
    count, panel, order = own.shape
    s = lax.axis_index("state")
    start, copies = starter(sems)
    for k in range(count):
        assemble(devices, start, lf.at[k], k, own, arrived)
    for copy in copies:
        copy.wait()
    for k in range(count):
        mirror(devices, lf.at[k], panel, order)
    ga = dot3(cov_trans[:order], lf[0], NN)
    gb = dot3(cov_trans[order:], lf[1], NN)
    a = (s % 2) * count
    mean_a, mean_b = info[pl.ds(a, 1), :], info[pl.ds(a + 1, 1), :]
    pred_a, pred_b = info[pl.ds(a + 8, 1), :], info[pl.ds(a + 9, 1), :]
    map_ref[order:, :] = jnp.concatenate(
        [mean_a + matvec(ga, mean_b - pred_a), mean_b, pred_b, jnp.zeros((5, order), F32)], axis=0
    )
    map_ref[:order, :] = dot3(ga, gb, NN)
    late_ref[...] = gb


def block_kernel(own, partner, map_ref, slots, sems):
    s, order = lax.axis_index("state"), own.shape[1]
    start, copies = starter(sems)
    start(own, slots.at[s % 2])
    start(partner, slots.at[1 - s % 2])
    for copy in copies:
        copy.wait()
    early, late = slots.at[0], slots.at[1]
    shift = early[order : order + 1, :] + matvec(early[:order, :], late[order : order + 1, :] - early[order + 2 : order + 3, :])
    map_ref[order:, :] = jnp.concatenate([shift, jnp.zeros((1, order), F32), late[order + 2 :, :]], axis=0)
    map_ref[:order, :] = dot3(early[:order, :], late[:order, :], NN)


def apply(map_ref, x):
    order = x.shape[1]
    vec = map_ref[order : order + 8, :]
    return vec[0:1] + matvec(map_ref[:order, :], x - vec[2:3])


def hop_kernel(x_ref, map_ref, out_ref):
    out_ref[...] = apply(map_ref, x_ref[...])


def last_kernel(devices, *refs):
    blocks = len(refs) - 4 - devices
    incoming, (own, partner, late_ref), outs, both = refs[:blocks], refs[blocks : blocks + 3], refs[blocks + 3 : -1], refs[-1]
    order, panel = own.shape[1], outs[0].shape[1]
    b, s = lax.axis_index("tm"), lax.axis_index("state")
    x = incoming[0][...]
    for k, ref in enumerate(incoming[1:], 1):
        x = jnp.where(lax.axis_size("tm") - 1 - b == k, ref[...], x)

    def give(x):
        vec = own[order : order + 8, :]
        later = vec[1:2] + matvec(late_ref[...], x - vec[2:3])
        pair = jnp.concatenate([apply(own, x), later], axis=0)
        for i in range(devices):
            both[i] = pair[:, i * panel : (i + 1) * panel]

    @pl.when(s % 2 == 0)
    def _():
        give(apply(partner, x))

    @pl.when(s % 2 == 1)
    def _():
        give(x)

    for off, out in enumerate(outs):
        out[...] = both[s ^ off]


def out_kernel(*refs):
    given, out_ref = refs[:-1], refs[-1]
    s = lax.axis_index("state")

    def pick(off):
        x = given[0][...]
        for k, ref in enumerate(given[1:], 1):
            x = jnp.where(off == k, ref[...], x)
        return x

    out_ref[...] = jnp.concatenate([pick(s), pick(s ^ 1)], axis=0)


def params(mebibytes):
    return pltpu.CompilerParams(vmem_limit_bytes=mebibytes * 2**20)


def local(filtered_covariance, pred_prec, transition, filt_means, terminal_mean):
    steps, panel, order = filtered_covariance.shape
    devices, blocks = lax.axis_size("state"), lax.axis_size("tm")
    count = steps // 2

    def swap(x, off, block_off=0):
        pairs = [(i, i ^ (block_off * devices + off)) for i in range(blocks * devices)]
        return lax.ppermute(x, ("tm", "state"), pairs)

    def shape(*dims):
        return jax.ShapeDtypeStruct(dims, F32)

    def call(kernel, name, mebibytes, outs, in_specs, scratch, args):
        return pl.pallas_call(
            kernel,
            out_shape=outs,
            in_specs=in_specs,
            out_specs=[VMEM] * len(outs),
            scratch_shapes=scratch,
            compiler_params=params(mebibytes),
            name=name,
        )(*args)

    cov, prec, trans, means, terminal = (
        pltpu.with_memory_space_constraint(x, pltpu.HBM)
        for x in (filtered_covariance, pred_prec, transition, filt_means, terminal_mean[None])
    )
    semaphores = pltpu.SemaphoreType.DMA((8 * devices,))
    far = [shape(count, panel, width(devices, panel, order, off)) for off in range(2, devices)]
    *pieces, trans_half, first = call(
        functools.partial(pack_kernel, devices),
        "pack",
        4,
        far + far + [shape(panel // 2, order), shape(1, order)],
        [HBM] * 4,
        [pltpu.VMEM((1, order), F32), semaphores],
        (cov, prec, trans, terminal),
    )
    whole = shape(count, panel, order)
    near_cov, near_prec, own_cov, own_prec, own_trans, own_means = call(
        load_kernel,
        "load",
        4,
        [whole] * 4 + [shape(panel, order), shape(steps, order)],
        [HBM] * 4 + [VMEM],
        [semaphores],
        (cov, prec, trans, means, first),
    )

    moved = [swap(own_trans, 1)]
    for off in range(2, devices, 2):
        across = swap(trans_half, off)
        around = swap(across, 0, 1)
        moved += [across, around, swap(across, 1), swap(around, 1)]
    cov_pieces = [swap(near_cov, 1)] + [swap(x, off) for off, x in enumerate(pieces[: devices - 2], 2)]
    prec_pieces = [swap(near_prec, 1)] + [swap(x, off) for off, x in enumerate(pieces[devices - 2 :], 2)]

    cov_trans, info = call(
        functools.partial(cov_kernel, devices),
        "cov",
        24,
        [shape(count * order, order), shape(16, order)],
        [ANY, VMEM] + [ANY] * (devices + len(moved)),
        [pltpu.VMEM((count * order + 16, order), F32), pltpu.VMEM((order, order), F32), semaphores],
        (own_cov, own_means, own_trans, *cov_pieces, *moved),
    )
    pair_map, late = call(
        functools.partial(gain_kernel, devices),
        "gain",
        24,
        [shape(order + 8, order), shape(order, order)],
        [VMEM, VMEM] + [ANY] * devices,
        [pltpu.VMEM((count, order, order), F32), semaphores],
        (cov_trans, info, own_prec, *prec_pieces),
    )
    partner_map = swap(pair_map, 1)
    (block_map,) = call(
        block_kernel,
        "block",
        12,
        [shape(order + 8, order)],
        [ANY, ANY],
        [pltpu.VMEM((2, order + 8, order), F32), semaphores],
        (pair_map, partner_map),
    )

    incoming = [first]
    for block in range(blocks - 1, 0, -1):
        (x,) = call(hop_kernel, "hop", 4, [shape(1, order)], [VMEM, VMEM], [], (incoming[-1], block_map))
        incoming.append(swap(x, 1, block ^ (block - 1)))

    given = call(
        functools.partial(last_kernel, devices),
        "last",
        6,
        [shape(count, panel)] * devices,
        [VMEM] * (blocks + 3),
        [pltpu.VMEM((devices, count, panel), F32)],
        (*incoming, pair_map, partner_map, late),
    )
    given = [given[0]] + [swap(x, off) for off, x in enumerate(given[1:], 1)]
    (out,) = call(out_kernel, "out", 4, [shape(steps, panel)], [VMEM] * devices, [], given)
    return out


def solution(mesh):
    return jax.shard_map(
        local,
        mesh=mesh,
        in_specs=(
            P("tm", "state", None),
            P("tm", "state", None),
            P("state", None),
            P("tm", None),
            P(),
        ),
        out_specs=P("tm", "state"),
        check_vma=False,
    )
```

```python
import functools

import jax
import jax.numpy as jnp
from jax import lax
from jax.experimental import pallas as pl
from jax.experimental.pallas import tpu as pltpu
from jax.sharding import PartitionSpec as P

F32, BF16 = jnp.float32, jnp.bfloat16
NN = (((1,), (0,)), ((), ()))
NT = (((1,), (1,)), ((), ()))
ANY = pl.BlockSpec(memory_space=pl.ANY)
HBM = pl.BlockSpec(memory_space=pltpu.HBM)
VMEM = pl.BlockSpec(memory_space=pltpu.VMEM)


def split(x):
    high = x.astype(BF16)
    return high, (x - high.astype(F32)).astype(BF16)


def dot3(a, b, dims):
    (ah, al), (bh, bl) = split(a), split(b)
    dot = functools.partial(lax.dot_general, dimension_numbers=dims, preferred_element_type=F32)
    return dot(ah, bh) + (dot(ah, bl) + dot(al, bh))


def matvec(matrix, row):
    order = matrix.shape[1]
    total = matrix[:, :128] * row[:, :128]
    for j in range(128, order, 128):
        total += matrix[:, j : j + 128] * row[:, j : j + 128]
    return jnp.sum(total.T, axis=0, keepdims=True)


def rows(i, panel):
    return pl.ds(pl.multiple_of(i * panel, panel), panel)


def starter(sems):
    copies = []

    def start(source, target):
        copy = pltpu.make_async_copy(source, target, sems.at[len(copies)])
        copy.start()
        copies.append(copy)

    return start, copies


def width(devices, panel, order, off):
    if off < 2:
        return order
    return panel if devices == 4 and off == 3 and panel % 128 == 0 else order - 2 * panel


def pack_kernel(devices, cov, prec, trans, terminal, *refs):
    far, (trans_half, first, vector, sems) = refs[:-4], refs[-4:]
    steps, panel, order = cov.shape
    b, s = lax.axis_index("tm"), lax.axis_index("state")
    start, copies = starter(sems)
    start(terminal, vector)
    start(trans.at[pl.ds(pl.multiple_of((b % 2) * (panel // 2), panel // 2), panel // 2), :], trans_half)
    pieces = iter(far)
    for matrix, groups in ((cov, 1), (prec, 2)):
        for group in range(groups):
            for off in range(2, devices):
                piece = next(pieces)
                count = piece.shape[0]
                step = ((s ^ off) % 2) * (steps // 2) + (groups - 1 - group) * count
                w = width(devices, panel, order, off)
                column = 2 * panel if w == order - 2 * panel else pl.multiple_of(s * panel, panel)
                start(matrix.at[pl.ds(step, count), :, pl.ds(column, w)], piece)
    copies[0].wait()
    first[...] = jnp.where(b == lax.axis_size("tm") - 1, vector[...], 0.0)
    for copy in copies[1:]:
        copy.wait()


def load_kernel(cov, prec, trans, means, after, near, own, own_means, sems):
    count = cov.shape[0] // 2
    s = lax.axis_index("state")
    start, copies = starter(sems)
    for target, half in ((near, 1 - s % 2), (own, s % 2)):
        start(cov.at[pl.ds(half * count, count)], target.at[pl.ds(0, count)])
        start(prec.at[pl.ds(half * count, count)], target.at[pl.ds(count, count)])
        start(trans, target.at[2 * count])
    start(means, own_means)
    for copy in copies:
        copy.wait()


def assemble(devices, start, full, panels):
    panel, order = panels[0].shape
    s = lax.axis_index("state")
    for off, piece in enumerate(panels):
        i = s ^ off
        w = width(devices, panel, order, off)
        target = full.at[rows(i, panel), :]
        if w < order:
            column = 2 * panel if w == order - 2 * panel else pl.multiple_of(i * panel, panel)
            target = full.at[rows(i, panel), pl.ds(column, w)]
        start(piece, target)


def mirror(devices, full, panel, order):
    s, known = lax.axis_index("state"), 2 * panel
    full[known:order, :known] = full[:known, known:order].T
    if width(devices, panel, order, 3) < order - known:
        i, j = s ^ 3, s ^ 2
        full[rows(i, panel), rows(j, panel)] = full[rows(j, panel), rows(i, panel)].T


def cov_kernel(devices, means, own, near, *refs):
    far, moved, (out, info, pf, af, sems) = refs[: devices - 2], refs[devices - 2 : -5], refs[-5:]
    _, panel, order = own.shape
    count = far[0].shape[0]
    steps = means.shape[0]
    b, s = lax.axis_index("tm"), lax.axis_index("state")
    start, copies = starter(sems)
    for k in range(count):
        panels = [own.at[k], near.at[k]] + [piece.at[k] for piece in far]
        assemble(devices, start, pf.at[pl.ds(k * order, order), :], panels)
    start(own.at[2 * count], af.at[rows(s, panel), :])
    start(near.at[2 * count], af.at[rows(s ^ 1, panel), :])
    spots = [(off ^ beside, half) for off in range(2, devices, 2) for beside in range(2) for half in range(2)]
    for piece, (off, half) in zip(moved, spots):
        at = (s ^ off) * panel + (b % 2 if half == 0 else 1 - b % 2) * (panel // 2)
        start(piece, af.at[pl.ds(pl.multiple_of(at, panel // 2), panel // 2), :])
    pf[count * order :, :] = jnp.concatenate([means[...], jnp.zeros((16 - steps, order), F32)], axis=0)
    for copy in copies:
        copy.wait()
    for k in range(count):
        mirror(devices, pf.at[pl.ds(k * order, order), :], panel, order)
    product = dot3(pf[...], af[...], NT)
    out[...] = product[: count * order]
    info[:8] = pf[count * order : count * order + 8, :]
    info[8:] = product[count * order : count * order + 8]


def gain_kernel(devices, k, cov_trans, own, near, *refs):
    far, (gain, lf, sems) = refs[: devices - 2], refs[-3:]
    count, (_, panel, order) = own.shape[0] // 2, own.shape
    start, copies = starter(sems)
    assemble(devices, start, lf, [own.at[count + k], near.at[count + k]] + [piece.at[0] for piece in far])
    for copy in copies:
        copy.wait()
    mirror(devices, lf, panel, order)
    gain[...] = dot3(cov_trans[k * order : (k + 1) * order, :], lf[...], NN)


def three_kernel(info, g1, g2, g3, c_ref, n_ref, vec_ref):
    mean, pred = info[0:4, :], info[8:12, :]
    late = mean[2:3] + matvec(g2[...], mean[3:4] - pred[2:3])
    early = mean[1:2] + matvec(g1[...], late - pred[1:2])
    vec_ref[...] = jnp.concatenate([pred[3:4], mean[3:4], late, early, mean[0:1], pred[0:1], mean[0:2]], axis=0)
    c = dot3(g2[...], g3[...], NN)
    c_ref[...] = c
    n_ref[...] = dot3(g1[...], c, NN)


def four_kernel(vec, n, g0, m_ref, out_ref):
    shift = vec[4:5, :] + matvec(g0[...], vec[3:4, :] - vec[5:6, :])
    out_ref[...] = jnp.concatenate([vec[0:1, :], shift, vec[0:6, :]], axis=0)
    m_ref[...] = dot3(g0[...], n[...], NN)


def hop_kernel(x, m, vec, out_ref):
    out_ref[...] = vec[1:2, :] + matvec(m[...], x[...] - vec[0:1, :])


def last_kernel(devices, *refs):
    blocks = len(refs) - 6 - devices
    incoming, (m, n, c, g3, vec), outs, cut = refs[:blocks], refs[blocks : blocks + 5], refs[blocks + 5 : -1], refs[-1]
    panel = outs[0].shape[1]
    b, s = lax.axis_index("tm"), lax.axis_index("state")
    x = incoming[0][...]
    for k, ref in enumerate(incoming[1:], 1):
        x = jnp.where(lax.axis_size("tm") - 1 - b == k, ref[...], x)
    gap = x - vec[0:1, :]
    shifts = (vec[1:2, :], vec[5:6, :], vec[4:5, :], vec[3:4, :])
    full = jnp.concatenate([v + matvec(g[...], gap) for v, g in zip(shifts, (m, n, c, g3))], axis=0)
    for i in range(devices):
        cut[i] = full[:, i * panel : (i + 1) * panel]
    for off, out in enumerate(outs):
        out[...] = cut[s ^ off]


def out_kernel(*refs):
    given, out_ref = refs[:-1], refs[-1]
    off = lax.axis_index("state") ^ 1
    x = given[0][...]
    for k, ref in enumerate(given[1:], 1):
        x = jnp.where(off == k, ref[...], x)
    out_ref[...] = x


def params(mebibytes):
    return pltpu.CompilerParams(vmem_limit_bytes=mebibytes * 2**20)


def local(filtered_covariance, pred_prec, transition, filt_means, terminal_mean):
    steps, panel, order = filtered_covariance.shape
    devices, blocks = lax.axis_size("state"), lax.axis_size("tm")
    count = steps // 2

    def swap(x, off, block_off=0):
        pairs = [(i, i ^ (block_off * devices + off)) for i in range(blocks * devices)]
        return lax.ppermute(x, ("tm", "state"), pairs)

    def shape(*dims):
        return jax.ShapeDtypeStruct(dims, F32)

    def call(kernel, name, mebibytes, outs, in_specs, scratch, args):
        return pl.pallas_call(
            kernel,
            out_shape=outs,
            in_specs=in_specs,
            out_specs=[VMEM] * len(outs),
            scratch_shapes=scratch,
            compiler_params=params(mebibytes),
            name=name,
        )(*args)

    cov, prec, trans, means, terminal = (
        pltpu.with_memory_space_constraint(x, pltpu.HBM)
        for x in (filtered_covariance, pred_prec, transition, filt_means, terminal_mean[None])
    )
    semaphores = pltpu.SemaphoreType.DMA((8 * devices,))
    square = shape(order, order)

    def far(k):
        return [shape(k, panel, width(devices, panel, order, off)) for off in range(2, devices)]

    *pieces, trans_half, first = call(
        functools.partial(pack_kernel, devices),
        "pack",
        4,
        far(count) + far(1) * count + [shape(panel // 2, order), shape(1, order)],
        [HBM] * 4,
        [pltpu.VMEM((1, order), F32), semaphores],
        (cov, prec, trans, terminal),
    )
    panels = shape(2 * count + 1, panel, order)
    near, own, own_means = call(
        load_kernel,
        "load",
        4,
        [panels, panels, shape(steps, order)],
        [HBM] * 4 + [VMEM],
        [semaphores],
        (cov, prec, trans, means, first),
    )

    across = [swap(trans_half, off) for off in range(2, devices, 2)]
    arrived = []
    for group in range(1 + count):
        at = group * (devices - 2)
        arrived.append([swap(x, off) for off, x in enumerate(pieces[at : at + devices - 2], 2)])
    near = swap(near, 1)
    moved = []
    for x in across:
        around = swap(x, 0, 1)
        moved += [x, around, swap(x, 1), swap(around, 1)]

    cov_trans, info = call(
        functools.partial(cov_kernel, devices),
        "cov",
        24,
        [shape(count * order, order), shape(16, order)],
        [VMEM] + [ANY] * (devices + len(moved)),
        [pltpu.VMEM((count * order + 16, order), F32), pltpu.VMEM((order, order), F32), semaphores],
        (own_means, own, near, *arrived[0], *moved),
    )

    def gain(k, far):
        (out,) = call(
            functools.partial(gain_kernel, devices, k),
            "gain",
            16,
            [square],
            [VMEM] + [ANY] * devices,
            [pltpu.VMEM((order, order), F32), semaphores],
            (cov_trans, own, near, *far),
        )
        return out

    g3 = gain(1, arrived[1])
    g1 = swap(g3, 1)
    g2 = gain(0, arrived[2])
    g0 = swap(g2, 1)
    c, n, vec = call(
        three_kernel, "three", 12, [square, square, shape(8, order)], [VMEM] * 4, [], (info, g1, g2, g3)
    )
    m, vec = call(four_kernel, "four", 12, [square, shape(8, order)], [VMEM] * 3, [], (vec, n, g0))

    incoming = [first]
    for block in range(blocks - 1, 0, -1):
        (x,) = call(hop_kernel, "hop", 4, [shape(1, order)], [VMEM] * 3, [], (incoming[-1], m, vec))
        if block % 2:
            x = swap(x, 0, 1)
        else:
            x = lax.ppermute(x, ("tm", "state"), [(block * devices + 1, (block - 1) * devices + 1)])
        incoming.append(x)

    given = call(
        functools.partial(last_kernel, devices),
        "last",
        8,
        [shape(steps, panel)] * devices,
        [VMEM] * (blocks + 5),
        [pltpu.VMEM((devices, steps, panel), F32)],
        (*incoming, m, n, c, g3, vec),
    )
    given = [given[0]] + [swap(x, off) for off, x in enumerate(given[1:], 1)]
    (out,) = call(out_kernel, "out", 4, [shape(steps, panel)], [VMEM] * devices, [], given)
    return out


def solution(mesh):
    return jax.shard_map(
        local,
        mesh=mesh,
        in_specs=(
            P("tm", "state", None),
            P("tm", "state", None),
            P("state", None),
            P("tm", None),
            P(),
        ),
        out_specs=P("tm", "state"),
        check_vma=False,
    )
```

```python
import functools

import jax
import jax.numpy as jnp
from jax import lax
from jax.experimental import pallas as pl
from jax.experimental.pallas import tpu as pltpu
from jax.sharding import PartitionSpec as P

F32, BF16 = jnp.float32, jnp.bfloat16
NN = (((1,), (0,)), ((), ()))
NT = (((1,), (1,)), ((), ()))
ANY = pl.BlockSpec(memory_space=pl.ANY)
HBM = pl.BlockSpec(memory_space=pltpu.HBM)
VMEM = pl.BlockSpec(memory_space=pltpu.VMEM)


def split(x):
    high = x.astype(BF16)
    return high, (x - high.astype(F32)).astype(BF16)


def dot3(a, b, dims):
    (ah, al), (bh, bl) = split(a), split(b)
    dot = functools.partial(lax.dot_general, dimension_numbers=dims, preferred_element_type=F32)
    return dot(ah, bh) + (dot(ah, bl) + dot(al, bh))


def matvec(matrix, row):
    order = matrix.shape[1]
    total = matrix[:, :128] * row[:, :128]
    for j in range(128, order, 128):
        total += matrix[:, j : j + 128] * row[:, j : j + 128]
    return jnp.sum(total.T, axis=0, keepdims=True)


def rows(i, panel):
    return pl.ds(pl.multiple_of(i * panel, panel), panel)


def starter(sems):
    copies = []

    def start(source, target):
        copy = pltpu.make_async_copy(source, target, sems.at[len(copies)])
        copy.start()
        copies.append(copy)

    return start, copies


def width(devices, panel, order, off):
    if off < 2:
        return order
    return panel if devices == 4 and off == 3 and panel % 128 == 0 else order - 2 * panel


def far_copies(devices, start, matrix, far):
    steps, panel, order = matrix.shape
    s = lax.axis_index("state")
    for off, piece in enumerate(far, 2):
        w = width(devices, panel, order, off)
        column = 2 * panel if w == order - 2 * panel else pl.multiple_of(s * panel, panel)
        mine = pl.ds(((s ^ off) % 2) * (steps // 2), steps // 2)
        start(matrix.at[mine, :, pl.ds(column, w)], piece)


def pack_kernel(devices, cov, prec, trans, means, terminal, *refs):
    far, (trans_half, first, near, own, own_means, vector, sems) = refs[: 2 * devices - 4], refs[2 * devices - 4 :]
    count, panel = cov.shape[0] // 2, cov.shape[1]
    b, s = lax.axis_index("tm"), lax.axis_index("state")
    start, copies = starter(sems)
    start(terminal, vector)
    start(trans.at[pl.ds(pl.multiple_of((b % 2) * (panel // 2), panel // 2), panel // 2), :], trans_half)
    far_copies(devices, start, cov, far[: devices - 2])
    far_copies(devices, start, prec, far[devices - 2 :])
    for target, half in ((near, 1 - s % 2), (own, s % 2)):
        start(cov.at[pl.ds(half * count, count)], target.at[pl.ds(0, count)])
        start(prec.at[pl.ds(half * count, count)], target.at[pl.ds(count, count)])
        start(trans, target.at[2 * count])
    start(means, own_means)
    copies[0].wait()
    first[...] = jnp.where(b == lax.axis_size("tm") - 1, vector[...], 0.0)
    for copy in copies[1:]:
        copy.wait()


def join_kernel(*refs):
    moved, (joined, sems) = refs[:-2], refs[-2:]
    half = moved[0].shape[0]
    b = lax.axis_index("tm")
    start, copies = starter(sems)
    for k, piece in enumerate(moved):
        at = (b % 2 if k % 2 == 0 else 1 - b % 2) * half
        start(piece, joined.at[k // 2, pl.ds(pl.multiple_of(at, half), half), :])
    for copy in copies:
        copy.wait()


def cov_kernel(means, own, near, joined, joined_near, *refs):
    far, (gains, late, info, pf, af, lf, sems) = refs[:-7], refs[-7:]
    _, panel, order = own.shape
    count, known = far[0].shape[0], 2 * panel
    steps = means.shape[0]
    e = lax.axis_index("state") % 2
    start, copies = starter(sems)
    for k in range(count):
        full = pf.at[pl.ds(k * order, order), :]
        start(own.at[k], full.at[rows(e, panel), :])
        start(near.at[k], full.at[rows(1 - e, panel), :])
        start(own.at[count + k], lf.at[k, rows(e, panel), :])
        start(near.at[count + k], lf.at[k, rows(1 - e, panel), :])
        for off, piece in enumerate(far, 2):
            i = e ^ off
            w = piece.shape[2]
            column = known if w == order - known else pl.multiple_of(i * panel, panel)
            start(piece.at[k], full.at[rows(i, panel), pl.ds(column, w)])
    for j in range(order // (2 * panel)):
        mine, theirs = (own.at[2 * count], near.at[2 * count]) if j == 0 else (joined.at[j - 1], joined_near.at[j - 1])
        start(mine, af.at[rows(e ^ (2 * j), panel), :])
        start(theirs, af.at[rows(e ^ (2 * j) ^ 1, panel), :])
    pf[count * order :, :] = jnp.concatenate([means[...], jnp.zeros((16 - steps, order), F32)], axis=0)
    for copy in copies:
        copy.wait()
    for k in range(count):
        full = pf.at[pl.ds(k * order, order), :]
        full[known:order, :known] = full[:known, known:order].T
        if far[-1].shape[2] < order - known:
            i, j = e ^ 3, e ^ 2
            full[rows(i, panel), rows(j, panel)] = full[rows(j, panel), rows(i, panel)].T
    product = dot3(pf[...], af[...], NT)
    info[:8] = pf[count * order : count * order + 8, :]
    info[8:] = product[count * order : count * order + 8]
    late[...] = product[: count * order, known:]
    for k in range(count):
        part = product[k * order : (k + 1) * order]
        partial = dot3(part[:, :known], lf[k], NN)
        gains[k, :, :known] = partial[:, :known] + dot3(part[:, known:], lf[k, :, known:], NT)
        gains[k, :, known:] = partial[:, known:]


def gain_kernel(info, gains, late, *refs):
    far, (map_ref, gain_ref, ff) = refs[:-3], refs[-3:]
    count, panel, _ = far[0].shape
    order = gains.shape[1]
    known = 2 * panel
    s = lax.axis_index("state")
    e = s % 2
    for k in range(count):
        for off, piece in enumerate(far, 2):
            i = (e ^ off) - 2
            if piece.shape[2] == order - known:
                ff[k, rows(i, panel), :] = piece[k]
            else:
                ff[k, rows(i, panel), rows(i, panel)] = piece[k]
        if far[-1].shape[2] < order - known:
            i, j = (e ^ 3) - 2, (e ^ 2) - 2
            ff[k, rows(i, panel), rows(j, panel)] = ff[k, rows(j, panel), rows(i, panel)].T

    def complete(k):
        rest = gains[k, :, known:] + dot3(late[k * order : (k + 1) * order, :], ff[k], NN)
        return jnp.concatenate([gains[k, :, :known], rest], axis=1)

    ga, gb = complete(0), complete(1)
    gain_ref[...] = gb
    a = e * count
    mean_a, mean_b = info[pl.ds(a, 1), :], info[pl.ds(a + 1, 1), :]
    pred_a, pred_b = info[pl.ds(a + 8, 1), :], info[pl.ds(a + 9, 1), :]
    map_ref[order:, :] = jnp.concatenate(
        [mean_a + matvec(ga, mean_b - pred_a), mean_b, pred_b, jnp.zeros((5, order), F32)], axis=0
    )
    map_ref[:order, :] = dot3(ga, gb, NN)


def block_kernel(late, early, m_ref, vec_ref):
    order = late.shape[1]
    shift = early[order : order + 1, :] + matvec(
        early[:order, :], late[order : order + 1, :] - early[order + 2 : order + 3, :]
    )
    vec_ref[...] = jnp.concatenate([late[order + 2 : order + 3, :], shift, jnp.zeros((6, order), F32)], axis=0)
    m_ref[...] = dot3(early[:order, :], late[:order, :], NN)


def hop_kernel(x, m, vec, out_ref):
    out_ref[...] = vec[1:2, :] + matvec(m[...], x[...] - vec[0:1, :])


def last_kernel(devices, *refs):
    blocks = len(refs) - 7 - devices
    incoming, (m, vec, late, g3, early, g1), outs, cut = refs[:blocks], refs[blocks : blocks + 6], refs[blocks + 6 : -1], refs[-1]
    order, panel = m.shape[1], outs[0].shape[1]
    b, s = lax.axis_index("tm"), lax.axis_index("state")
    x = incoming[0][...]
    for k, ref in enumerate(incoming[1:], 1):
        x = jnp.where(lax.axis_size("tm") - 1 - b == k, ref[...], x)
    gap = x - vec[0:1, :]
    x3 = late[order + 1 : order + 2, :] + matvec(g3[...], gap)
    x2 = late[order : order + 1, :] + matvec(late[:order, :], gap)
    x0 = vec[1:2, :] + matvec(m[...], gap)
    x1 = early[order + 1 : order + 2, :] + matvec(g1[...], x2 - early[order + 2 : order + 3, :])
    full = jnp.concatenate([x0, x1, x2, x3], axis=0)
    for i in range(devices):
        cut[i] = full[:, i * panel : (i + 1) * panel]
    for off, out in enumerate(outs):
        out[...] = cut[s ^ off]


def out_kernel(*refs):
    given, out_ref = refs[:-1], refs[-1]
    off = lax.axis_index("state") ^ 1
    x = given[0][...]
    for k, ref in enumerate(given[1:], 1):
        x = jnp.where(off == k, ref[...], x)
    out_ref[...] = x


def params(mebibytes):
    return pltpu.CompilerParams(vmem_limit_bytes=mebibytes * 2**20)


def local(filtered_covariance, pred_prec, transition, filt_means, terminal_mean):
    steps, panel, order = filtered_covariance.shape
    devices, blocks = lax.axis_size("state"), lax.axis_size("tm")
    count = steps // 2

    def swap(x, off, block_off=0):
        pairs = [(i, i ^ (block_off * devices + off)) for i in range(blocks * devices)]
        return lax.ppermute(x, ("tm", "state"), pairs)

    def shape(*dims):
        return jax.ShapeDtypeStruct(dims, F32)

    def call(kernel, name, mebibytes, outs, in_specs, scratch, args):
        return pl.pallas_call(
            kernel,
            out_shape=outs,
            in_specs=in_specs,
            out_specs=[VMEM] * len(outs),
            scratch_shapes=scratch,
            compiler_params=params(mebibytes),
            name=name,
        )(*args)

    cov, prec, trans, means, terminal = (
        pltpu.with_memory_space_constraint(x, pltpu.HBM)
        for x in (filtered_covariance, pred_prec, transition, filt_means, terminal_mean[None])
    )
    semaphores = pltpu.SemaphoreType.DMA((8 * devices,))
    square = shape(order, order)

    far = [shape(count, panel, width(devices, panel, order, off)) for off in range(2, devices)]
    panels = shape(2 * count + 1, panel, order)
    *far, trans_half, first, near, own, own_means = call(
        functools.partial(pack_kernel, devices),
        "pack",
        4,
        far + far + [shape(panel // 2, order), shape(1, order), panels, panels, shape(steps, order)],
        [HBM] * 5,
        [pltpu.VMEM((1, order), F32), semaphores],
        (cov, prec, trans, means, terminal),
    )
    across = [swap(trans_half, off) for off in range(2, devices, 2)]
    cov_far, prec_far = ([swap(x, off) for off, x in enumerate(part, 2)] for part in (far[: devices - 2], far[devices - 2 :]))
    near = swap(near, 1)
    moved = [y for x in across for y in (x, swap(x, 0, 1))]
    (joined,) = call(
        join_kernel, "join", 4, [shape(devices // 2 - 1, panel, order)], [ANY] * len(moved), [semaphores], moved
    )
    joined_near = swap(joined, 1)

    gains, late, info = call(
        cov_kernel,
        "cov",
        28,
        [shape(count, order, order), shape(count * order, order - 2 * panel), shape(16, order)],
        [VMEM] + [ANY] * (devices + 2),
        [
            pltpu.VMEM((count * order + 16, order), F32),
            pltpu.VMEM((order, order), F32),
            pltpu.VMEM((count, 2 * panel, order), F32),
            semaphores,
        ],
        (own_means, own, near, joined, joined_near, *cov_far),
    )
    late_map, g3 = call(
        gain_kernel,
        "gain",
        20,
        [shape(order + 8, order), square],
        [VMEM] * (1 + devices),
        [pltpu.VMEM((count, order - 2 * panel, order - 2 * panel), F32)],
        (info, gains, late, *prec_far),
    )
    early_map = swap(late_map, 1)
    m, vec = call(block_kernel, "block", 12, [square, shape(8, order)], [VMEM] * 2, [], (late_map, early_map))

    incoming = [first]
    for block in range(blocks - 1, 0, -1):
        (x,) = call(hop_kernel, "hop", 4, [shape(1, order)], [VMEM] * 3, [], (incoming[-1], m, vec))
        if block % 2:
            x = swap(x, 0, 1)
        else:
            x = lax.ppermute(x, ("tm", "state"), [(block * devices + 1, (block - 1) * devices + 1)])
        incoming.append(x)
    g1 = swap(lax.optimization_barrier((g3, incoming[1]))[0], 1)

    given = list(call(
        functools.partial(last_kernel, devices),
        "last",
        8,
        [shape(steps, panel)] * devices,
        [VMEM] * (blocks + 6),
        [pltpu.VMEM((devices, steps, panel), F32)],
        (*incoming, m, vec, late_map, g3, early_map, g1),
    ))
    for off in range(devices - 1, 0, -1):
        given[off] = swap(given[off], off)
    (out,) = call(out_kernel, "out", 4, [shape(steps, panel)], [VMEM] * devices, [], given)
    return out


def solution(mesh):
    return jax.shard_map(
        local,
        mesh=mesh,
        in_specs=(
            P("tm", "state", None),
            P("tm", "state", None),
            P("state", None),
            P("tm", None),
            P(),
        ),
        out_specs=P("tm", "state"),
        check_vma=False,
    )
```

```python
import functools

import jax
import jax.numpy as jnp
from jax import lax
from jax.experimental import pallas as pl
from jax.experimental.pallas import tpu as pltpu
from jax.sharding import PartitionSpec as P

F32, BF16 = jnp.float32, jnp.bfloat16
NN = (((1,), (0,)), ((), ()))
NT = (((1,), (1,)), ((), ()))
ANY = pl.BlockSpec(memory_space=pl.ANY)
HBM = pl.BlockSpec(memory_space=pltpu.HBM)
VMEM = pl.BlockSpec(memory_space=pltpu.VMEM)


def split(x):
    high = x.astype(BF16)
    return high, (x - high.astype(F32)).astype(BF16)


def dot3(a, b, dims):
    ah, al = split(a)
    bh, bl = split(b) if hasattr(b, "dtype") and b.dtype == F32 else (b[0][...], b[1][...])
    dot = functools.partial(lax.dot_general, dimension_numbers=dims, preferred_element_type=F32)
    return dot(ah, bh) + (dot(ah, bl) + dot(al, bh))


def matvec(matrix, row):
    order = matrix.shape[1]
    total = matrix[:, :128] * row[:, :128]
    for j in range(128, order, 128):
        total += matrix[:, j : j + 128] * row[:, j : j + 128]
    return jnp.sum(total.T, axis=0, keepdims=True)


def rows(i, panel):
    return pl.ds(pl.multiple_of(i * panel, panel), panel)


def starter(sems):
    copies = []

    def start(source, target):
        copy = pltpu.make_async_copy(source, target, sems.at[len(copies)])
        copy.start()
        copies.append(copy)

    return start, copies


def width(devices, panel, order, off):
    if off < 2:
        return order
    return panel if devices == 4 and off == 3 and panel % 128 == 0 else order - 2 * panel


def pack_kernel(devices, cov, prec, trans, terminal, *refs):
    far, (trans_half, first, near, vector, sems) = refs[: devices - 2], refs[devices - 2 :]
    count, panel, order = cov.shape[0] // 2, *cov.shape[1:]
    b, s = lax.axis_index("tm"), lax.axis_index("state")
    start, copies = starter(sems)
    start(terminal, vector)
    start(trans.at[pl.ds(pl.multiple_of((b % 2) * (panel // 2), panel // 2), panel // 2), :], trans_half)
    for off, piece in enumerate(far, 2):
        w = width(devices, panel, order, off)
        column = 2 * panel if w == order - 2 * panel else pl.multiple_of(s * panel, panel)
        theirs = pl.ds(((s ^ off) % 2) * count, count)
        for k, matrix in enumerate((cov, prec)):
            start(matrix.at[theirs, :, pl.ds(column, w)], piece.at[pl.ds(k * count, count)])
    theirs = pl.ds((1 - s % 2) * count, count)
    start(cov.at[theirs], near.at[pl.ds(0, count)])
    start(prec.at[theirs], near.at[pl.ds(count, count)])
    start(trans, near.at[2 * count])
    copies[0].wait()
    first[...] = jnp.where(b == lax.axis_size("tm") - 1, vector[...], 0.0)
    for copy in copies[1:]:
        copy.wait()


def join_kernel(*refs):
    moved, (joined, sems) = refs[:-2], refs[-2:]
    half = moved[0].shape[0]
    b = lax.axis_index("tm")
    start, copies = starter(sems)
    for k, piece in enumerate(moved):
        at = (b % 2 if k % 2 == 0 else 1 - b % 2) * half
        start(piece, joined.at[k // 2, pl.ds(pl.multiple_of(at, half), half), :])
    for copy in copies:
        copy.wait()


def early_kernel(cov, prec, trans, means, near, joined, joined_near, *refs):
    info, a_far, l_known, c_known, c_far, g_known, pf, af, lf, sems = refs
    steps, panel, order = cov.shape
    count, known = steps // 2, 2 * panel
    s = lax.axis_index("state")
    e = s % 2
    start, copies = starter(sems)
    for k in range(count):
        step = e * count + k
        start(cov.at[step], pf.at[pl.ds(pl.multiple_of(k * known + e * panel, panel), panel), :])
        start(near.at[k], pf.at[pl.ds(pl.multiple_of(k * known + (1 - e) * panel, panel), panel), :])
        start(prec.at[step], lf.at[k, rows(e, panel), :])
        start(near.at[count + k], lf.at[k, rows(1 - e, panel), :])
    start(trans, af.at[rows(e, panel), :])
    start(near.at[2 * count], af.at[rows(1 - e, panel), :])
    for j in range(1, order // known):
        start(joined.at[j - 1], af.at[rows(e ^ (2 * j), panel), :])
        start(joined_near.at[j - 1], af.at[rows(e ^ (2 * j) ^ 1, panel), :])
    pf[count * known :, :] = jnp.concatenate([means[...], jnp.zeros((16 - steps, order), F32)], axis=0)
    for copy in copies:
        copy.wait()
    product = dot3(pf[...], af[...], NT)
    info[:8] = pf[count * known : count * known + 8, :]
    info[8:] = product[count * known : count * known + 8]
    for half, x in enumerate(split(af[:, known:])):
        a_far[half] = x
    across = jnp.concatenate([pf[k * known : (k + 1) * known, known:].T for k in range(count)], axis=0)
    rest = dot3(across, af[:, :known], NT)
    for k in range(count):
        part = product[k * known : (k + 1) * known]
        for half, x in enumerate(split(lf[k])):
            l_known[k, half] = x
        partial = dot3(part[:, :known], lf[k], NN)
        g_known[k, :, :known] = partial[:, :known] + dot3(part[:, known:], lf[k, :, known:], NT)
        g_known[k, :, known:] = partial[:, known:]
        c_known[k] = part[:, known:]
        c_far[k] = rest[k * (order - known) : (k + 1) * (order - known)]


def late_kernel(info, a_far, l_known, c_known, c_far, g_known, *refs):
    far, (map_ref, gain_ref, ff) = refs[:-3], refs[-3:]
    count, known, order = g_known.shape
    panel = known // 2
    e = lax.axis_index("state") % 2
    for k in range(2 * count):
        for off, piece in enumerate(far, 2):
            i = (e ^ off) - 2
            if piece.shape[2] == order - known:
                ff[k, rows(i, panel), :] = piece[k]
            else:
                ff[k, rows(i, panel), rows(i, panel)] = piece[k]
        if far[-1].shape[2] < order - known:
            i, j = (e ^ 3) - 2, (e ^ 2) - 2
            ff[k, rows(i, panel), rows(j, panel)] = ff[k, rows(j, panel), rows(i, panel)].T

    def complete(k):
        c = c_far[k] + dot3(ff[k], a_far, NT)
        known_rows = (l_known.at[k, 0], l_known.at[k, 1])
        share = dot3(jnp.concatenate([c_known[k], c[:, known:]], axis=0), ff[count + k], NN)
        low = dot3(c[:, :known], known_rows, NN)
        left = low[:, :known] + dot3(c[:, known:], [x[:, known:] for x in known_rows], NT)
        top = jnp.concatenate([g_known[k, :, :known], g_known[k, :, known:] + share[:known]], axis=1)
        return jnp.concatenate([top, jnp.concatenate([left, low[:, known:] + share[known:]], axis=1)], axis=0)

    ga, gb = complete(0), complete(1)
    gain_ref[...] = gb
    a = e * count
    mean_a, mean_b = info[pl.ds(a, 1), :], info[pl.ds(a + 1, 1), :]
    pred_a, pred_b = info[pl.ds(a + 8, 1), :], info[pl.ds(a + 9, 1), :]
    map_ref[order:, :] = jnp.concatenate(
        [mean_a + matvec(ga, mean_b - pred_a), mean_b, pred_b, jnp.zeros((5, order), F32)], axis=0
    )
    map_ref[:order, :] = dot3(ga, gb, NN)


def block_kernel(late, early, m_ref, vec_ref):
    order = late.shape[1]
    shift = early[order : order + 1, :] + matvec(
        early[:order, :], late[order : order + 1, :] - early[order + 2 : order + 3, :]
    )
    vec_ref[...] = jnp.concatenate([late[order + 2 : order + 3, :], shift, jnp.zeros((6, order), F32)], axis=0)
    m_ref[...] = dot3(early[:order, :], late[:order, :], NN)


def hop_kernel(x, m, vec, out_ref):
    out_ref[...] = vec[1:2, :] + matvec(m[...], x[...] - vec[0:1, :])


def last_kernel(devices, *refs):
    blocks = len(refs) - 7 - devices
    incoming, (m, vec, late, g3, early, g1), outs, cut = refs[:blocks], refs[blocks : blocks + 6], refs[blocks + 6 : -1], refs[-1]
    order, panel = m.shape[1], outs[0].shape[1]
    b, s = lax.axis_index("tm"), lax.axis_index("state")
    x = incoming[0][...]
    for k, ref in enumerate(incoming[1:], 1):
        x = jnp.where(lax.axis_size("tm") - 1 - b == k, ref[...], x)
    gap = x - vec[0:1, :]
    x3 = late[order + 1 : order + 2, :] + matvec(g3[...], gap)
    x2 = late[order : order + 1, :] + matvec(late[:order, :], gap)
    x0 = vec[1:2, :] + matvec(m[...], gap)
    x1 = early[order + 1 : order + 2, :] + matvec(g1[...], x2 - early[order + 2 : order + 3, :])
    full = jnp.concatenate([x0, x1, x2, x3], axis=0)
    for i in range(devices):
        cut[i] = full[:, i * panel : (i + 1) * panel]
    for off, out in enumerate(outs):
        out[...] = cut[s ^ off]


def out_kernel(*refs):
    given, out_ref = [refs[0], *refs[-2:0:-1]], refs[-1]
    off = lax.axis_index("state") ^ 1
    x = given[0][...]
    for k, ref in enumerate(given[1:], 1):
        x = jnp.where(off == k, ref[...], x)
    out_ref[...] = x


def params(mebibytes):
    return pltpu.CompilerParams(vmem_limit_bytes=mebibytes * 2**20)


def local(filtered_covariance, pred_prec, transition, filt_means, terminal_mean):
    steps, panel, order = filtered_covariance.shape
    devices, blocks = lax.axis_size("state"), lax.axis_size("tm")
    count = steps // 2

    def swap(x, off, block_off=0):
        pairs = [(i, i ^ (block_off * devices + off)) for i in range(blocks * devices)]
        return lax.ppermute(x, ("tm", "state"), pairs)

    def shape(*dims):
        return jax.ShapeDtypeStruct(dims, F32)

    def call(kernel, name, mebibytes, outs, in_specs, scratch, args):
        return pl.pallas_call(
            kernel,
            out_shape=outs,
            in_specs=in_specs,
            out_specs=[VMEM] * len(outs),
            scratch_shapes=scratch,
            compiler_params=params(mebibytes),
            name=name,
        )(*args)

    cov, prec, trans, means, terminal = (
        pltpu.with_memory_space_constraint(x, pltpu.HBM)
        for x in (filtered_covariance, pred_prec, transition, filt_means, terminal_mean[None])
    )
    semaphores = pltpu.SemaphoreType.DMA((8 * devices,))
    square = shape(order, order)

    far = [shape(2 * count, panel, width(devices, panel, order, off)) for off in range(2, devices)]
    *far, trans_half, first, near = call(
        functools.partial(pack_kernel, devices),
        "pack",
        6,
        far + [shape(panel // 2, order), shape(1, order), shape(2 * count + 1, panel, order)],
        [HBM] * 4,
        [pltpu.VMEM((1, order), F32), semaphores],
        (cov, prec, trans, terminal),
    )
    across = [swap(trans_half, off) for off in range(2, devices, 2)]
    far = [swap(x, off) for off, x in enumerate(far, 2)]
    near = swap(near, 1)
    moved = [y for x in across for y in (x, swap(x, 0, 1))]
    (joined,) = call(
        join_kernel, "join", 4, [shape(devices // 2 - 1, panel, order)], [ANY] * len(moved), [semaphores], moved
    )
    joined_near = swap(joined, 1)

    known = 2 * panel
    parts = call(
        early_kernel,
        "early",
        24,
        [
            shape(16, order),
            jax.ShapeDtypeStruct((2, order, order - known), BF16),
            jax.ShapeDtypeStruct((count, 2, known, order), BF16),
            shape(count, known, order - known),
            shape(count, order - known, order),
            shape(count, known, order),
        ],
        [HBM] * 3 + [VMEM] + [ANY] * 3,
        [
            pltpu.VMEM((count * known + 16, order), F32),
            pltpu.VMEM((order, order), F32),
            pltpu.VMEM((count, known, order), F32),
            semaphores,
        ],
        (cov, prec, trans, means, near, joined, joined_near),
    )
    late_map, g3 = call(
        late_kernel,
        "late",
        24,
        [shape(order + 8, order), square],
        [VMEM] * (6 + len(far)),
        [pltpu.VMEM((2 * count, order - known, order - known), F32)],
        (*parts, *far),
    )
    early_map = swap(late_map, 1)
    g1 = swap(lax.optimization_barrier((g3, early_map))[0], 1)
    m, vec = call(block_kernel, "block", 12, [square, shape(8, order)], [VMEM] * 2, [], (late_map, early_map))

    incoming = [first]
    for block in range(blocks - 1, 0, -1):
        (x,) = call(hop_kernel, "hop", 4, [shape(1, order)], [VMEM] * 3, [], (incoming[-1], m, vec))
        if block % 2:
            x = swap(x, 0, 1)
        else:
            x = lax.ppermute(x, ("tm", "state"), [(block * devices + 1, (block - 1) * devices + 1)])
        incoming.append(x)

    given = list(call(
        functools.partial(last_kernel, devices),
        "last",
        8,
        [shape(steps, panel)] * devices,
        [VMEM] * (blocks + 6),
        [pltpu.VMEM((devices, steps, panel), F32)],
        (*incoming, m, vec, late_map, g3, early_map, g1),
    ))
    for off in range(devices - 1, 0, -1):
        given[off] = swap(given[off], off)
    given = [given[0], *given[:0:-1]]
    (out,) = call(out_kernel, "out", 4, [shape(steps, panel)], [VMEM] * devices, [], given)
    return out


def solution(mesh):
    return jax.shard_map(
        local,
        mesh=mesh,
        in_specs=(
            P("tm", "state", None),
            P("tm", "state", None),
            P("state", None),
            P("tm", None),
            P(),
        ),
        out_specs=P("tm", "state"),
        check_vma=False,
    )
```

```python
import functools

import jax
import jax.numpy as jnp
from jax import lax
from jax.experimental import pallas as pl
from jax.experimental.pallas import tpu as pltpu
from jax.sharding import PartitionSpec as P

F32, BF16 = jnp.float32, jnp.bfloat16
NN = (((1,), (0,)), ((), ()))
NT = (((1,), (1,)), ((), ()))
ANY = pl.BlockSpec(memory_space=pl.ANY)
HBM = pl.BlockSpec(memory_space=pltpu.HBM)
VMEM = pl.BlockSpec(memory_space=pltpu.VMEM)


def split(x):
    high = x.astype(BF16)
    return high, (x - high.astype(F32)).astype(BF16)


def dot3(a, b, dims):
    ah, al = split(a)
    bh, bl = split(b) if hasattr(b, "dtype") and b.dtype == F32 else (b[0][...], b[1][...])
    dot = functools.partial(lax.dot_general, dimension_numbers=dims, preferred_element_type=F32)
    return dot(ah, bh) + (dot(ah, bl) + dot(al, bh))


def matvec(matrix, row):
    order = matrix.shape[1]
    total = matrix[:, :128] * row[:, :128]
    for j in range(128, order, 128):
        total += matrix[:, j : j + 128] * row[:, j : j + 128]
    return jnp.sum(total.T, axis=0, keepdims=True)


def rows(i, panel):
    return pl.ds(pl.multiple_of(i * panel, panel), panel)


def starter(sems):
    copies = []

    def start(source, target):
        copy = pltpu.make_async_copy(source, target, sems.at[len(copies)])
        copy.start()
        copies.append(copy)

    return start, copies


def trimmed(devices, panel):
    return devices == 4 and panel == 128


def far_shape(devices, count, panel, order, off):
    if trimmed(devices, panel):
        return (2 * count, panel * 3 // 4 + (panel if off == 2 else 0), panel)
    return (2 * count, panel, order - 2 * panel)


def fold(block):
    lane = lax.broadcasted_iota(jnp.int32, (32, 128), 1)
    return jnp.concatenate([block[:64], jnp.where(lane < 64, pltpu.roll(block[64:96], 64, 1), block[96:])], axis=0)


def unfold(folded):
    top, right = folded[:64], folded[64:]
    lane = lax.broadcasted_iota(jnp.int32, (64, 128), 1)
    mirrored = jnp.concatenate([top, top], axis=0).T[64:]
    lower = jnp.where(lane < 64, mirrored, jnp.concatenate([pltpu.roll(right, 64, 1), right], axis=0))
    return jnp.concatenate([top, lower], axis=0)


def pack_kernel(devices, cov, prec, trans, terminal, *refs):
    far, (trans_half, first, near, vector, diagonal, sems) = refs[: devices - 2], refs[devices - 2 :]
    count, panel, order = cov.shape[0] // 2, *cov.shape[1:]
    b, s = lax.axis_index("tm"), lax.axis_index("state")
    start, copies = starter(sems)
    start(terminal, vector)
    start(trans.at[pl.ds(pl.multiple_of((b % 2) * (panel // 2), panel // 2), panel // 2), :], trans_half)
    trim = trimmed(devices, panel)
    if trim:
        for k, matrix in enumerate((cov, prec)):
            start(matrix.at[:, :, rows(s, panel)], diagonal.at[k])
    for off, piece in enumerate(far, 2):
        theirs = pl.ds(((s ^ off) % 2) * count, count)
        for k, matrix in enumerate((cov, prec)):
            target = piece.at[pl.ds(k * count, count)]
            if not trim:
                start(matrix.at[theirs, :, 2 * panel :], target)
            elif off == 2:
                start(matrix.at[theirs, :, rows(s ^ 1, panel)], target.at[:, :panel])
    theirs = pl.ds((1 - s % 2) * count, count)
    start(cov.at[theirs], near.at[pl.ds(0, count)])
    start(prec.at[theirs], near.at[pl.ds(count, count)])
    start(trans, near.at[2 * count])
    copies[0].wait()
    first[...] = jnp.where(b == lax.axis_size("tm") - 1, vector[...], 0.0)
    for copy in copies[1:]:
        copy.wait()
    if trim:
        for off, piece in enumerate(far, 2):
            for k in range(2 * count):
                block = diagonal[k // count, ((s ^ off) % 2) * count + k % count]
                piece[k, piece.shape[1] - panel * 3 // 4 :, :] = fold(block)


def join_kernel(*refs):
    moved, (joined, sems) = refs[:-2], refs[-2:]
    half = moved[0].shape[0]
    b = lax.axis_index("tm")
    start, copies = starter(sems)
    for k, piece in enumerate(moved):
        at = (b % 2 if k % 2 == 0 else 1 - b % 2) * half
        start(piece, joined.at[k // 2, pl.ds(pl.multiple_of(at, half), half), :])
    for copy in copies:
        copy.wait()


def early_kernel(cov, prec, trans, means, near, joined, joined_near, *refs):
    info, a_far, l_known, c_known, c_far, g_known, pf, af, lf, sems = refs
    steps, panel, order = cov.shape
    count, known = steps // 2, 2 * panel
    s = lax.axis_index("state")
    e = s % 2
    start, copies = starter(sems)
    for k in range(count):
        step = e * count + k
        start(cov.at[step], pf.at[pl.ds(pl.multiple_of(k * known + e * panel, panel), panel), :])
        start(near.at[k], pf.at[pl.ds(pl.multiple_of(k * known + (1 - e) * panel, panel), panel), :])
        start(prec.at[step], lf.at[k, rows(e, panel), :])
        start(near.at[count + k], lf.at[k, rows(1 - e, panel), :])
    start(trans, af.at[rows(e, panel), :])
    start(near.at[2 * count], af.at[rows(1 - e, panel), :])
    for j in range(1, order // known):
        start(joined.at[j - 1], af.at[rows(e ^ (2 * j), panel), :])
        start(joined_near.at[j - 1], af.at[rows(e ^ (2 * j) ^ 1, panel), :])
    pf[count * known :, :] = jnp.concatenate([means[...], jnp.zeros((16 - steps, order), F32)], axis=0)
    for copy in copies:
        copy.wait()
    product = dot3(pf[...], af[...], NT)
    info[:8] = pf[count * known : count * known + 8, :]
    info[8:] = product[count * known : count * known + 8]
    for half, x in enumerate(split(af[:, known:])):
        a_far[half] = x
    across = jnp.concatenate([pf[k * known : (k + 1) * known, known:].T for k in range(count)], axis=0)
    rest = dot3(across, af[:, :known], NT)
    for k in range(count):
        part = product[k * known : (k + 1) * known]
        for half, x in enumerate(split(lf[k])):
            l_known[k, half] = x
        partial = dot3(part[:, :known], lf[k], NN)
        g_known[k, :, :known] = partial[:, :known] + dot3(part[:, known:], lf[k, :, known:], NT)
        g_known[k, :, known:] = partial[:, known:]
        c_known[k] = part[:, known:]
        c_far[k] = rest[k * (order - known) : (k + 1) * (order - known)]


def late_kernel(info, a_far, l_known, c_known, c_far, g_known, *refs):
    far, (map_ref, gain_ref, ff) = refs[:-3], refs[-3:]
    count, known, order = g_known.shape
    panel = known // 2
    e = lax.axis_index("state") % 2
    for k in range(2 * count):
        if not trimmed(len(far) + 2, panel):
            for off, piece in enumerate(far, 2):
                ff[k, rows((e ^ off) - 2, panel), :] = piece[k]
            continue
        i, j = (e ^ 2) - 2, (e ^ 3) - 2
        beside, folded = far[0][k, :panel], far[0][k, panel:]
        ff[k, rows(i, panel), rows(i, panel)] = unfold(folded)
        ff[k, rows(j, panel), rows(j, panel)] = unfold(far[1][k])
        ff[k, rows(i, panel), rows(j, panel)] = beside
        ff[k, rows(j, panel), rows(i, panel)] = beside.T

    def complete(k):
        c = c_far[k] + dot3(ff[k], a_far, NT)
        known_rows = (l_known.at[k, 0], l_known.at[k, 1])
        share = dot3(jnp.concatenate([c_known[k], c[:, known:]], axis=0), ff[count + k], NN)
        low = dot3(c[:, :known], known_rows, NN)
        left = low[:, :known] + dot3(c[:, known:], [x[:, known:] for x in known_rows], NT)
        top = jnp.concatenate([g_known[k, :, :known], g_known[k, :, known:] + share[:known]], axis=1)
        return jnp.concatenate([top, jnp.concatenate([left, low[:, known:] + share[known:]], axis=1)], axis=0)

    ga, gb = complete(0), complete(1)
    gain_ref[...] = gb
    a = e * count
    mean_a, mean_b = info[pl.ds(a, 1), :], info[pl.ds(a + 1, 1), :]
    pred_a, pred_b = info[pl.ds(a + 8, 1), :], info[pl.ds(a + 9, 1), :]
    map_ref[order:, :] = jnp.concatenate(
        [mean_a + matvec(ga, mean_b - pred_a), mean_b, pred_b, jnp.zeros((5, order), F32)], axis=0
    )
    map_ref[:order, :] = dot3(ga, gb, NN)


def block_kernel(late, early, m_ref, vec_ref):
    order = late.shape[1]
    shift = early[order : order + 1, :] + matvec(
        early[:order, :], late[order : order + 1, :] - early[order + 2 : order + 3, :]
    )
    vec_ref[...] = jnp.concatenate([late[order + 2 : order + 3, :], shift, jnp.zeros((6, order), F32)], axis=0)
    m_ref[...] = dot3(early[:order, :], late[:order, :], NN)


def pair_hop_kernel(x, late, early, out_ref):
    order = x.shape[1]
    y = late[order : order + 1, :] + matvec(late[:order, :], x[...] - late[order + 2 : order + 3, :])
    out_ref[...] = early[order : order + 1, :] + matvec(early[:order, :], y - early[order + 2 : order + 3, :])


def hop_kernel(x, m, vec, out_ref):
    out_ref[...] = vec[1:2, :] + matvec(m[...], x[...] - vec[0:1, :])


def last_kernel(devices, *refs):
    blocks = len(refs) - 7 - devices
    incoming, (m, vec, late, g3, early, g1), outs, cut = refs[:blocks], refs[blocks : blocks + 6], refs[blocks + 6 : -1], refs[-1]
    order, panel = m.shape[1], outs[0].shape[1]
    b, s = lax.axis_index("tm"), lax.axis_index("state")
    x = incoming[0][...]
    for k, ref in enumerate(incoming[1:], 1):
        x = jnp.where(lax.axis_size("tm") - 1 - b == k, ref[...], x)
    gap = x - vec[0:1, :]
    x3 = late[order + 1 : order + 2, :] + matvec(g3[...], gap)
    x2 = late[order : order + 1, :] + matvec(late[:order, :], gap)
    x0 = vec[1:2, :] + matvec(m[...], gap)
    x1 = early[order + 1 : order + 2, :] + matvec(g1[...], x2 - early[order + 2 : order + 3, :])
    full = jnp.concatenate([x0, x1, x2, x3], axis=0)
    for i in range(devices):
        cut[i] = full[:, i * panel : (i + 1) * panel]
    for off, out in enumerate(outs):
        out[...] = cut[s ^ off]


def out_kernel(*refs):
    given, out_ref = [refs[0], *refs[-2:0:-1]], refs[-1]
    off = lax.axis_index("state") ^ 1
    x = given[0][...]
    for k, ref in enumerate(given[1:], 1):
        x = jnp.where(off == k, ref[...], x)
    out_ref[...] = x


def params(mebibytes):
    return pltpu.CompilerParams(vmem_limit_bytes=mebibytes * 2**20)


def local(filtered_covariance, pred_prec, transition, filt_means, terminal_mean):
    steps, panel, order = filtered_covariance.shape
    devices, blocks = lax.axis_size("state"), lax.axis_size("tm")
    count = steps // 2

    def swap(x, off, block_off=0):
        pairs = [(i, i ^ (block_off * devices + off)) for i in range(blocks * devices)]
        return lax.ppermute(x, ("tm", "state"), pairs)

    def shape(*dims):
        return jax.ShapeDtypeStruct(dims, F32)

    def call(kernel, name, mebibytes, outs, in_specs, scratch, args):
        return pl.pallas_call(
            kernel,
            out_shape=outs,
            in_specs=in_specs,
            out_specs=[VMEM] * len(outs),
            scratch_shapes=scratch,
            compiler_params=params(mebibytes),
            name=name,
        )(*args)

    cov, prec, trans, means, terminal = (
        pltpu.with_memory_space_constraint(x, pltpu.HBM)
        for x in (filtered_covariance, pred_prec, transition, filt_means, terminal_mean[None])
    )
    semaphores = pltpu.SemaphoreType.DMA((8 * devices,))
    square = shape(order, order)

    far = [shape(*far_shape(devices, count, panel, order, off)) for off in range(2, devices)]
    *far, trans_half, first, near = call(
        functools.partial(pack_kernel, devices),
        "pack",
        6,
        far + [shape(panel // 2, order), shape(1, order), shape(2 * count + 1, panel, order)],
        [HBM] * 4,
        [pltpu.VMEM((1, order), F32), pltpu.VMEM((2, steps, panel, panel), F32), semaphores],
        (cov, prec, trans, terminal),
    )
    across = [swap(trans_half, off) for off in range(2, devices, 2)]
    far = [swap(x, off) for off, x in enumerate(far, 2)]
    near = swap(near, 1)
    moved = [y for x in across for y in (x, swap(x, 0, 1))]
    (joined,) = call(
        join_kernel, "join", 4, [shape(devices // 2 - 1, panel, order)], [ANY] * len(moved), [semaphores], moved
    )
    joined_near = swap(joined, 1)

    known = 2 * panel
    parts = call(
        early_kernel,
        "early",
        24,
        [
            shape(16, order),
            jax.ShapeDtypeStruct((2, order, order - known), BF16),
            jax.ShapeDtypeStruct((count, 2, known, order), BF16),
            shape(count, known, order - known),
            shape(count, order - known, order),
            shape(count, known, order),
        ],
        [HBM] * 3 + [VMEM] + [ANY] * 3,
        [
            pltpu.VMEM((count * known + 16, order), F32),
            pltpu.VMEM((order, order), F32),
            pltpu.VMEM((count, known, order), F32),
            semaphores,
        ],
        (cov, prec, trans, means, near, joined, joined_near),
    )
    late_map, g3 = call(
        late_kernel,
        "late",
        24,
        [shape(order + 8, order), square],
        [VMEM] * (6 + len(far)),
        [pltpu.VMEM((2 * count, order - known, order - known), F32)],
        (*parts, *far),
    )
    early_map = swap(late_map, 1)
    (x,) = call(pair_hop_kernel, "pair_hop", 4, [shape(1, order)], [VMEM] * 3, [], (first, late_map, early_map))
    g1 = swap(lax.optimization_barrier((g3, x))[0], 1)
    incoming = [first, swap(x, 0, 1)]
    m, vec = call(block_kernel, "block", 12, [square, shape(8, order)], [VMEM] * 2, [], (late_map, early_map))
    for block in range(blocks - 2, 0, -1):
        (x,) = call(hop_kernel, "hop", 4, [shape(1, order)], [VMEM] * 3, [], (incoming[-1], m, vec))
        if block % 2 or block == 2:
            x = swap(x, 0, block ^ (block - 1))
        else:
            x = lax.ppermute(x, ("tm", "state"), [(block * devices + 1, (block - 1) * devices + 1)])
        incoming.append(x)

    given = list(call(
        functools.partial(last_kernel, devices),
        "last",
        8,
        [shape(steps, panel)] * devices,
        [VMEM] * (blocks + 6),
        [pltpu.VMEM((devices, steps, panel), F32)],
        (*incoming, m, vec, late_map, g3, early_map, g1),
    ))
    for off in range(devices - 1, 0, -1):
        given[off] = swap(given[off], off)
    given = [given[0], *given[:0:-1]]
    (out,) = call(out_kernel, "out", 4, [shape(steps, panel)], [VMEM] * devices, [], given)
    return out


def solution(mesh):
    return jax.shard_map(
        local,
        mesh=mesh,
        in_specs=(
            P("tm", "state", None),
            P("tm", "state", None),
            P("state", None),
            P("tm", None),
            P(),
        ),
        out_specs=P("tm", "state"),
        check_vma=False,
    )
```

```python
import functools

import jax
import jax.numpy as jnp
from jax import lax
from jax.experimental import pallas as pl
from jax.experimental.pallas import tpu as pltpu
from jax.sharding import PartitionSpec as P

F32, BF16 = jnp.float32, jnp.bfloat16
NN = (((1,), (0,)), ((), ()))
NT = (((1,), (1,)), ((), ()))
ANY = pl.BlockSpec(memory_space=pl.ANY)
HBM = pl.BlockSpec(memory_space=pltpu.HBM)
VMEM = pl.BlockSpec(memory_space=pltpu.VMEM)


def split(x):
    high = x.astype(BF16)
    return high, (x - high.astype(F32)).astype(BF16)


def dot3(a, b, dims):
    ah, al = split(a)
    bh, bl = split(b) if hasattr(b, "dtype") and b.dtype == F32 else (b[0][...], b[1][...])
    dot = functools.partial(lax.dot_general, dimension_numbers=dims, preferred_element_type=F32)
    return dot(ah, bh) + (dot(ah, bl) + dot(al, bh))


def matvec(matrix, row):
    order = matrix.shape[1]
    total = matrix[:, :128] * row[:, :128]
    for j in range(128, order, 128):
        total += matrix[:, j : j + 128] * row[:, j : j + 128]
    return jnp.sum(total.T, axis=0, keepdims=True)


def rows(i, panel):
    return pl.ds(pl.multiple_of(i * panel, panel), panel)


def starter(sems):
    copies = []

    def start(source, target):
        copy = pltpu.make_async_copy(source, target, sems.at[len(copies)])
        copy.start()
        copies.append(copy)

    return start, copies


def trimmed(devices, panel):
    return devices == 4 and panel == 128


def far_shape(devices, count, panel, order, off):
    if trimmed(devices, panel):
        return (2 * count, panel * 3 // 4 + (panel if off == 2 else 0), panel)
    return (2 * count, panel, order - 2 * panel)


def fold(block):
    lane = lax.broadcasted_iota(jnp.int32, (32, 128), 1)
    return jnp.concatenate([block[:64], jnp.where(lane < 64, pltpu.roll(block[64:96], 64, 1), block[96:])], axis=0)


def unfold(folded):
    top, right = folded[:64], folded[64:]
    lane = lax.broadcasted_iota(jnp.int32, (64, 128), 1)
    mirrored = jnp.concatenate([top, top], axis=0).T[64:]
    lower = jnp.where(lane < 64, mirrored, jnp.concatenate([pltpu.roll(right, 64, 1), right], axis=0))
    return jnp.concatenate([top, lower], axis=0)


def pack_kernel(devices, cov, prec, trans, terminal, *refs):
    far, (trans_half, first, vector, diagonal, sems) = refs[: devices - 2], refs[devices - 2 :]
    count, panel, order = cov.shape[0] // 2, *cov.shape[1:]
    b, s = lax.axis_index("tm"), lax.axis_index("state")
    start, copies = starter(sems)
    start(terminal, vector)
    start(trans.at[pl.ds(pl.multiple_of((b % 2) * (panel // 2), panel // 2), panel // 2), :], trans_half)
    trim = trimmed(devices, panel)
    if trim:
        for k, matrix in enumerate((cov, prec)):
            start(matrix.at[:, :, rows(s, panel)], diagonal.at[k])
    for off, piece in enumerate(far, 2):
        theirs = pl.ds(((s ^ off) % 2) * count, count)
        for k, matrix in enumerate((cov, prec)):
            target = piece.at[pl.ds(k * count, count)]
            if not trim:
                start(matrix.at[theirs, :, 2 * panel :], target)
            elif off == 2:
                start(matrix.at[theirs, :, rows(s ^ 1, panel)], target.at[:, :panel])
    copies[0].wait()
    first[...] = jnp.where(b == lax.axis_size("tm") - 1, vector[...], 0.0)
    for copy in copies[1:]:
        copy.wait()
    if trim:
        for off, piece in enumerate(far, 2):
            for k in range(2 * count):
                block = diagonal[k // count, ((s ^ off) % 2) * count + k % count]
                piece[k, piece.shape[1] - panel * 3 // 4 :, :] = fold(block)


def near_kernel(cov, prec, trans, after, near_cov, near_prec, near_trans, sems):
    count = cov.shape[0] // 2
    theirs = pl.ds((1 - lax.axis_index("state") % 2) * count, count)
    start, copies = starter(sems)
    start(cov.at[theirs], near_cov)
    start(prec.at[theirs], near_prec)
    start(trans, near_trans)
    for copy in copies:
        copy.wait()


def join_kernel(*refs):
    moved, (joined, sems) = refs[:-2], refs[-2:]
    half = moved[0].shape[0]
    b = lax.axis_index("tm")
    start, copies = starter(sems)
    for k, piece in enumerate(moved):
        at = (b % 2 if k % 2 == 0 else 1 - b % 2) * half
        start(piece, joined.at[k // 2, pl.ds(pl.multiple_of(at, half), half), :])
    for copy in copies:
        copy.wait()


def early_kernel(cov, prec, trans, means, near_cov, near_prec, near_trans, joined, joined_near, *refs):
    info, a_far, l_known, c_known, c_far, g_known, pf, af, lf, sems = refs
    steps, panel, order = cov.shape
    count, known = steps // 2, 2 * panel
    s = lax.axis_index("state")
    e = s % 2
    start, copies = starter(sems)
    for k in range(count):
        step = e * count + k
        start(cov.at[step], pf.at[pl.ds(pl.multiple_of(k * known + e * panel, panel), panel), :])
        start(near_cov.at[k], pf.at[pl.ds(pl.multiple_of(k * known + (1 - e) * panel, panel), panel), :])
        start(prec.at[step], lf.at[k, rows(e, panel), :])
        start(near_prec.at[k], lf.at[k, rows(1 - e, panel), :])
    start(trans, af.at[rows(e, panel), :])
    start(near_trans, af.at[rows(1 - e, panel), :])
    for j in range(1, order // known):
        start(joined.at[j - 1], af.at[rows(e ^ (2 * j), panel), :])
        start(joined_near.at[j - 1], af.at[rows(e ^ (2 * j) ^ 1, panel), :])
    pf[count * known :, :] = jnp.concatenate([means[...], jnp.zeros((16 - steps, order), F32)], axis=0)
    for copy in copies:
        copy.wait()
    product = dot3(pf[...], af[...], NT)
    info[:8] = pf[count * known : count * known + 8, :]
    info[8:] = product[count * known : count * known + 8]
    for half, x in enumerate(split(af[:, known:])):
        a_far[half] = x
    across = jnp.concatenate([pf[k * known : (k + 1) * known, known:].T for k in range(count)], axis=0)
    rest = dot3(across, af[:, :known], NT)
    for k in range(count):
        part = product[k * known : (k + 1) * known]
        for half, x in enumerate(split(lf[k])):
            l_known[k, half] = x
        partial = dot3(part[:, :known], lf[k], NN)
        g_known[k, :, :known] = partial[:, :known] + dot3(part[:, known:], lf[k, :, known:], NT)
        g_known[k, :, known:] = partial[:, known:]
        c_known[k] = part[:, known:]
        c_far[k] = rest[k * (order - known) : (k + 1) * (order - known)]


def steps_of(info, count):
    a = (lax.axis_index("state") % 2) * count
    return [info[pl.ds(a + shift, 1), :] for shift in (0, 1, 8, 9)]


def late_kernel(first, info, a_far, l_known, c_known, c_far, g_known, *refs):
    far, (ga_ref, gb_ref, mean_ref, ff) = refs[:-4], refs[-4:]
    count, known, order = g_known.shape
    panel = known // 2
    e = lax.axis_index("state") % 2
    for k in range(2 * count):
        if not trimmed(len(far) + 2, panel):
            for off, piece in enumerate(far, 2):
                ff[k, rows((e ^ off) - 2, panel), :] = piece[k]
            continue
        i, j = (e ^ 2) - 2, (e ^ 3) - 2
        beside, folded = far[0][k, :panel], far[0][k, panel:]
        ff[k, rows(i, panel), rows(i, panel)] = unfold(folded)
        ff[k, rows(j, panel), rows(j, panel)] = unfold(far[1][k])
        ff[k, rows(i, panel), rows(j, panel)] = beside
        ff[k, rows(j, panel), rows(i, panel)] = beside.T

    def complete(k):
        c = c_far[k] + dot3(ff[k], a_far, NT)
        known_rows = (l_known.at[k, 0], l_known.at[k, 1])
        share = dot3(jnp.concatenate([c_known[k], c[:, known:]], axis=0), ff[count + k], NN)
        low = dot3(c[:, :known], known_rows, NN)
        left = low[:, :known] + dot3(c[:, known:], [x[:, known:] for x in known_rows], NT)
        top = jnp.concatenate([g_known[k, :, :known], g_known[k, :, known:] + share[:known]], axis=1)
        return jnp.concatenate([top, jnp.concatenate([left, low[:, known:] + share[known:]], axis=1)], axis=0)

    ga, gb = complete(0), complete(1)
    ga_ref[...] = ga
    gb_ref[...] = gb
    mean_a, mean_b, pred_a, pred_b = steps_of(info, count)
    mean_ref[...] = mean_a + matvec(ga, mean_b + matvec(gb, first[...] - pred_b) - pred_a)


def two_kernel(x, info, ga, gb, out_ref):
    mean_a, mean_b, pred_a, pred_b = steps_of(info, 2)
    out_ref[...] = mean_a + matvec(ga[...], mean_b + matvec(gb[...], x[...] - pred_b) - pred_a)


def pair_kernel(info, ga, gb, map_ref):
    order = ga.shape[1]
    mean_a, mean_b, pred_a, pred_b = steps_of(info, 2)
    map_ref[order:, :] = jnp.concatenate(
        [mean_a + matvec(ga[...], mean_b - pred_a), mean_b, pred_b, jnp.zeros((5, order), F32)], axis=0
    )
    map_ref[:order, :] = dot3(ga[...], gb[...], NN)


def block_kernel(late, early, m_ref, vec_ref):
    order = late.shape[1]
    shift = early[order : order + 1, :] + matvec(
        early[:order, :], late[order : order + 1, :] - early[order + 2 : order + 3, :]
    )
    vec_ref[...] = jnp.concatenate([late[order + 2 : order + 3, :], shift, jnp.zeros((6, order), F32)], axis=0)
    m_ref[...] = dot3(early[:order, :], late[:order, :], NN)


def hop_kernel(x, m, vec, out_ref):
    out_ref[...] = vec[1:2, :] + matvec(m[...], x[...] - vec[0:1, :])


def last_kernel(devices, *refs):
    blocks = len(refs) - 7 - devices
    incoming, (m, vec, late, g3, early, g1), outs, cut = refs[:blocks], refs[blocks : blocks + 6], refs[blocks + 6 : -1], refs[-1]
    order, panel = m.shape[1], outs[0].shape[1]
    b, s = lax.axis_index("tm"), lax.axis_index("state")
    x = incoming[0][...]
    for k, ref in enumerate(incoming[1:], 1):
        x = jnp.where(lax.axis_size("tm") - 1 - b == k, ref[...], x)
    gap = x - vec[0:1, :]
    x3 = late[order + 1 : order + 2, :] + matvec(g3[...], gap)
    x2 = late[order : order + 1, :] + matvec(late[:order, :], gap)
    x0 = vec[1:2, :] + matvec(m[...], gap)
    x1 = early[order + 1 : order + 2, :] + matvec(g1[...], x2 - early[order + 2 : order + 3, :])
    full = jnp.concatenate([x0, x1, x2, x3], axis=0)
    for i in range(devices):
        cut[i] = full[:, i * panel : (i + 1) * panel]
    for off, out in enumerate(outs):
        out[...] = cut[s ^ off]


def out_kernel(*refs):
    given, out_ref = [refs[0], *refs[-2:0:-1]], refs[-1]
    off = lax.axis_index("state") ^ 1
    x = given[0][...]
    for k, ref in enumerate(given[1:], 1):
        x = jnp.where(off == k, ref[...], x)
    out_ref[...] = x


def params(mebibytes):
    return pltpu.CompilerParams(vmem_limit_bytes=mebibytes * 2**20)


def local(filtered_covariance, pred_prec, transition, filt_means, terminal_mean):
    steps, panel, order = filtered_covariance.shape
    devices, blocks = lax.axis_size("state"), lax.axis_size("tm")
    count = steps // 2

    def swap(x, off, block_off=0):
        pairs = [(i, i ^ (block_off * devices + off)) for i in range(blocks * devices)]
        return lax.ppermute(x, ("tm", "state"), pairs)

    def shape(*dims):
        return jax.ShapeDtypeStruct(dims, F32)

    def call(kernel, name, mebibytes, outs, in_specs, scratch, args):
        return pl.pallas_call(
            kernel,
            out_shape=outs,
            in_specs=in_specs,
            out_specs=[VMEM] * len(outs),
            scratch_shapes=scratch,
            compiler_params=params(mebibytes),
            name=name,
        )(*args)

    cov, prec, trans, means, terminal = (
        pltpu.with_memory_space_constraint(x, pltpu.HBM)
        for x in (filtered_covariance, pred_prec, transition, filt_means, terminal_mean[None])
    )
    semaphores = pltpu.SemaphoreType.DMA((8 * devices,))
    square = shape(order, order)

    far = [shape(*far_shape(devices, count, panel, order, off)) for off in range(2, devices)]
    *far, trans_half, first = call(
        functools.partial(pack_kernel, devices),
        "pack",
        6,
        far + [shape(panel // 2, order), shape(1, order)],
        [HBM] * 4,
        [pltpu.VMEM((1, order), F32), pltpu.VMEM((2, steps, panel, panel), F32), semaphores],
        (cov, prec, trans, terminal),
    )
    across = [swap(trans_half, off) for off in range(2, devices, 2)]
    far = [swap(x, off) for off, x in enumerate(far, 2)]
    near = call(
        near_kernel,
        "near",
        4,
        [shape(count, panel, order), shape(count, panel, order), shape(panel, order)],
        [HBM] * 3 + [ANY],
        [semaphores],
        (cov, prec, trans, first),
    )
    near = [swap(x, 1) for x in near]
    moved = [y for x in across for y in (x, swap(x, 0, 1))]
    (joined,) = call(
        join_kernel, "join", 4, [shape(devices // 2 - 1, panel, order)], [ANY] * len(moved), [semaphores], moved
    )
    joined_near = swap(joined, 1)

    known = 2 * panel
    parts = call(
        early_kernel,
        "early",
        24,
        [
            shape(16, order),
            jax.ShapeDtypeStruct((2, order, order - known), BF16),
            jax.ShapeDtypeStruct((count, 2, known, order), BF16),
            shape(count, known, order - known),
            shape(count, order - known, order),
            shape(count, known, order),
        ],
        [HBM] * 3 + [VMEM] + [ANY] * 5,
        [
            pltpu.VMEM((count * known + 16, order), F32),
            pltpu.VMEM((order, order), F32),
            pltpu.VMEM((count, known, order), F32),
            semaphores,
        ],
        (cov, prec, trans, means, *near, joined, joined_near),
    )
    info = parts[0]
    ga, gb, mean = call(
        late_kernel,
        "late",
        24,
        [square, square, shape(1, order)],
        [VMEM] * (7 + len(far)),
        [pltpu.VMEM((2 * count, order - known, order - known), F32)],
        (first, *parts, *far),
    )
    mean = swap(mean, 1)
    (late_map,) = call(pair_kernel, "pair", 12, [shape(order + 8, order)], [VMEM] * 3, [], (info, ga, gb))
    early_map = swap(lax.optimization_barrier((late_map, mean))[0], 1)
    (mean,) = call(two_kernel, "two", 6, [shape(1, order)], [VMEM] * 4, [], (mean, info, ga, gb))

    incoming = [first, swap(mean, 1, 1)]
    m, vec = call(block_kernel, "block", 12, [square, shape(8, order)], [VMEM] * 2, [], (late_map, early_map))
    for block in range(blocks - 2, 0, -1):
        (x,) = call(hop_kernel, "hop", 4, [shape(1, order)], [VMEM] * 3, [], (incoming[-1], m, vec))
        if block % 2:
            x = swap(x, 0, 1)
        else:
            x = lax.ppermute(x, ("tm", "state"), [(block * devices + 1, (block - 1) * devices + 1)])
        incoming.append(x)
    g1 = swap(lax.optimization_barrier((gb, incoming[2]))[0], 1)

    given = list(call(
        functools.partial(last_kernel, devices),
        "last",
        8,
        [shape(steps, panel)] * devices,
        [VMEM] * (blocks + 6),
        [pltpu.VMEM((devices, steps, panel), F32)],
        (*incoming, m, vec, late_map, gb, early_map, g1),
    ))
    for off in range(devices - 1, 0, -1):
        given[off] = swap(given[off], off)
    given = [given[0], *given[:0:-1]]
    (out,) = call(out_kernel, "out", 4, [shape(steps, panel)], [VMEM] * devices, [], given)
    return out


def solution(mesh):
    return jax.shard_map(
        local,
        mesh=mesh,
        in_specs=(
            P("tm", "state", None),
            P("tm", "state", None),
            P("state", None),
            P("tm", None),
            P(),
        ),
        out_specs=P("tm", "state"),
        check_vma=False,
    )
```

```python
import functools

import jax
import jax.numpy as jnp
from jax import lax
from jax.experimental import pallas as pl
from jax.experimental.pallas import tpu as pltpu
from jax.sharding import PartitionSpec as P

F32, BF16 = jnp.float32, jnp.bfloat16
NN = (((1,), (0,)), ((), ()))
NT = (((1,), (1,)), ((), ()))
ANY = pl.BlockSpec(memory_space=pl.ANY)
HBM = pl.BlockSpec(memory_space=pltpu.HBM)
VMEM = pl.BlockSpec(memory_space=pltpu.VMEM)


def split(x):
    high = x.astype(BF16)
    return high, (x - high.astype(F32)).astype(BF16)


def dot3(a, b, dims):
    (ah, al), (bh, bl) = (split(x) if getattr(x, "dtype", None) == F32 else (x[0][...], x[1][...]) for x in (a, b))
    dot = functools.partial(lax.dot_general, dimension_numbers=dims, preferred_element_type=F32)
    return dot(ah, bh) + (dot(ah, bl) + dot(al, bh))


def matvec(matrix, row):
    order = matrix.shape[1]
    total = matrix[:, :128] * row[:, :128]
    for j in range(128, order, 128):
        total += matrix[:, j : j + 128] * row[:, j : j + 128]
    return jnp.sum(total.T, axis=0, keepdims=True)


def rows(i, panel):
    return pl.ds(pl.multiple_of(i * panel, panel), panel)


def starter(sems):
    copies = []

    def start(source, target):
        copy = pltpu.make_async_copy(source, target, sems.at[len(copies)])
        copy.start()
        copies.append(copy)

    return start, copies


def trimmed(devices, panel):
    return devices == 4 and panel == 128


def far_shape(devices, count, panel, order, off):
    if trimmed(devices, panel):
        return (2 * count, panel * 3 // 4 + (panel if off == 2 else 0), panel)
    return (2 * count, panel, order - 2 * panel)


def fold(block):
    lane = lax.broadcasted_iota(jnp.int32, (32, 128), 1)
    return jnp.concatenate([block[:64], jnp.where(lane < 64, pltpu.roll(block[64:96], 64, 1), block[96:])], axis=0)


def unfold(folded):
    top, right = folded[:64], folded[64:]
    lane = lax.broadcasted_iota(jnp.int32, (64, 128), 1)
    mirrored = jnp.concatenate([top, top], axis=0).T[64:]
    lower = jnp.where(lane < 64, mirrored, jnp.concatenate([pltpu.roll(right, 64, 1), right], axis=0))
    return jnp.concatenate([top, lower], axis=0)


def pack_kernel(devices, cov, prec, trans, terminal, *refs):
    far, (trans_half, first, vector, diagonal, sems) = refs[: devices - 2], refs[devices - 2 :]
    count, panel, order = cov.shape[0] // 2, *cov.shape[1:]
    b, s = lax.axis_index("tm"), lax.axis_index("state")
    start, copies = starter(sems)
    start(terminal, vector)
    start(trans.at[pl.ds(pl.multiple_of((b % 2) * (panel // 2), panel // 2), panel // 2), :], trans_half)
    trim = trimmed(devices, panel)
    if trim:
        for k, matrix in enumerate((cov, prec)):
            start(matrix.at[:, :, rows(s, panel)], diagonal.at[k])
    for off, piece in enumerate(far, 2):
        theirs = pl.ds(((s ^ off) % 2) * count, count)
        for k, matrix in enumerate((cov, prec)):
            target = piece.at[pl.ds(k * count, count)]
            if not trim:
                start(matrix.at[theirs, :, 2 * panel :], target)
            elif off == 2:
                start(matrix.at[theirs, :, rows(s ^ 1, panel)], target.at[:, :panel])
    copies[0].wait()
    first[...] = jnp.where(b == lax.axis_size("tm") - 1, vector[...], 0.0)
    for copy in copies[1:]:
        copy.wait()
    if trim:
        for off, piece in enumerate(far, 2):
            for k in range(2 * count):
                block = diagonal[k // count, ((s ^ off) % 2) * count + k % count]
                piece[k, piece.shape[1] - panel * 3 // 4 :, :] = fold(block)


def near_kernel(cov, prec, trans, after, near_cov, near_prec, near_trans, sems):
    count = cov.shape[0] // 2
    theirs = pl.ds((1 - lax.axis_index("state") % 2) * count, count)
    start, copies = starter(sems)
    start(cov.at[theirs], near_cov)
    start(prec.at[theirs], near_prec)
    start(trans, near_trans)
    for copy in copies:
        copy.wait()


def near_kernel(cov, prec, after, *refs):
    pieces, sems = refs[:-1], refs[-1]
    count, panel = cov.shape[0] // 2, cov.shape[1]
    first = (1 - lax.axis_index("state") % 2) * count
    start, copies = starter(sems)
    for k in range(2 * count):
        matrix = (cov, prec)[k // count]
        for piece, at, source, size in spans(pieces, k, panel):
            start(matrix.at[first + k % count, pl.ds(source, size), :], pieces[piece].at[pl.ds(at, size), :])
    for copy in copies:
        copy.wait()


def spans(pieces, k, panel):
    found, base = [], 0
    for i, piece in enumerate(pieces):
        low, high = max(base, k * panel), min(base + piece.shape[0], (k + 1) * panel)
        if low < high:
            found.append((i, low - base, low - k * panel, high - low))
        base += piece.shape[0]
    return found


def own_kernel(cov, prec, trans, means, after, own, own_trans, own_means, sems):
    count = cov.shape[0] // 2
    mine = pl.ds((lax.axis_index("state") % 2) * count, count)
    start, copies = starter(sems)
    start(cov.at[mine], own.at[pl.ds(0, count)])
    start(prec.at[mine], own.at[pl.ds(count, count)])
    start(trans, own_trans)
    start(means, own_means)
    for copy in copies:
        copy.wait()


def join_kernel(after, *refs):
    moved, (joined, sems) = refs[:-2], refs[-2:]
    half = moved[0].shape[0]
    b = lax.axis_index("tm")
    start, copies = starter(sems)
    for k, piece in enumerate(moved):
        at = (b % 2 if k % 2 == 0 else 1 - b % 2) * half
        start(piece, joined.at[k // 2, pl.ds(pl.multiple_of(at, half), half), :])
    for copy in copies:
        copy.wait()


def early_kernel(own, means, trans, trans_near, joined, joined_near, *refs):
    near, (info, a_far, l_known, c_known, c_far, g_known, pf, af, lf, sems) = refs[:-10], refs[-10:]
    panel, order = own.shape[1:]
    count, known = own.shape[0] // 2, 2 * panel
    steps = means.shape[0]
    e = lax.axis_index("state") % 2
    start, copies = starter(sems)
    for k in range(2 * count):
        target, base = (pf, k * known) if k < count else (lf.at[k - count], 0)
        start(own.at[k], target.at[pl.ds(pl.multiple_of(base + e * panel, panel), panel), :])
        for piece, at, row, size in spans(near, k, panel):
            to = pl.multiple_of(base + (1 - e) * panel + row, 8)
            start(near[piece].at[pl.ds(at, size), :], target.at[pl.ds(to, size), :])
    for j in range(order // known):
        mine, theirs = (joined.at[j - 1], joined_near.at[j - 1]) if j else (trans, trans_near)
        start(mine, af.at[rows(e ^ (2 * j), panel), :])
        start(theirs, af.at[rows(e ^ (2 * j) ^ 1, panel), :])
    pf[count * known :, :] = jnp.concatenate([means[...], jnp.zeros((16 - steps, order), F32)], axis=0)
    for copy in copies:
        copy.wait()
    product = dot3(pf[...], af[...], NT)
    info[:8] = pf[count * known : count * known + 8, :]
    info[8:] = product[count * known : count * known + 8]
    for half, x in enumerate(split(af[:, known:].T)):
        a_far[half] = x
    across = jnp.concatenate([pf[k * known : (k + 1) * known, known:].T for k in range(count)], axis=0)
    rest = dot3(across, af[:, :known], NT)
    for k in range(count):
        part = product[k * known : (k + 1) * known]
        for half, x in enumerate(split(lf[k])):
            l_known[k, half] = x
        partial = dot3(part[:, :known], lf[k], NN)
        g_known[k, :, :known] = partial[:, :known] + dot3(part[:, known:], lf[k, :, known:], NT)
        g_known[k, :, known:] = partial[:, known:]
        c_known[k] = part[:, known:]
        c_far[k] = rest[k * (order - known) : (k + 1) * (order - known)]


def steps_of(info, count):
    a = (lax.axis_index("state") % 2) * count
    return [info[pl.ds(a + shift, 1), :] for shift in (0, 1, 8, 9)]


def far_row(j, panel):
    return pl.ds(pl.multiple_of(j * panel, panel), panel)


def middle_kernel(a_far, l_known, c_known, c_far, g_known, *refs):
    far, (ga_ref, gb_ref, col_ref, h_ref, ff) = refs[:-5], refs[-5:]
    count, known, order = g_known.shape
    panel = known // 2
    e = lax.axis_index("state") % 2
    i, j = e, 1 - e
    for k in range(2 * count):
        if len(far) > 1:
            for off, piece in enumerate(far, 2):
                ff[k, rows((e ^ off) - 2, panel), :] = piece[k]
            continue
        beside, folded = far[0][k, :panel], far[0][k, panel:]
        ff[k, rows(i, panel), rows(i, panel)] = unfold(folded)
        ff[k, rows(j, panel), rows(j, panel)] = jnp.zeros((panel, panel), F32)
        ff[k, rows(i, panel), rows(j, panel)] = beside
        ff[k, rows(j, panel), rows(i, panel)] = beside.T

    for k, out in enumerate((ga_ref, gb_ref)):
        c = c_far[k] + dot3(ff[k], a_far, NN)
        known_rows = (l_known.at[k, 0], l_known.at[k, 1])
        known_far = [x[:, known:] for x in known_rows]
        l_far = split(ff[count + k])
        column = jnp.concatenate([c_known[k], c[:, known:]], axis=0)
        share = dot3(column, l_far, NN)
        low = dot3(c[:, :known], known_rows, NN)
        out[:known, :known] = g_known[k, :, :known]
        out[:known, known:] = g_known[k, :, known:] + share[:known]
        out[known:, :known] = low[:, :known] + dot3(c[:, known:], known_far, NT)
        out[known:, known:] = low[:, known:] + share[known:]
        if len(far) == 1:
            col_ref[k] = jnp.where(j == 0, column[:, :panel], column[:, panel:])
            halves = a_far[0, far_row(j, panel), :], a_far[1, far_row(j, panel), :]
            head, tail = [x[:, :known] for x in halves], [x[:, known:] for x in halves]
            h = dot3(head, known_rows, NN)
            h_ref[k, :, :known] = h[:, :known] + dot3(tail, known_far, NT)
            h_ref[k, :, known:] = h[:, known:] + dot3(tail, l_far, NN)


def steps_of(info, count):
    a = (lax.axis_index("state") % 2) * count
    return [info[pl.ds(a + shift, 1), :] for shift in (0, 1, 8, 9)]


def late_kernel(first, info, a_far, ga, gb, col, h, *refs):
    far, (ga_ref, gb_ref, mean_ref) = refs[:-3], refs[-3:]
    count, panel, order = h.shape
    j = 1 - lax.axis_index("state") % 2
    for k, (gain, out) in enumerate(((ga, ga_ref), (gb, gb_ref))):
        out[...] = gain[...]
        if far:
            at = far_row(2 + j, panel)
            p_last, l_last = unfold(far[0][k]), unfold(far[0][count + k])
            corner = [a_far[half, far_row(j, panel), at] for half in range(2)]
            out[at, :] += dot3(p_last, h[k], NN)
            out[:, at] += dot3(col[k], l_last, NN)
            out[at, at] += dot3(dot3(p_last, corner, NN), l_last, NN)
    mean_a, mean_b, pred_a, pred_b = steps_of(info, count)
    mean_ref[...] = mean_a + matvec(ga_ref[...], mean_b + matvec(gb_ref[...], first[...] - pred_b) - pred_a)


def two_kernel(x, info, ga, gb, out_ref):
    mean_a, mean_b, pred_a, pred_b = steps_of(info, 2)
    out_ref[...] = mean_a + matvec(ga[...], mean_b + matvec(gb[...], x[...] - pred_b) - pred_a)


def pair_kernel(info, ga, gb, map_ref):
    order = ga.shape[1]
    mean_a, mean_b, pred_a, pred_b = steps_of(info, 2)
    map_ref[order:, :] = jnp.concatenate(
        [mean_a + matvec(ga[...], mean_b - pred_a), mean_b, pred_b, jnp.zeros((5, order), F32)], axis=0
    )
    map_ref[:order, :] = dot3(ga[...], gb[...], NN)


def block_kernel(late, early, m_ref, vec_ref):
    order = late.shape[1]
    shift = early[order : order + 1, :] + matvec(
        early[:order, :], late[order : order + 1, :] - early[order + 2 : order + 3, :]
    )
    vec_ref[...] = jnp.concatenate([late[order + 2 : order + 3, :], shift, jnp.zeros((6, order), F32)], axis=0)
    m_ref[...] = dot3(early[:order, :], late[:order, :], NN)


def hop_kernel(x, m, vec, out_ref):
    out_ref[...] = vec[1:2, :] + matvec(m[...], x[...] - vec[0:1, :])


def last_kernel(devices, *refs):
    blocks = len(refs) - 7 - devices
    incoming, (m, vec, late, g3, early, g1), outs, cut = refs[:blocks], refs[blocks : blocks + 6], refs[blocks + 6 : -1], refs[-1]
    order, panel = m.shape[1], outs[0].shape[1]
    b, s = lax.axis_index("tm"), lax.axis_index("state")
    x = incoming[0][...]
    for k, ref in enumerate(incoming[1:], 1):
        x = jnp.where(lax.axis_size("tm") - 1 - b == k, ref[...], x)
    gap = x - vec[0:1, :]
    x3 = late[order + 1 : order + 2, :] + matvec(g3[...], gap)
    x2 = late[order : order + 1, :] + matvec(late[:order, :], gap)
    x0 = vec[1:2, :] + matvec(m[...], gap)
    x1 = early[order + 1 : order + 2, :] + matvec(g1[...], x2 - early[order + 2 : order + 3, :])
    full = jnp.concatenate([x0, x1, x2, x3], axis=0)
    for i in range(devices):
        cut[i] = full[:, i * panel : (i + 1) * panel]
    for off, out in enumerate(outs):
        out[...] = cut[s ^ off]


def out_kernel(*refs):
    given, out_ref = [refs[0], *refs[-2:0:-1]], refs[-1]
    off = lax.axis_index("state") ^ 1
    x = given[0][...]
    for k, ref in enumerate(given[1:], 1):
        x = jnp.where(off == k, ref[...], x)
    out_ref[...] = x


def params(mebibytes):
    return pltpu.CompilerParams(vmem_limit_bytes=mebibytes * 2**20)


def local(filtered_covariance, pred_prec, transition, filt_means, terminal_mean):
    steps, panel, order = filtered_covariance.shape
    devices, blocks = lax.axis_size("state"), lax.axis_size("tm")
    count = steps // 2

    def swap(x, off, block_off=0):
        pairs = [(i, i ^ (block_off * devices + off)) for i in range(blocks * devices)]
        return lax.ppermute(x, ("tm", "state"), pairs)

    def shape(*dims):
        return jax.ShapeDtypeStruct(dims, F32)

    def call(kernel, name, mebibytes, outs, in_specs, scratch, args):
        return pl.pallas_call(
            kernel,
            out_shape=outs,
            in_specs=in_specs,
            out_specs=[VMEM] * len(outs),
            scratch_shapes=scratch,
            compiler_params=params(mebibytes),
            name=name,
        )(*args)

    cov, prec, trans, means, terminal = (
        pltpu.with_memory_space_constraint(x, pltpu.HBM)
        for x in (filtered_covariance, pred_prec, transition, filt_means, terminal_mean[None])
    )
    semaphores = pltpu.SemaphoreType.DMA((8 * devices,))
    square = shape(order, order)

    far = [shape(*far_shape(devices, count, panel, order, off)) for off in range(2, devices)]
    *far, trans_half, first = call(
        functools.partial(pack_kernel, devices),
        "pack",
        6,
        far + [shape(panel // 2, order), shape(1, order)],
        [HBM] * 4,
        [pltpu.VMEM((1, order), F32), pltpu.VMEM((2, steps, panel, panel), F32), semaphores],
        (cov, prec, trans, terminal),
    )
    across = [swap(trans_half, off) for off in range(2, devices, 2)]
    far = [swap(x, off) for off, x in enumerate(far, 2)]
    moved = [y for x in across for y in (x, swap(x, 0, 1))]
    near = call(
        near_kernel,
        "near",
        4,
        [shape(count * panel, order)] * 2,
        [HBM] * 2 + [ANY],
        [semaphores],
        (cov, prec, first),
    )
    near = [swap(x, 1) for x in near]
    own, own_trans, own_means = call(
        own_kernel,
        "own",
        4,
        [shape(2 * count, panel, order), shape(panel, order), shape(steps, order)],
        [HBM] * 4 + [ANY],
        [semaphores],
        (cov, prec, trans, means, across[0]),
    )
    (joined,) = call(
        join_kernel,
        "join",
        4,
        [shape(devices // 2 - 1, panel, order)],
        [ANY] * (1 + len(moved)),
        [semaphores],
        (own_trans, *moved),
    )
    joined_near = swap(joined, 1)
    trans_near = swap(transition, 1)

    known = 2 * panel
    parts = call(
        early_kernel,
        "early",
        24,
        [
            shape(16, order),
            jax.ShapeDtypeStruct((2, order - known, order), BF16),
            jax.ShapeDtypeStruct((count, 2, known, order), BF16),
            shape(count, known, order - known),
            shape(count, order - known, order),
            shape(count, known, order),
        ],
        [ANY, VMEM] + [ANY] * 2 + [ANY] * 4,
        [
            pltpu.VMEM((count * known + 16, order), F32),
            pltpu.VMEM((order, order), F32),
            pltpu.VMEM((count, known, order), F32),
            semaphores,
        ],
        (own, own_means, own_trans, trans_near, joined, joined_near, *near),
    )
    info, a_far = parts[:2]
    last = far[1:] if trimmed(devices, panel) else []
    ga, gb, col, h = call(
        middle_kernel,
        "middle",
        24,
        [square, square, shape(count, order, panel), shape(count, panel, order)],
        [VMEM] * (5 + len(far) - len(last)),
        [pltpu.VMEM((2 * count, order - known, order - known), F32)],
        (*parts[1:], *far[: len(far) - len(last)]),
    )
    ga, gb, mean = call(
        late_kernel,
        "late",
        12,
        [square, square, shape(1, order)],
        [VMEM] * (7 + len(last)),
        [],
        (first, info, a_far, ga, gb, col, h, *last),
    )
    mean = swap(mean, 1)
    (late_map,) = call(pair_kernel, "pair", 12, [shape(order + 8, order)], [VMEM] * 3, [], (info, ga, gb))
    early_map = swap(lax.optimization_barrier((late_map, mean))[0], 1)
    (mean,) = call(two_kernel, "two", 6, [shape(1, order)], [VMEM] * 4, [], (mean, info, ga, gb))

    incoming = [first, swap(mean, 1, 1)]
    m, vec = call(block_kernel, "block", 12, [square, shape(8, order)], [VMEM] * 2, [], (late_map, early_map))
    for block in range(blocks - 2, 0, -1):
        (x,) = call(hop_kernel, "hop", 4, [shape(1, order)], [VMEM] * 3, [], (incoming[-1], m, vec))
        if block % 2:
            x = swap(x, 0, 1)
        else:
            x = lax.ppermute(x, ("tm", "state"), [(block * devices + 1, (block - 1) * devices + 1)])
        incoming.append(x)
    g1 = swap(lax.optimization_barrier((gb, incoming[2]))[0], 1)

    given = list(call(
        functools.partial(last_kernel, devices),
        "last",
        8,
        [shape(steps, panel)] * devices,
        [VMEM] * (blocks + 6),
        [pltpu.VMEM((devices, steps, panel), F32)],
        (*incoming, m, vec, late_map, gb, early_map, g1),
    ))
    for off in range(devices - 1, 0, -1):
        given[off] = swap(given[off], off)
    given = [given[0], *given[:0:-1]]
    (out,) = call(out_kernel, "out", 4, [shape(steps, panel)], [VMEM] * devices, [], given)
    return out


def solution(mesh):
    return jax.shard_map(
        local,
        mesh=mesh,
        in_specs=(
            P("tm", "state", None),
            P("tm", "state", None),
            P("state", None),
            P("tm", None),
            P(),
        ),
        out_specs=P("tm", "state"),
        check_vma=False,
    )
```

```python
import functools

import jax
import jax.numpy as jnp
from jax import lax
from jax.experimental import pallas as pl
from jax.experimental.pallas import tpu as pltpu
from jax.sharding import PartitionSpec as P

F32, BF16 = jnp.float32, jnp.bfloat16
NN = (((1,), (0,)), ((), ()))
NT = (((1,), (1,)), ((), ()))
ANY = pl.BlockSpec(memory_space=pl.ANY)
HBM = pl.BlockSpec(memory_space=pltpu.HBM)
VMEM = pl.BlockSpec(memory_space=pltpu.VMEM)


def split(x):
    high = x.astype(BF16)
    return high, (x - high.astype(F32)).astype(BF16)


def dot3(a, b, dims):
    (ah, al), (bh, bl) = (split(x) if getattr(x, "dtype", None) == F32 else (x[0][...], x[1][...]) for x in (a, b))
    dot = functools.partial(lax.dot_general, dimension_numbers=dims, preferred_element_type=F32)
    return dot(ah, bh) + (dot(ah, bl) + dot(al, bh))


def matvec(matrix, row):
    order = matrix.shape[1]
    total = matrix[:, :128] * row[:, :128]
    for j in range(128, order, 128):
        total += matrix[:, j : j + 128] * row[:, j : j + 128]
    return jnp.sum(total.T, axis=0, keepdims=True)


def rows(i, panel):
    return pl.ds(pl.multiple_of(i * panel, panel), panel)


def starter(sems):
    copies = []

    def start(source, target):
        copy = pltpu.make_async_copy(source, target, sems.at[len(copies)])
        copy.start()
        copies.append(copy)

    return start, copies


def trimmed(devices, panel):
    return devices == 4 and panel == 128


def far_shape(devices, count, panel, order, off):
    if trimmed(devices, panel):
        return (2 * count, panel * 3 // 4 + (panel if off == 2 else 0), panel)
    return (2 * count, panel, order - 2 * panel)


def fold(block):
    lane = lax.broadcasted_iota(jnp.int32, (32, 128), 1)
    return jnp.concatenate([block[:64], jnp.where(lane < 64, pltpu.roll(block[64:96], 64, 1), block[96:])], axis=0)


def unfold(folded):
    top, right = folded[:64], folded[64:]
    lane = lax.broadcasted_iota(jnp.int32, (64, 128), 1)
    mirrored = jnp.concatenate([top, top], axis=0).T[64:]
    lower = jnp.where(lane < 64, mirrored, jnp.concatenate([pltpu.roll(right, 64, 1), right], axis=0))
    return jnp.concatenate([top, lower], axis=0)


def pack_kernel(devices, cov, prec, trans, terminal, *refs):
    far, (trans_half, first, vector, diagonal, sems) = refs[: devices - 2], refs[devices - 2 :]
    count, panel, order = cov.shape[0] // 2, *cov.shape[1:]
    b, s = lax.axis_index("tm"), lax.axis_index("state")
    start, copies = starter(sems)
    start(terminal, vector)
    start(trans.at[pl.ds(pl.multiple_of((b % 2) * (panel // 2), panel // 2), panel // 2), :], trans_half)
    trim = trimmed(devices, panel)
    if trim:
        for k, matrix in enumerate((cov, prec)):
            start(matrix.at[:, :, rows(s, panel)], diagonal.at[k])
    for off, piece in enumerate(far, 2):
        theirs = pl.ds(((s ^ off) % 2) * count, count)
        for k, matrix in enumerate((cov, prec)):
            target = piece.at[pl.ds(k * count, count)]
            if not trim:
                start(matrix.at[theirs, :, 2 * panel :], target)
            elif off == 2:
                start(matrix.at[theirs, :, rows(s ^ 1, panel)], target.at[:, :panel])
    copies[0].wait()
    first[...] = jnp.where(b == lax.axis_size("tm") - 1, vector[...], 0.0)
    for copy in copies[1:]:
        copy.wait()
    if trim:
        for off, piece in enumerate(far, 2):
            for k in range(2 * count):
                block = diagonal[k // count, ((s ^ off) % 2) * count + k % count]
                piece[k, piece.shape[1] - panel * 3 // 4 :, :] = fold(block)


def near_kernel(cov, prec, trans, after, near_cov, near_prec, near_trans, sems):
    count = cov.shape[0] // 2
    theirs = pl.ds((1 - lax.axis_index("state") % 2) * count, count)
    start, copies = starter(sems)
    start(cov.at[theirs], near_cov)
    start(prec.at[theirs], near_prec)
    start(trans, near_trans)
    for copy in copies:
        copy.wait()


def near_kernel(cov, prec, after, *refs):
    pieces, sems = refs[:-1], refs[-1]
    count, panel = cov.shape[0] // 2, cov.shape[1]
    first = (1 - lax.axis_index("state") % 2) * count
    start, copies = starter(sems)
    for k in range(2 * count):
        matrix = (cov, prec)[k // count]
        for piece, at, source, size in spans(pieces, k, panel):
            start(matrix.at[first + k % count, pl.ds(source, size), :], pieces[piece].at[pl.ds(at, size), :])
    for copy in copies:
        copy.wait()


def spans(pieces, k, panel):
    found, base = [], 0
    for i, piece in enumerate(pieces):
        low, high = max(base, k * panel), min(base + piece.shape[0], (k + 1) * panel)
        if low < high:
            found.append((i, low - base, low - k * panel, high - low))
        base += piece.shape[0]
    return found


def own_kernel(cov, prec, trans, means, after, own, own_trans, own_means, sems):
    count = cov.shape[0] // 2
    mine = pl.ds((lax.axis_index("state") % 2) * count, count)
    start, copies = starter(sems)
    start(cov.at[mine], own.at[pl.ds(0, count)])
    start(prec.at[mine], own.at[pl.ds(count, count)])
    start(trans, own_trans)
    start(means, own_means)
    for copy in copies:
        copy.wait()


def join_kernel(after, *refs):
    moved, (joined, sems) = refs[:-2], refs[-2:]
    half = moved[0].shape[0]
    b = lax.axis_index("tm")
    start, copies = starter(sems)
    for k, piece in enumerate(moved):
        at = (b % 2 if k % 2 == 0 else 1 - b % 2) * half
        start(piece, joined.at[k // 2, pl.ds(pl.multiple_of(at, half), half), :])
    for copy in copies:
        copy.wait()


def early_kernel(own, means, trans, trans_near, joined, joined_near, *refs):
    near, (info, a_far, l_known, c_known, c_far, g_known, pf, af, lf, sems) = refs[:-10], refs[-10:]
    panel, order = own.shape[1:]
    count, known = own.shape[0] // 2, 2 * panel
    steps = means.shape[0]
    e = lax.axis_index("state") % 2
    start, copies = starter(sems)
    for k in range(2 * count):
        target, base = (pf, k * known) if k < count else (lf.at[k - count], 0)
        start(own.at[k], target.at[pl.ds(pl.multiple_of(base + e * panel, panel), panel), :])
        for piece, at, row, size in spans(near, k, panel):
            to = pl.multiple_of(base + (1 - e) * panel + row, 8)
            start(near[piece].at[pl.ds(at, size), :], target.at[pl.ds(to, size), :])
    for j in range(order // known):
        mine, theirs = (joined.at[j - 1], joined_near.at[j - 1]) if j else (trans, trans_near)
        start(mine, af.at[rows(e ^ (2 * j), panel), :])
        start(theirs, af.at[rows(e ^ (2 * j) ^ 1, panel), :])
    pf[count * known :, :] = jnp.concatenate([means[...], jnp.zeros((16 - steps, order), F32)], axis=0)
    for copy in copies:
        copy.wait()
    product = dot3(pf[...], af[...], NT)
    info[:8] = pf[count * known : count * known + 8, :]
    info[8:] = product[count * known : count * known + 8]
    for half, x in enumerate(split(af[:, known:].T)):
        a_far[half] = x
    across = jnp.concatenate([pf[k * known : (k + 1) * known, known:].T for k in range(count)], axis=0)
    rest = dot3(across, af[:, :known], NT)
    for k in range(count):
        part = product[k * known : (k + 1) * known]
        for half, x in enumerate(split(lf[k])):
            l_known[k, half] = x
        partial = dot3(part[:, :known], lf[k], NN)
        g_known[k, :, :known] = partial[:, :known] + dot3(part[:, known:], lf[k, :, known:], NT)
        g_known[k, :, known:] = partial[:, known:]
        c_known[k] = part[:, known:]
        c_far[k] = rest[k * (order - known) : (k + 1) * (order - known)]


def steps_of(info, count):
    a = (lax.axis_index("state") % 2) * count
    return [info[pl.ds(a + shift, 1), :] for shift in (0, 1, 8, 9)]


def far_row(j, panel):
    return pl.ds(pl.multiple_of(j * panel, panel), panel)


def middle_kernel(a_far, l_known, c_known, c_far, g_known, *refs):
    far, (ga_ref, gb_ref, col_ref, h_ref, ff) = refs[:-5], refs[-5:]
    count, known, order = g_known.shape
    panel = known // 2
    e = lax.axis_index("state") % 2
    i, j = e, 1 - e
    for k in range(2 * count):
        if len(far) > 1:
            for off, piece in enumerate(far, 2):
                ff[k, rows((e ^ off) - 2, panel), :] = piece[k]
            continue
        beside, folded = far[0][k, :panel], far[0][k, panel:]
        ff[k, rows(i, panel), rows(i, panel)] = unfold(folded)
        ff[k, rows(j, panel), rows(j, panel)] = jnp.zeros((panel, panel), F32)
        ff[k, rows(i, panel), rows(j, panel)] = beside
        ff[k, rows(j, panel), rows(i, panel)] = beside.T

    for k, out in enumerate((ga_ref, gb_ref)):
        c = c_far[k] + dot3(ff[k], a_far, NN)
        known_rows = (l_known.at[k, 0], l_known.at[k, 1])
        known_far = [x[:, known:] for x in known_rows]
        l_far = split(ff[count + k])
        column = jnp.concatenate([c_known[k], c[:, known:]], axis=0)
        share = dot3(column, l_far, NN)
        low = dot3(c[:, :known], known_rows, NN)
        out[:known, :known] = g_known[k, :, :known]
        out[:known, known:] = g_known[k, :, known:] + share[:known]
        out[known:, :known] = low[:, :known] + dot3(c[:, known:], known_far, NT)
        out[known:, known:] = low[:, known:] + share[known:]
        if len(far) == 1:
            col_ref[k] = jnp.where(j == 0, column[:, :panel], column[:, panel:])
            halves = a_far[0, far_row(j, panel), :], a_far[1, far_row(j, panel), :]
            head, tail = [x[:, :known] for x in halves], [x[:, known:] for x in halves]
            h = dot3(head, known_rows, NN)
            h_ref[k, :, :known] = h[:, :known] + dot3(tail, known_far, NT)
            h_ref[k, :, known:] = h[:, known:] + dot3(tail, l_far, NN)


def steps_of(info, count):
    a = (lax.axis_index("state") % 2) * count
    return [info[pl.ds(a + shift, 1), :] for shift in (0, 1, 8, 9)]


def late_kernel(first, info, a_far, ga, gb, col, h, *refs):
    far, (ga_ref, gb_ref, mean_ref) = refs[:-3], refs[-3:]
    count, panel, order = h.shape
    j = 1 - lax.axis_index("state") % 2
    for k, (gain, out) in enumerate(((ga, ga_ref), (gb, gb_ref))):
        out[...] = gain[...]
        if far:
            at = far_row(2 + j, panel)
            p_last, l_last = unfold(far[0][k]), unfold(far[0][count + k])
            corner = [a_far[half, far_row(j, panel), at] for half in range(2)]
            out[at, :] += dot3(p_last, h[k], NN)
            out[:, at] += dot3(col[k], l_last, NN)
            out[at, at] += dot3(dot3(p_last, corner, NN), l_last, NN)
    mean_a, mean_b, pred_a, pred_b = steps_of(info, count)
    mean_ref[...] = mean_a + matvec(ga_ref[...], mean_b + matvec(gb_ref[...], first[...] - pred_b) - pred_a)


def two_kernel(x, info, ga, gb, out_ref):
    mean_a, mean_b, pred_a, pred_b = steps_of(info, 2)
    out_ref[...] = mean_a + matvec(ga[...], mean_b + matvec(gb[...], x[...] - pred_b) - pred_a)


def pair_kernel(info, ga, gb, map_ref):
    order = ga.shape[1]
    mean_a, mean_b, pred_a, pred_b = steps_of(info, 2)
    map_ref[order:, :] = jnp.concatenate(
        [mean_a + matvec(ga[...], mean_b - pred_a), mean_b, pred_b, jnp.zeros((5, order), F32)], axis=0
    )
    map_ref[:order, :] = dot3(ga[...], gb[...], NN)


def block_kernel(late, early, m_ref, vec_ref):
    order = late.shape[1]
    shift = early[order : order + 1, :] + matvec(
        early[:order, :], late[order : order + 1, :] - early[order + 2 : order + 3, :]
    )
    vec_ref[...] = jnp.concatenate([late[order + 2 : order + 3, :], shift, jnp.zeros((6, order), F32)], axis=0)
    m_ref[...] = dot3(early[:order, :], late[:order, :], NN)


def hop_kernel(x, m, vec, out_ref):
    out_ref[...] = vec[1:2, :] + matvec(m[...], x[...] - vec[0:1, :])


def last_kernel(devices, *refs):
    blocks = len(refs) - 7 - devices
    incoming, (m, vec, late, g3, early, g1), outs, cut = refs[:blocks], refs[blocks : blocks + 6], refs[blocks + 6 : -1], refs[-1]
    order, panel = m.shape[1], outs[0].shape[1]
    b, s = lax.axis_index("tm"), lax.axis_index("state")
    x = incoming[0][...]
    for k, ref in enumerate(incoming[1:], 1):
        x = jnp.where(lax.axis_size("tm") - 1 - b == k, ref[...], x)
    gap = x - vec[0:1, :]
    x3 = late[order + 1 : order + 2, :] + matvec(g3[...], gap)
    x2 = late[order : order + 1, :] + matvec(late[:order, :], gap)
    x0 = vec[1:2, :] + matvec(m[...], gap)
    x1 = early[order + 1 : order + 2, :] + matvec(g1[...], x2 - early[order + 2 : order + 3, :])
    full = jnp.concatenate([x0, x1, x2, x3], axis=0)
    for i in range(devices):
        cut[i] = full[:, i * panel : (i + 1) * panel]
    for off, out in enumerate(outs):
        out[...] = cut[s ^ off]


def out_kernel(*refs):
    given, out_ref = [refs[0], *refs[-2:0:-1]], refs[-1]
    off = lax.axis_index("state") ^ 1
    x = given[0][...]
    for k, ref in enumerate(given[1:], 1):
        x = jnp.where(off == k, ref[...], x)
    out_ref[...] = x


def params(mebibytes):
    return pltpu.CompilerParams(vmem_limit_bytes=mebibytes * 2**20)


def local(filtered_covariance, pred_prec, transition, filt_means, terminal_mean):
    steps, panel, order = filtered_covariance.shape
    devices, blocks = lax.axis_size("state"), lax.axis_size("tm")
    count = steps // 2

    def swap(x, off, block_off=0):
        pairs = [(i, i ^ (block_off * devices + off)) for i in range(blocks * devices)]
        return lax.ppermute(x, ("tm", "state"), pairs)

    def shape(*dims):
        return jax.ShapeDtypeStruct(dims, F32)

    def call(kernel, name, mebibytes, outs, in_specs, scratch, args):
        return pl.pallas_call(
            kernel,
            out_shape=outs,
            in_specs=in_specs,
            out_specs=[VMEM] * len(outs),
            scratch_shapes=scratch,
            compiler_params=params(mebibytes),
            name=name,
        )(*args)

    cov, prec, trans, means, terminal = (
        pltpu.with_memory_space_constraint(x, pltpu.HBM)
        for x in (filtered_covariance, pred_prec, transition, filt_means, terminal_mean[None])
    )
    semaphores = pltpu.SemaphoreType.DMA((8 * devices,))
    square = shape(order, order)

    far = [shape(*far_shape(devices, count, panel, order, off)) for off in range(2, devices)]
    *far, trans_half, first = call(
        functools.partial(pack_kernel, devices),
        "pack",
        6,
        far + [shape(panel // 2, order), shape(1, order)],
        [HBM] * 4,
        [pltpu.VMEM((1, order), F32), pltpu.VMEM((2, steps, panel, panel), F32), semaphores],
        (cov, prec, trans, terminal),
    )
    across = [swap(trans_half, off) for off in range(2, devices, 2)]
    far = [swap(x, off) for off, x in enumerate(far, 2)]
    moved = [y for x in across for y in (x, swap(x, 0, 1))]
    near = call(
        near_kernel,
        "near",
        4,
        [shape(count * panel, order)] * 2,
        [HBM] * 2 + [ANY],
        [semaphores],
        (cov, prec, first),
    )
    near = [swap(x, 1) for x in near]
    own, own_trans, own_means = call(
        own_kernel,
        "own",
        4,
        [shape(2 * count, panel, order), shape(panel, order), shape(steps, order)],
        [HBM] * 4 + [ANY],
        [semaphores],
        (cov, prec, trans, means, across[0]),
    )
    (joined,) = call(
        join_kernel,
        "join",
        4,
        [shape(devices // 2 - 1, panel, order)],
        [ANY] * (1 + len(moved)),
        [semaphores],
        (own_trans, *moved),
    )
    joined_near = swap(joined, 1)
    trans_near = swap(transition, 1)

    known = 2 * panel
    parts = call(
        early_kernel,
        "early",
        24,
        [
            shape(16, order),
            jax.ShapeDtypeStruct((2, order - known, order), BF16),
            jax.ShapeDtypeStruct((count, 2, known, order), BF16),
            shape(count, known, order - known),
            shape(count, order - known, order),
            shape(count, known, order),
        ],
        [ANY, VMEM] + [ANY] * 2 + [ANY] * 4,
        [
            pltpu.VMEM((count * known + 16, order), F32),
            pltpu.VMEM((order, order), F32),
            pltpu.VMEM((count, known, order), F32),
            semaphores,
        ],
        (own, own_means, own_trans, trans_near, joined, joined_near, *near),
    )
    info, a_far = parts[:2]
    last = far[1:] if trimmed(devices, panel) else []
    ga, gb, col, h = call(
        middle_kernel,
        "middle",
        24,
        [square, square, shape(count, order, panel), shape(count, panel, order)],
        [VMEM] * (5 + len(far) - len(last)),
        [pltpu.VMEM((2 * count, order - known, order - known), F32)],
        (*parts[1:], *far[: len(far) - len(last)]),
    )
    ga, gb, mean = call(
        late_kernel,
        "late",
        12,
        [square, square, shape(1, order)],
        [VMEM] * (7 + len(last)),
        [],
        (first, info, a_far, ga, gb, col, h, *last),
    )
    mean = swap(mean, 1)
    (late_map,) = call(pair_kernel, "pair", 12, [shape(order + 8, order)], [VMEM] * 3, [], (info, ga, gb))
    early_map = swap(lax.optimization_barrier((late_map, mean))[0], 1)
    (mean,) = call(two_kernel, "two", 6, [shape(1, order)], [VMEM] * 4, [], (mean, info, ga, gb))

    incoming = [first, swap(mean, 1, 1)]
    m, vec = call(block_kernel, "block", 12, [square, shape(8, order)], [VMEM] * 2, [], (late_map, early_map))
    for block in range(blocks - 2, 0, -1):
        (x,) = call(hop_kernel, "hop", 4, [shape(1, order)], [VMEM] * 3, [], (incoming[-1], m, vec))
        partner = {at * devices + i: to * devices + i for at, to in ((block, block - 1), (block - 1, block)) for i in range(2)}
        x = lax.ppermute(x, ("tm", "state"), [(i, partner.get(i, i ^ 1)) for i in range(blocks * devices)])
        incoming.append(x)
    g1 = swap(lax.optimization_barrier((gb, incoming[2]))[0], 1)

    given = list(call(
        functools.partial(last_kernel, devices),
        "last",
        8,
        [shape(steps, panel)] * devices,
        [VMEM] * (blocks + 6),
        [pltpu.VMEM((devices, steps, panel), F32)],
        (*incoming, m, vec, late_map, gb, early_map, g1),
    ))
    for off in range(devices - 1, 0, -1):
        given[off] = swap(given[off], off)
    given = [given[0], *given[:0:-1]]
    (out,) = call(out_kernel, "out", 4, [shape(steps, panel)], [VMEM] * devices, [], given)
    return out


def solution(mesh):
    return jax.shard_map(
        local,
        mesh=mesh,
        in_specs=(
            P("tm", "state", None),
            P("tm", "state", None),
            P("state", None),
            P("tm", None),
            P(),
        ),
        out_specs=P("tm", "state"),
        check_vma=False,
    )
```

```python
import functools

import jax
import jax.numpy as jnp
from jax import lax
from jax.experimental import pallas as pl
from jax.experimental.pallas import tpu as pltpu
from jax.sharding import PartitionSpec as P

F32, BF16 = jnp.float32, jnp.bfloat16
NN = (((1,), (0,)), ((), ()))
NT = (((1,), (1,)), ((), ()))
ANY = pl.BlockSpec(memory_space=pl.ANY)
HBM = pl.BlockSpec(memory_space=pltpu.HBM)
VMEM = pl.BlockSpec(memory_space=pltpu.VMEM)


def split(x):
    high = x.astype(BF16)
    return high, (x - high.astype(F32)).astype(BF16)


def dot3(a, b, dims):
    (ah, al), (bh, bl) = (split(x) if getattr(x, "dtype", None) == F32 else (x[0][...], x[1][...]) for x in (a, b))
    dot = functools.partial(lax.dot_general, dimension_numbers=dims, preferred_element_type=F32)
    return dot(ah, bh) + (dot(ah, bl) + dot(al, bh))


def matvec(matrix, row):
    order = matrix.shape[1]
    total = matrix[:, :128] * row[:, :128]
    for j in range(128, order, 128):
        total += matrix[:, j : j + 128] * row[:, j : j + 128]
    return jnp.sum(total.T, axis=0, keepdims=True)


def rows(i, panel):
    return pl.ds(pl.multiple_of(i * panel, panel), panel)


def starter(sems):
    copies = []

    def start(source, target):
        copy = pltpu.make_async_copy(source, target, sems.at[len(copies)])
        copy.start()
        copies.append(copy)

    return start, copies


def trimmed(devices, panel):
    return devices == 4 and panel == 128


def far_shape(devices, count, panel, order, off):
    if trimmed(devices, panel):
        return (2 * count, panel * 3 // 4 + (panel if off == 2 else 0), panel)
    return (2 * count, panel, order - 2 * panel)


def fold(block):
    lane = lax.broadcasted_iota(jnp.int32, (32, 128), 1)
    return jnp.concatenate([block[:64], jnp.where(lane < 64, pltpu.roll(block[64:96], 64, 1), block[96:])], axis=0)


def unfold(folded):
    top, right = folded[:64], folded[64:]
    lane = lax.broadcasted_iota(jnp.int32, (64, 128), 1)
    mirrored = jnp.concatenate([top, top], axis=0).T[64:]
    lower = jnp.where(lane < 64, mirrored, jnp.concatenate([pltpu.roll(right, 64, 1), right], axis=0))
    return jnp.concatenate([top, lower], axis=0)


def pack_kernel(devices, cov, prec, trans, terminal, *refs):
    far, (trans_half, first, vector, diagonal, sems) = refs[: devices - 2], refs[devices - 2 :]
    count, panel, order = cov.shape[0] // 2, *cov.shape[1:]
    b, s = lax.axis_index("tm"), lax.axis_index("state")
    start, copies = starter(sems)
    start(terminal, vector)
    start(trans.at[pl.ds(pl.multiple_of((b % 2) * (panel // 2), panel // 2), panel // 2), :], trans_half)
    trim = trimmed(devices, panel)
    if trim:
        for k, matrix in enumerate((cov, prec)):
            start(matrix.at[:, :, rows(s, panel)], diagonal.at[k])
    for off, piece in enumerate(far, 2):
        theirs = pl.ds(((s ^ off) % 2) * count, count)
        for k, matrix in enumerate((cov, prec)):
            target = piece.at[pl.ds(k * count, count)]
            if not trim:
                start(matrix.at[theirs, :, 2 * panel :], target)
            elif off == 2:
                start(matrix.at[theirs, :, rows(s ^ 1, panel)], target.at[:, :panel])
    copies[0].wait()
    first[...] = jnp.where(b == lax.axis_size("tm") - 1, vector[...], 0.0)
    for copy in copies[1:]:
        copy.wait()
    if trim:
        for off, piece in enumerate(far, 2):
            for k in range(2 * count):
                block = diagonal[k // count, ((s ^ off) % 2) * count + k % count]
                piece[k, piece.shape[1] - panel * 3 // 4 :, :] = fold(block)


def near_kernel(cov, prec, trans, after, near_cov, near_prec, near_trans, sems):
    count = cov.shape[0] // 2
    theirs = pl.ds((1 - lax.axis_index("state") % 2) * count, count)
    start, copies = starter(sems)
    start(cov.at[theirs], near_cov)
    start(prec.at[theirs], near_prec)
    start(trans, near_trans)
    for copy in copies:
        copy.wait()


def near_kernel(cov, prec, after, *refs):
    pieces, sems = refs[:-1], refs[-1]
    count, panel = cov.shape[0] // 2, cov.shape[1]
    first = (1 - lax.axis_index("state") % 2) * count
    start, copies = starter(sems)
    for k in range(2 * count):
        matrix = (cov, prec)[k // count]
        for piece, at, source, size in spans(pieces, k, panel):
            start(matrix.at[first + k % count, pl.ds(source, size), :], pieces[piece].at[pl.ds(at, size), :])
    for copy in copies:
        copy.wait()


def spans(pieces, k, panel):
    found, base = [], 0
    for i, piece in enumerate(pieces):
        low, high = max(base, k * panel), min(base + piece.shape[0], (k + 1) * panel)
        if low < high:
            found.append((i, low - base, low - k * panel, high - low))
        base += piece.shape[0]
    return found


def own_kernel(cov, prec, trans, means, after, own, own_trans, own_means, sems):
    count = cov.shape[0] // 2
    mine = pl.ds((lax.axis_index("state") % 2) * count, count)
    start, copies = starter(sems)
    start(cov.at[mine], own.at[pl.ds(0, count)])
    start(prec.at[mine], own.at[pl.ds(count, count)])
    start(trans, own_trans)
    start(means, own_means)
    for copy in copies:
        copy.wait()


def join_kernel(after, *refs):
    moved, (joined, sems) = refs[:-2], refs[-2:]
    half = moved[0].shape[0]
    b = lax.axis_index("tm")
    start, copies = starter(sems)
    for k, piece in enumerate(moved):
        at = (b % 2 if k % 2 == 0 else 1 - b % 2) * half
        start(piece, joined.at[k // 2, pl.ds(pl.multiple_of(at, half), half), :])
    for copy in copies:
        copy.wait()


def early_kernel(own, means, trans, trans_near, joined, joined_near, *refs):
    near, (info, a_far, l_known, c_known, c_far, g_known, pf, af, lf, sems) = refs[:-10], refs[-10:]
    panel, order = own.shape[1:]
    count, known = own.shape[0] // 2, 2 * panel
    steps = means.shape[0]
    e = lax.axis_index("state") % 2
    start, copies = starter(sems)
    for k in range(2 * count):
        target, base = (pf, k * known) if k < count else (lf.at[k - count], 0)
        start(own.at[k], target.at[pl.ds(pl.multiple_of(base + e * panel, panel), panel), :])
        for piece, at, row, size in spans(near, k, panel):
            to = pl.multiple_of(base + (1 - e) * panel + row, 8)
            start(near[piece].at[pl.ds(at, size), :], target.at[pl.ds(to, size), :])
    for j in range(order // known):
        mine, theirs = (joined.at[j - 1], joined_near.at[j - 1]) if j else (trans, trans_near)
        start(mine, af.at[rows(e ^ (2 * j), panel), :])
        start(theirs, af.at[rows(e ^ (2 * j) ^ 1, panel), :])
    pf[count * known :, :] = jnp.concatenate([means[...], jnp.zeros((16 - steps, order), F32)], axis=0)
    for copy in copies:
        copy.wait()
    product = dot3(pf[...], af[...], NT)
    info[:8] = pf[count * known : count * known + 8, :]
    info[8:] = product[count * known : count * known + 8]
    for half, x in enumerate(split(af[:, known:].T)):
        a_far[half] = x
    across = jnp.concatenate([pf[k * known : (k + 1) * known, known:].T for k in range(count)], axis=0)
    rest = dot3(across, af[:, :known], NT)
    for k in range(count):
        part = product[k * known : (k + 1) * known]
        for half, x in enumerate(split(lf[k])):
            l_known[k, half] = x
        partial = dot3(part[:, :known], lf[k], NN)
        g_known[k, :, :known] = partial[:, :known] + dot3(part[:, known:], lf[k, :, known:], NT)
        g_known[k, :, known:] = partial[:, known:]
        c_known[k] = part[:, known:]
        c_far[k] = rest[k * (order - known) : (k + 1) * (order - known)]


def steps_of(info, count):
    a = (lax.axis_index("state") % 2) * count
    return [info[pl.ds(a + shift, 1), :] for shift in (0, 1, 8, 9)]


def far_row(j, panel):
    return pl.ds(pl.multiple_of(j * panel, panel), panel)


def middle_kernel(a_far, l_known, c_known, c_far, g_known, *refs):
    far, (ga_ref, gb_ref, col_ref, h_ref, ff) = refs[:-5], refs[-5:]
    count, known, order = g_known.shape
    panel = known // 2
    e = lax.axis_index("state") % 2
    i, j = e, 1 - e
    for k in range(2 * count):
        if len(far) > 1:
            for off, piece in enumerate(far, 2):
                ff[k, rows((e ^ off) - 2, panel), :] = piece[k]
            continue
        beside, folded = far[0][k, :panel], far[0][k, panel:]
        ff[k, rows(i, panel), rows(i, panel)] = unfold(folded)
        ff[k, rows(j, panel), rows(j, panel)] = jnp.zeros((panel, panel), F32)
        ff[k, rows(i, panel), rows(j, panel)] = beside
        ff[k, rows(j, panel), rows(i, panel)] = beside.T

    for k, out in enumerate((ga_ref, gb_ref)):
        c = c_far[k] + dot3(ff[k], a_far, NN)
        known_rows = (l_known.at[k, 0], l_known.at[k, 1])
        known_far = [x[:, known:] for x in known_rows]
        l_far = split(ff[count + k])
        column = jnp.concatenate([c_known[k], c[:, known:]], axis=0)
        share = dot3(column, l_far, NN)
        low = dot3(c[:, :known], known_rows, NN)
        out[:known, :known] = g_known[k, :, :known]
        out[:known, known:] = g_known[k, :, known:] + share[:known]
        out[known:, :known] = low[:, :known] + dot3(c[:, known:], known_far, NT)
        out[known:, known:] = low[:, known:] + share[known:]
        if len(far) == 1:
            col_ref[k] = jnp.where(j == 0, column[:, :panel], column[:, panel:])
            halves = a_far[0, far_row(j, panel), :], a_far[1, far_row(j, panel), :]
            head, tail = [x[:, :known] for x in halves], [x[:, known:] for x in halves]
            h = dot3(head, known_rows, NN)
            h_ref[k, :, :known] = h[:, :known] + dot3(tail, known_far, NT)
            h_ref[k, :, known:] = h[:, known:] + dot3(tail, l_far, NN)


def steps_of(info, count):
    a = (lax.axis_index("state") % 2) * count
    return [info[pl.ds(a + shift, 1), :] for shift in (0, 1, 8, 9)]


def late_kernel(first, info, a_far, ga, gb, col, h, *refs):
    far, (ga_ref, gb_ref, mean_ref) = refs[:-3], refs[-3:]
    count, panel, order = h.shape
    j = 1 - lax.axis_index("state") % 2
    for k, (gain, out) in enumerate(((ga, ga_ref), (gb, gb_ref))):
        out[...] = gain[...]
        if far:
            at = far_row(2 + j, panel)
            p_last, l_last = unfold(far[0][k]), unfold(far[0][count + k])
            corner = [a_far[half, far_row(j, panel), at] for half in range(2)]
            out[at, :] += dot3(p_last, h[k], NN)
            out[:, at] += dot3(col[k], l_last, NN)
            out[at, at] += dot3(dot3(p_last, corner, NN), l_last, NN)
    mean_a, mean_b, pred_a, pred_b = steps_of(info, count)
    mean_ref[...] = mean_a + matvec(ga_ref[...], mean_b + matvec(gb_ref[...], first[...] - pred_b) - pred_a)


def two_kernel(x, info, ga, gb, out_ref):
    mean_a, mean_b, pred_a, pred_b = steps_of(info, 2)
    out_ref[...] = mean_a + matvec(ga[...], mean_b + matvec(gb[...], x[...] - pred_b) - pred_a)


def pair_kernel(info, ga, gb, map_ref):
    order = ga.shape[1]
    mean_a, mean_b, pred_a, pred_b = steps_of(info, 2)
    map_ref[order:, :] = jnp.concatenate(
        [mean_a + matvec(ga[...], mean_b - pred_a), mean_b, pred_b, jnp.zeros((5, order), F32)], axis=0
    )
    map_ref[:order, :] = dot3(ga[...], gb[...], NN)


def block_kernel(late, early, m_ref, vec_ref):
    order = late.shape[1]
    shift = early[order : order + 1, :] + matvec(
        early[:order, :], late[order : order + 1, :] - early[order + 2 : order + 3, :]
    )
    vec_ref[...] = jnp.concatenate([late[order + 2 : order + 3, :], shift, jnp.zeros((6, order), F32)], axis=0)
    m_ref[...] = dot3(early[:order, :], late[:order, :], NN)


def hop_kernel(x, m, vec, out_ref):
    out_ref[...] = vec[1:2, :] + matvec(m[...], x[...] - vec[0:1, :])


def last_kernel(devices, *refs):
    blocks = len(refs) - 7 - devices
    incoming, (m, vec, late, g3, early, g1), outs, cut = refs[:blocks], refs[blocks : blocks + 6], refs[blocks + 6 : -1], refs[-1]
    order, panel = m.shape[1], outs[0].shape[1]
    b, s = lax.axis_index("tm"), lax.axis_index("state")
    x = incoming[0][...]
    for k, ref in enumerate(incoming[1:], 1):
        x = jnp.where(lax.axis_size("tm") - 1 - b == k, ref[...], x)
    gap = x - vec[0:1, :]
    x3 = late[order + 1 : order + 2, :] + matvec(g3[...], gap)
    x2 = late[order : order + 1, :] + matvec(late[:order, :], gap)
    x0 = vec[1:2, :] + matvec(m[...], gap)
    x1 = early[order + 1 : order + 2, :] + matvec(g1[...], x2 - early[order + 2 : order + 3, :])
    full = jnp.concatenate([x0, x1, x2, x3], axis=0)
    for i in range(devices):
        cut[i] = full[:, i * panel : (i + 1) * panel]
    for off, out in enumerate(outs):
        out[...] = cut[s ^ off]


def out_kernel(*refs):
    given, out_ref = [refs[0], *refs[-2:0:-1]], refs[-1]
    off = lax.axis_index("state") ^ 1
    x = given[0][...]
    for k, ref in enumerate(given[1:], 1):
        x = jnp.where(off == k, ref[...], x)
    out_ref[...] = x


def params(mebibytes):
    return pltpu.CompilerParams(vmem_limit_bytes=mebibytes * 2**20)


def local(filtered_covariance, pred_prec, transition, filt_means, terminal_mean):
    steps, panel, order = filtered_covariance.shape
    devices, blocks = lax.axis_size("state"), lax.axis_size("tm")
    count = steps // 2

    def swap(x, off, block_off=0):
        pairs = [(i, i ^ (block_off * devices + off)) for i in range(blocks * devices)]
        return lax.ppermute(x, ("tm", "state"), pairs)

    def shape(*dims):
        return jax.ShapeDtypeStruct(dims, F32)

    def call(kernel, name, mebibytes, outs, in_specs, scratch, args):
        return pl.pallas_call(
            kernel,
            out_shape=outs,
            in_specs=in_specs,
            out_specs=[VMEM] * len(outs),
            scratch_shapes=scratch,
            compiler_params=params(mebibytes),
            name=name,
        )(*args)

    cov, prec, trans, means, terminal = (
        pltpu.with_memory_space_constraint(x, pltpu.HBM)
        for x in (filtered_covariance, pred_prec, transition, filt_means, terminal_mean[None])
    )
    semaphores = pltpu.SemaphoreType.DMA((8 * devices,))
    square = shape(order, order)

    far = [shape(*far_shape(devices, count, panel, order, off)) for off in range(2, devices)]
    *far, trans_half, first = call(
        functools.partial(pack_kernel, devices),
        "pack",
        6,
        far + [shape(panel // 2, order), shape(1, order)],
        [HBM] * 4,
        [pltpu.VMEM((1, order), F32), pltpu.VMEM((2, steps, panel, panel), F32), semaphores],
        (cov, prec, trans, terminal),
    )
    across = [swap(trans_half, off) for off in range(2, devices, 2)]
    far = [swap(x, off) for off, x in enumerate(far, 2)]
    moved = [y for x in across for y in (x, swap(x, 0, 1))]
    near = call(
        near_kernel,
        "near",
        4,
        [shape(count * panel, order)] * 2,
        [HBM] * 2 + [ANY],
        [semaphores],
        (cov, prec, first),
    )
    near = [swap(x, 1) for x in near]
    own, own_trans, own_means = call(
        own_kernel,
        "own",
        4,
        [shape(2 * count, panel, order), shape(panel, order), shape(steps, order)],
        [HBM] * 4 + [ANY],
        [semaphores],
        (cov, prec, trans, means, across[0]),
    )
    (joined,) = call(
        join_kernel,
        "join",
        4,
        [shape(devices // 2 - 1, panel, order)],
        [ANY] * (1 + len(moved)),
        [semaphores],
        (own_trans, *moved),
    )
    joined_near = swap(joined, 1)
    trans_near = swap(transition, 1)

    known = 2 * panel
    parts = call(
        early_kernel,
        "early",
        24,
        [
            shape(16, order),
            jax.ShapeDtypeStruct((2, order - known, order), BF16),
            jax.ShapeDtypeStruct((count, 2, known, order), BF16),
            shape(count, known, order - known),
            shape(count, order - known, order),
            shape(count, known, order),
        ],
        [ANY, VMEM] + [ANY] * 2 + [ANY] * 4,
        [
            pltpu.VMEM((count * known + 16, order), F32),
            pltpu.VMEM((order, order), F32),
            pltpu.VMEM((count, known, order), F32),
            semaphores,
        ],
        (own, own_means, own_trans, trans_near, joined, joined_near, *near),
    )
    info, a_far = parts[:2]
    last = far[1:] if trimmed(devices, panel) else []
    ga, gb, col, h = call(
        middle_kernel,
        "middle",
        24,
        [square, square, shape(count, order, panel), shape(count, panel, order)],
        [VMEM] * (5 + len(far) - len(last)),
        [pltpu.VMEM((2 * count, order - known, order - known), F32)],
        (*parts[1:], *far[: len(far) - len(last)]),
    )
    ga, gb, mean = call(
        late_kernel,
        "late",
        12,
        [square, square, shape(1, order)],
        [VMEM] * (7 + len(last)),
        [],
        (first, info, a_far, ga, gb, col, h, *last),
    )
    mean = swap(mean, 1)
    (late_map,) = call(pair_kernel, "pair", 12, [shape(order + 8, order)], [VMEM] * 3, [], (info, ga, gb))
    early_map = swap(lax.optimization_barrier((late_map, mean))[0], 1)
    (mean,) = call(two_kernel, "two", 6, [shape(1, order)], [VMEM] * 4, [], (mean, info, ga, gb))

    incoming = [first, swap(mean, 1, 1)]
    m, vec = call(block_kernel, "block", 12, [square, shape(8, order)], [VMEM] * 2, [], (late_map, early_map))
    for block in range(blocks - 2, 0, -1):
        (x,) = call(hop_kernel, "hop", 4, [shape(1, order)], [VMEM] * 3, [], (incoming[-1], m, vec))
        target = {i: i ^ 1 for i in range(blocks * devices)}
        for at, to in ((block, block - 1), (block - 1, block)):
            target[at * devices + 1] = to * devices + 1
            target.update({at * devices + i: at * devices + j for i, j in ((0, 2), (2, 3), (3, 0))})
        x = lax.ppermute(x, ("tm", "state"), list(target.items()))
        incoming.append(x)
    g1 = swap(lax.optimization_barrier((gb, incoming[2]))[0], 1)

    given = list(call(
        functools.partial(last_kernel, devices),
        "last",
        8,
        [shape(steps, panel)] * devices,
        [VMEM] * (blocks + 6),
        [pltpu.VMEM((devices, steps, panel), F32)],
        (*incoming, m, vec, late_map, gb, early_map, g1),
    ))
    for off in range(devices - 1, 0, -1):
        given[off] = swap(given[off], off)
    given = [given[0], *given[:0:-1]]
    (out,) = call(out_kernel, "out", 4, [shape(steps, panel)], [VMEM] * devices, [], given)
    return out


def solution(mesh):
    return jax.shard_map(
        local,
        mesh=mesh,
        in_specs=(
            P("tm", "state", None),
            P("tm", "state", None),
            P("state", None),
            P("tm", None),
            P(),
        ),
        out_specs=P("tm", "state"),
        check_vma=False,
    )
```

```python
import functools

import jax
import jax.numpy as jnp
from jax import lax
from jax.experimental import pallas as pl
from jax.experimental.pallas import tpu as pltpu
from jax.sharding import PartitionSpec as P

F32, BF16 = jnp.float32, jnp.bfloat16
NN = (((1,), (0,)), ((), ()))
NT = (((1,), (1,)), ((), ()))
ANY = pl.BlockSpec(memory_space=pl.ANY)
HBM = pl.BlockSpec(memory_space=pltpu.HBM)
VMEM = pl.BlockSpec(memory_space=pltpu.VMEM)


def split(x):
    high = x.astype(BF16)
    return high, (x - high.astype(F32)).astype(BF16)


def dot3(a, b, dims):
    (ah, al), (bh, bl) = (split(x) if getattr(x, "dtype", None) == F32 else (x[0][...], x[1][...]) for x in (a, b))
    dot = functools.partial(lax.dot_general, dimension_numbers=dims, preferred_element_type=F32)
    return dot(ah, bh) + (dot(ah, bl) + dot(al, bh))


def matvec(matrix, row):
    order = matrix.shape[1]
    total = matrix[:, :128] * row[:, :128]
    for j in range(128, order, 128):
        total += matrix[:, j : j + 128] * row[:, j : j + 128]
    return jnp.sum(total.T, axis=0, keepdims=True)


def rows(i, panel):
    return pl.ds(pl.multiple_of(i * panel, panel), panel)


def starter(sems):
    copies = []

    def start(source, target):
        copy = pltpu.make_async_copy(source, target, sems.at[len(copies)])
        copy.start()
        copies.append(copy)

    return start, copies


def trimmed(devices, panel):
    return devices == 4 and panel == 128


def far_shape(devices, count, panel, order, off):
    if trimmed(devices, panel):
        return (2 * count, panel * 5 // 8 + (panel if off == 2 else 0), panel)
    return (2 * count, panel, order - 2 * panel)


def lanes(rows):
    return lax.broadcasted_iota(jnp.int32, (rows, 128), 1)


def fold(block):
    corner = jnp.where(lanes(32) < 32, pltpu.roll(block[96:], 32, 1), block[32:64])
    third = jnp.where(lanes(16) < 64, pltpu.roll(block[64:80], 64, 1), block[80:96])
    return jnp.concatenate([block[:32], corner, third], axis=0)


def unfold(folded):
    corner, third = folded[32:64], folded[64:]
    upper = jnp.concatenate(
        [folded[:64], pltpu.roll(third, 64, 1), third, pltpu.roll(corner, 96, 1)], axis=0
    )
    row = lax.broadcasted_iota(jnp.int32, (128, 128), 0)
    return jnp.where(row // 32 <= lanes(128) // 32, upper, upper.T)


def base(device, count):
    return (1 - device % 2) * count


def pack_kernel(devices, cov, prec, trans, terminal, *refs):
    far, (trans_half, first, vector, diagonal, sems) = refs[: devices - 2], refs[devices - 2 :]
    count, panel, order = cov.shape[0] // 2, *cov.shape[1:]
    b, s = lax.axis_index("tm"), lax.axis_index("state")
    start, copies = starter(sems)
    start(terminal, vector)
    start(trans.at[pl.ds(pl.multiple_of((b % 2) * (panel // 2), panel // 2), panel // 2), :], trans_half)
    trim = trimmed(devices, panel)
    if trim:
        for k, matrix in enumerate((cov, prec)):
            start(matrix.at[:, :, rows(s, panel)], diagonal.at[k])
    for off, piece in enumerate(far, 2):
        theirs = pl.ds(base(s ^ off, count), count)
        for k, matrix in enumerate((cov, prec)):
            target = piece.at[pl.ds(k * count, count)]
            if not trim:
                start(matrix.at[theirs, :, 2 * panel :], target)
            elif off == 2:
                start(matrix.at[theirs, :, rows(s ^ 1, panel)], target.at[:, :panel])
    copies[0].wait()
    first[...] = jnp.where(b == lax.axis_size("tm") - 1, vector[...], 0.0)
    for copy in copies[1:]:
        copy.wait()
    if trim:
        for off, piece in enumerate(far, 2):
            for k in range(2 * count):
                block = diagonal[k // count, base(s ^ off, count) + k % count]
                piece[k, piece.shape[1] - panel * 5 // 8 :, :] = fold(block)


def near_kernel(cov, prec, trans, after, near_cov, near_prec, near_trans, sems):
    count = cov.shape[0] // 2
    theirs = pl.ds((1 - lax.axis_index("state") % 2) * count, count)
    start, copies = starter(sems)
    start(cov.at[theirs], near_cov)
    start(prec.at[theirs], near_prec)
    start(trans, near_trans)
    for copy in copies:
        copy.wait()


def near_kernel(cov, prec, after, *refs):
    pieces, sems = refs[:-1], refs[-1]
    count, panel = cov.shape[0] // 2, cov.shape[1]
    first = base(lax.axis_index("state") ^ 1, count)
    start, copies = starter(sems)
    for k in range(2 * count):
        matrix = (cov, prec)[k // count]
        for piece, at, source, size in spans(pieces, k, panel):
            start(matrix.at[first + k % count, pl.ds(source, size), :], pieces[piece].at[pl.ds(at, size), :])
    for copy in copies:
        copy.wait()


def spans(pieces, k, panel):
    found, at = [], 0
    for i, piece in enumerate(pieces):
        low, high = max(at, k * panel), min(at + piece.shape[0], (k + 1) * panel)
        if low < high:
            found.append((i, low - at, low - k * panel, high - low))
        at += piece.shape[0]
    return found


def own_kernel(cov, prec, trans, means, after, own, own_trans, own_means, sems):
    count = cov.shape[0] // 2
    mine = pl.ds(base(lax.axis_index("state"), count), count)
    start, copies = starter(sems)
    start(cov.at[mine], own.at[pl.ds(0, count)])
    start(prec.at[mine], own.at[pl.ds(count, count)])
    start(trans, own_trans)
    start(means, own_means)
    for copy in copies:
        copy.wait()


def join_kernel(after, *refs):
    moved, (joined, sems) = refs[:-2], refs[-2:]
    half = moved[0].shape[0]
    b = lax.axis_index("tm")
    start, copies = starter(sems)
    for k, piece in enumerate(moved):
        at = (b % 2 if k % 2 == 0 else 1 - b % 2) * half
        start(piece, joined.at[k // 2, pl.ds(pl.multiple_of(at, half), half), :])
    for copy in copies:
        copy.wait()


def early_kernel(own, means, trans, trans_near, joined, joined_near, *refs):
    near, (info, a_far, l_known, c_known, c_far, g_known, pf, af, lf, sems) = refs[:-10], refs[-10:]
    panel, order = own.shape[1:]
    count, known = own.shape[0] // 2, 2 * panel
    steps = means.shape[0]
    e = lax.axis_index("state") % 2
    start, copies = starter(sems)
    for k in range(2 * count):
        target, top = (pf, k * known) if k < count else (lf.at[k - count], 0)
        start(own.at[k], target.at[pl.ds(pl.multiple_of(top + e * panel, panel), panel), :])
        for piece, at, row, size in spans(near, k, panel):
            to = pl.multiple_of(top + (1 - e) * panel + row, 8)
            start(near[piece].at[pl.ds(at, size), :], target.at[pl.ds(to, size), :])
    for j in range(order // known):
        mine, theirs = (joined.at[j - 1], joined_near.at[j - 1]) if j else (trans, trans_near)
        start(mine, af.at[rows(e ^ (2 * j), panel), :])
        start(theirs, af.at[rows(e ^ (2 * j) ^ 1, panel), :])
    pf[count * known :, :] = jnp.concatenate([means[...], jnp.zeros((16 - steps, order), F32)], axis=0)
    for copy in copies:
        copy.wait()
    product = dot3(pf[...], af[...], NT)
    info[:8] = pf[count * known : count * known + 8, :]
    info[8:] = product[count * known : count * known + 8]
    for half, x in enumerate(split(af[:, known:].T)):
        a_far[half] = x
    across = jnp.concatenate([pf[k * known : (k + 1) * known, known:].T for k in range(count)], axis=0)
    rest = dot3(across, af[:, :known], NT)
    for k in range(count):
        part = product[k * known : (k + 1) * known]
        for half, x in enumerate(split(lf[k])):
            l_known[k, half] = x
        partial = dot3(part[:, :known], lf[k], NN)
        g_known[k, :, :known] = partial[:, :known] + dot3(part[:, known:], lf[k, :, known:], NT)
        g_known[k, :, known:] = partial[:, known:]
        c_known[k] = part[:, known:]
        c_far[k] = rest[k * (order - known) : (k + 1) * (order - known)]


def steps_of(info, count):
    a = base(lax.axis_index("state"), count)
    return [info[pl.ds(a + shift, 1), :] for shift in (0, 1, 8, 9)]


def far_row(j, panel):
    return pl.ds(pl.multiple_of(j * panel, panel), panel)


def middle_kernel(a_far, l_known, c_known, c_far, g_known, *refs):
    far, (ga_ref, gb_ref, col_ref, h_ref, ff) = refs[:-5], refs[-5:]
    count, known, order = g_known.shape
    panel = known // 2
    e = lax.axis_index("state") % 2
    i, j = e, 1 - e
    for k in range(2 * count):
        if len(far) > 1:
            for off, piece in enumerate(far, 2):
                ff[k, rows((e ^ off) - 2, panel), :] = piece[k]
            continue
        beside, folded = far[0][k, :panel], far[0][k, panel:]
        ff[k, rows(i, panel), rows(i, panel)] = unfold(folded)
        ff[k, rows(j, panel), rows(j, panel)] = jnp.zeros((panel, panel), F32)
        ff[k, rows(i, panel), rows(j, panel)] = beside
        ff[k, rows(j, panel), rows(i, panel)] = beside.T

    for k, out in enumerate((ga_ref, gb_ref)):
        c = c_far[k] + dot3(ff[k], a_far, NN)
        known_rows = (l_known.at[k, 0], l_known.at[k, 1])
        known_far = [x[:, known:] for x in known_rows]
        l_far = split(ff[count + k])
        column = jnp.concatenate([c_known[k], c[:, known:]], axis=0)
        share = dot3(column, l_far, NN)
        low = dot3(c[:, :known], known_rows, NN)
        out[:known, :known] = g_known[k, :, :known]
        out[:known, known:] = g_known[k, :, known:] + share[:known]
        out[known:, :known] = low[:, :known] + dot3(c[:, known:], known_far, NT)
        out[known:, known:] = low[:, known:] + share[known:]
        if len(far) == 1:
            col_ref[k] = jnp.where(j == 0, column[:, :panel], column[:, panel:])
            halves = a_far[0, far_row(j, panel), :], a_far[1, far_row(j, panel), :]
            head, tail = [x[:, :known] for x in halves], [x[:, known:] for x in halves]
            h = dot3(head, known_rows, NN)
            h_ref[k, :, :known] = h[:, :known] + dot3(tail, known_far, NT)
            h_ref[k, :, known:] = h[:, known:] + dot3(tail, l_far, NN)


def steps_of(info, count):
    a = base(lax.axis_index("state"), count)
    return [info[pl.ds(a + shift, 1), :] for shift in (0, 1, 8, 9)]


def late_kernel(first, info, a_far, ga, gb, col, h, *refs):
    far, (ga_ref, gb_ref, mean_ref) = refs[:-3], refs[-3:]
    count, panel, order = h.shape
    j = 1 - lax.axis_index("state") % 2
    for k, (gain, out) in enumerate(((ga, ga_ref), (gb, gb_ref))):
        out[...] = gain[...]
        if far:
            at = far_row(2 + j, panel)
            p_last, l_last = unfold(far[0][k]), unfold(far[0][count + k])
            corner = [a_far[half, far_row(j, panel), at] for half in range(2)]
            out[at, :] += dot3(p_last, h[k], NN)
            out[:, at] += dot3(col[k], l_last, NN)
            out[at, at] += dot3(dot3(p_last, corner, NN), l_last, NN)
    mean_a, mean_b, pred_a, pred_b = steps_of(info, count)
    mean_ref[...] = mean_a + matvec(ga_ref[...], mean_b + matvec(gb_ref[...], first[...] - pred_b) - pred_a)


def two_kernel(x, info, ga, gb, out_ref):
    mean_a, mean_b, pred_a, pred_b = steps_of(info, 2)
    out_ref[...] = mean_a + matvec(ga[...], mean_b + matvec(gb[...], x[...] - pred_b) - pred_a)


def pair_kernel(info, ga, gb, map_ref):
    order = ga.shape[1]
    mean_a, mean_b, pred_a, pred_b = steps_of(info, 2)
    map_ref[order:, :] = jnp.concatenate(
        [mean_a + matvec(ga[...], mean_b - pred_a), mean_b, pred_b, jnp.zeros((5, order), F32)], axis=0
    )
    map_ref[:order, :] = dot3(ga[...], gb[...], NN)


def block_kernel(late, early, m_ref, vec_ref):
    order = late.shape[1]
    shift = early[order : order + 1, :] + matvec(
        early[:order, :], late[order : order + 1, :] - early[order + 2 : order + 3, :]
    )
    vec_ref[...] = jnp.concatenate([late[order + 2 : order + 3, :], shift, jnp.zeros((6, order), F32)], axis=0)
    m_ref[...] = dot3(early[:order, :], late[:order, :], NN)


def pair_hop_kernel(x, late, early, out_ref):
    order = x.shape[1]
    y = late[order : order + 1, :] + matvec(late[:order, :], x[...] - late[order + 2 : order + 3, :])
    out_ref[...] = early[order : order + 1, :] + matvec(early[:order, :], y - early[order + 2 : order + 3, :])


def hop_kernel(x, m, vec, out_ref):
    out_ref[...] = vec[1:2, :] + matvec(m[...], x[...] - vec[0:1, :])


def last_kernel(devices, *refs):
    blocks = len(refs) - 7 - devices
    incoming, (m, vec, late, g3, early, g1), outs, cut = refs[:blocks], refs[blocks : blocks + 6], refs[blocks + 6 : -1], refs[-1]
    order, panel = m.shape[1], outs[0].shape[1]
    b, s = lax.axis_index("tm"), lax.axis_index("state")
    x = incoming[0][...]
    for k, ref in enumerate(incoming[1:], 1):
        x = jnp.where(lax.axis_size("tm") - 1 - b == k, ref[...], x)
    gap = x - vec[0:1, :]
    x3 = late[order + 1 : order + 2, :] + matvec(g3[...], gap)
    x2 = late[order : order + 1, :] + matvec(late[:order, :], gap)
    x0 = vec[1:2, :] + matvec(m[...], gap)
    x1 = early[order + 1 : order + 2, :] + matvec(g1[...], x2 - early[order + 2 : order + 3, :])
    full = jnp.concatenate([x0, x1, x2, x3], axis=0)
    for i in range(devices):
        cut[i] = full[:, i * panel : (i + 1) * panel]
    for off, out in enumerate(outs):
        out[...] = cut[s ^ off]


def out_kernel(*refs):
    given, out_ref = [refs[0], *refs[-2:0:-1]], refs[-1]
    off = lax.axis_index("state") ^ 1
    x = given[0][...]
    for k, ref in enumerate(given[1:], 1):
        x = jnp.where(off == k, ref[...], x)
    out_ref[...] = x


def params(mebibytes):
    return pltpu.CompilerParams(vmem_limit_bytes=mebibytes * 2**20)


def local(filtered_covariance, pred_prec, transition, filt_means, terminal_mean):
    steps, panel, order = filtered_covariance.shape
    devices, blocks = lax.axis_size("state"), lax.axis_size("tm")
    count = steps // 2

    def swap(x, off, block_off=0):
        pairs = [(i, i ^ (block_off * devices + off)) for i in range(blocks * devices)]
        return lax.ppermute(x, ("tm", "state"), pairs)

    def shape(*dims):
        return jax.ShapeDtypeStruct(dims, F32)

    def call(kernel, name, mebibytes, outs, in_specs, scratch, args):
        return pl.pallas_call(
            kernel,
            out_shape=outs,
            in_specs=in_specs,
            out_specs=[VMEM] * len(outs),
            scratch_shapes=scratch,
            compiler_params=params(mebibytes),
            name=name,
        )(*args)

    cov, prec, trans, means, terminal = (
        pltpu.with_memory_space_constraint(x, pltpu.HBM)
        for x in (filtered_covariance, pred_prec, transition, filt_means, terminal_mean[None])
    )
    semaphores = pltpu.SemaphoreType.DMA((8 * devices,))
    square = shape(order, order)

    far = [shape(*far_shape(devices, count, panel, order, off)) for off in range(2, devices)]
    *far, trans_half, first = call(
        functools.partial(pack_kernel, devices),
        "pack",
        6,
        far + [shape(panel // 2, order), shape(1, order)],
        [HBM] * 4,
        [pltpu.VMEM((1, order), F32), pltpu.VMEM((2, steps, panel, panel), F32), semaphores],
        (cov, prec, trans, terminal),
    )
    across = [swap(trans_half, off) for off in range(2, devices, 2)]
    far = [swap(x, off) for off, x in enumerate(far, 2)]
    moved = [y for x in across for y in (x, swap(x, 0, 1))]
    near = call(
        near_kernel,
        "near",
        4,
        [shape(count * panel, order)] * 2,
        [HBM] * 2 + [ANY],
        [semaphores],
        (cov, prec, first),
    )
    near = [swap(x, 1) for x in near]
    own, own_trans, own_means = call(
        own_kernel,
        "own",
        4,
        [shape(2 * count, panel, order), shape(panel, order), shape(steps, order)],
        [HBM] * 4 + [ANY],
        [semaphores],
        (cov, prec, trans, means, across[0]),
    )
    (joined,) = call(
        join_kernel,
        "join",
        4,
        [shape(devices // 2 - 1, panel, order)],
        [ANY] * (1 + len(moved)),
        [semaphores],
        (own_trans, *moved),
    )
    joined_near = swap(joined, 1)
    trans_near = swap(transition, 1)

    known = 2 * panel
    parts = call(
        early_kernel,
        "early",
        24,
        [
            shape(16, order),
            jax.ShapeDtypeStruct((2, order - known, order), BF16),
            jax.ShapeDtypeStruct((count, 2, known, order), BF16),
            shape(count, known, order - known),
            shape(count, order - known, order),
            shape(count, known, order),
        ],
        [ANY, VMEM] + [ANY] * 2 + [ANY] * 4,
        [
            pltpu.VMEM((count * known + 16, order), F32),
            pltpu.VMEM((order, order), F32),
            pltpu.VMEM((count, known, order), F32),
            semaphores,
        ],
        (own, own_means, own_trans, trans_near, joined, joined_near, *near),
    )
    info, a_far = parts[:2]
    last = far[1:] if trimmed(devices, panel) else []
    ga, gb, col, h = call(
        middle_kernel,
        "middle",
        24,
        [square, square, shape(count, order, panel), shape(count, panel, order)],
        [VMEM] * (5 + len(far) - len(last)),
        [pltpu.VMEM((2 * count, order - known, order - known), F32)],
        (*parts[1:], *far[: len(far) - len(last)]),
    )
    ga, gb, mean = call(
        late_kernel,
        "late",
        12,
        [square, square, shape(1, order)],
        [VMEM] * (7 + len(last)),
        [],
        (first, info, a_far, ga, gb, col, h, *last),
    )
    mean = swap(mean, 1)
    (early_map,) = call(pair_kernel, "pair", 12, [shape(order + 8, order)], [VMEM] * 3, [], (info, ga, gb))
    late_map = swap(lax.optimization_barrier((early_map, mean))[0], 1)
    (mean,) = call(two_kernel, "two", 6, [shape(1, order)], [VMEM] * 4, [], (mean, info, ga, gb))

    incoming = [first, swap(mean, 0, 1)]
    (x,) = call(pair_hop_kernel, "pair_hop", 4, [shape(1, order)], [VMEM] * 3, [], (incoming[-1], late_map, early_map))
    m, vec = call(block_kernel, "block", 12, [square, shape(8, order)], [VMEM] * 2, [], (late_map, early_map))
    for block in range(blocks - 2, 0, -1):
        if block < blocks - 2:
            (x,) = call(hop_kernel, "hop", 4, [shape(1, order)], [VMEM] * 3, [], (incoming[-1], m, vec))
        target = {i: i ^ 1 for i in range(blocks * devices)}
        for at, to in ((block, block - 1), (block - 1, block)):
            target[at * devices + 1] = to * devices + 1
            target.update({at * devices + i: at * devices + j for i, j in ((0, 2), (2, 3), (3, 0))})
        x = lax.ppermute(x, ("tm", "state"), list(target.items()))
        incoming.append(x)
    g3 = swap(lax.optimization_barrier((gb, incoming[3]))[0], 1)

    given = list(call(
        functools.partial(last_kernel, devices),
        "last",
        8,
        [shape(steps, panel)] * devices,
        [VMEM] * (blocks + 6),
        [pltpu.VMEM((devices, steps, panel), F32)],
        (*incoming, m, vec, late_map, g3, early_map, gb),
    ))
    for off in range(devices - 1, 0, -1):
        given[off] = swap(given[off], off)
    given = [given[0], *given[:0:-1]]
    (out,) = call(out_kernel, "out", 4, [shape(steps, panel)], [VMEM] * devices, [], given)
    return out


def solution(mesh):
    return jax.shard_map(
        local,
        mesh=mesh,
        in_specs=(
            P("tm", "state", None),
            P("tm", "state", None),
            P("state", None),
            P("tm", None),
            P(),
        ),
        out_specs=P("tm", "state"),
        check_vma=False,
    )
```

```python
import functools

import jax
import jax.numpy as jnp
from jax import lax
from jax.experimental import pallas as pl
from jax.experimental.pallas import tpu as pltpu
from jax.sharding import PartitionSpec as P

F32, BF16 = jnp.float32, jnp.bfloat16
NN = (((1,), (0,)), ((), ()))
NT = (((1,), (1,)), ((), ()))
ANY = pl.BlockSpec(memory_space=pl.ANY)
HBM = pl.BlockSpec(memory_space=pltpu.HBM)
VMEM = pl.BlockSpec(memory_space=pltpu.VMEM)


def split(x):
    high = x.astype(BF16)
    return high, (x - high.astype(F32)).astype(BF16)


def dot3(a, b, dims):
    (ah, al), (bh, bl) = (split(x) if getattr(x, "dtype", None) == F32 else (x[0][...], x[1][...]) for x in (a, b))
    dot = functools.partial(lax.dot_general, dimension_numbers=dims, preferred_element_type=F32)
    return dot(ah, bh) + (dot(ah, bl) + dot(al, bh))


def matvec(matrix, row):
    order = matrix.shape[1]
    total = matrix[:, :128] * row[:, :128]
    for j in range(128, order, 128):
        total += matrix[:, j : j + 128] * row[:, j : j + 128]
    return jnp.sum(total.T, axis=0, keepdims=True)


def rows(i, panel):
    return pl.ds(pl.multiple_of(i * panel, panel), panel)


def starter(sems):
    copies = []

    def start(source, target):
        copy = pltpu.make_async_copy(source, target, sems.at[len(copies)])
        copy.start()
        copies.append(copy)

    return start, copies


def trimmed(devices, panel):
    return devices == 4 and panel == 128


def far_shape(devices, count, panel, order, off):
    if trimmed(devices, panel):
        return (2 * count, panel * 9 // 16 + (panel if off == 2 else 0), panel)
    return (2 * count, panel, order - 2 * panel)


def lanes(rows):
    return lax.broadcasted_iota(jnp.int32, (rows, 128), 1)


def fold(block):
    lower = ((112, 16), (96, 32), (80, 48))
    filled = [
        jnp.where(lanes(16) < width, pltpu.roll(block[row : row + 16], width, 1), block[width : width + 16])
        for row, width in lower
    ]
    rest = jnp.where(lanes(8) < 64, pltpu.roll(block[64:72], 64, 1), block[72:80])
    return jnp.concatenate([block[:16], *filled, rest], axis=0)


def unfold(folded):
    rest = folded[64:]
    moved = [pltpu.roll(folded[width : width + 16], 128 - width, 1) for width in (48, 32, 16)]
    upper = jnp.concatenate([folded[:64], pltpu.roll(rest, 64, 1), rest, *moved], axis=0)
    row = lax.broadcasted_iota(jnp.int32, (128, 128), 0)
    return jnp.where(row // 16 <= lanes(128) // 16, upper, upper.T)


def base(device, count):
    return (1 - device % 2) * count


def pack_kernel(devices, cov, prec, trans, terminal, *refs):
    far, (trans_half, first, vector, diagonal, sems) = refs[: devices - 2], refs[devices - 2 :]
    count, panel, order = cov.shape[0] // 2, *cov.shape[1:]
    b, s = lax.axis_index("tm"), lax.axis_index("state")
    start, copies = starter(sems)
    start(terminal, vector)
    start(trans.at[pl.ds(pl.multiple_of((b % 2) * (panel // 2), panel // 2), panel // 2), :], trans_half)
    trim = trimmed(devices, panel)
    if trim:
        for k, matrix in enumerate((cov, prec)):
            start(matrix.at[:, :, rows(s, panel)], diagonal.at[k])
    for off, piece in enumerate(far, 2):
        theirs = pl.ds(base(s ^ off, count), count)
        for k, matrix in enumerate((cov, prec)):
            target = piece.at[pl.ds(k * count, count)]
            if not trim:
                start(matrix.at[theirs, :, 2 * panel :], target)
            elif off == 2:
                start(matrix.at[theirs, :, rows(s ^ 1, panel)], target.at[:, :panel])
    copies[0].wait()
    first[...] = jnp.where(b == lax.axis_size("tm") - 1, vector[...], 0.0)
    for copy in copies[1:]:
        copy.wait()
    if trim:
        for off, piece in enumerate(far, 2):
            for k in range(2 * count):
                block = diagonal[k // count, base(s ^ off, count) + k % count]
                piece[k, piece.shape[1] - panel * 9 // 16 :, :] = fold(block)


def near_kernel(cov, prec, trans, after, near_cov, near_prec, near_trans, sems):
    count = cov.shape[0] // 2
    theirs = pl.ds((1 - lax.axis_index("state") % 2) * count, count)
    start, copies = starter(sems)
    start(cov.at[theirs], near_cov)
    start(prec.at[theirs], near_prec)
    start(trans, near_trans)
    for copy in copies:
        copy.wait()


def near_kernel(cov, prec, after, *refs):
    pieces, sems = refs[:-1], refs[-1]
    count, panel = cov.shape[0] // 2, cov.shape[1]
    first = base(lax.axis_index("state") ^ 1, count)
    start, copies = starter(sems)
    for k in range(2 * count):
        matrix = (cov, prec)[k // count]
        for piece, at, source, size in spans(pieces, k, panel):
            start(matrix.at[first + k % count, pl.ds(source, size), :], pieces[piece].at[pl.ds(at, size), :])
    for copy in copies:
        copy.wait()


def spans(pieces, k, panel):
    found, at = [], 0
    for i, piece in enumerate(pieces):
        low, high = max(at, k * panel), min(at + piece.shape[0], (k + 1) * panel)
        if low < high:
            found.append((i, low - at, low - k * panel, high - low))
        at += piece.shape[0]
    return found


def own_kernel(cov, prec, trans, means, after, own, own_trans, own_means, sems):
    count = cov.shape[0] // 2
    mine = pl.ds(base(lax.axis_index("state"), count), count)
    start, copies = starter(sems)
    start(cov.at[mine], own.at[pl.ds(0, count)])
    start(prec.at[mine], own.at[pl.ds(count, count)])
    start(trans, own_trans)
    start(means, own_means)
    for copy in copies:
        copy.wait()


def join_kernel(after, *refs):
    moved, (joined, sems) = refs[:-2], refs[-2:]
    half = moved[0].shape[0]
    b = lax.axis_index("tm")
    start, copies = starter(sems)
    for k, piece in enumerate(moved):
        at = (b % 2 if k % 2 == 0 else 1 - b % 2) * half
        start(piece, joined.at[k // 2, pl.ds(pl.multiple_of(at, half), half), :])
    for copy in copies:
        copy.wait()


def early_kernel(own, means, trans, trans_near, joined, joined_near, *refs):
    near, (info, a_far, l_known, c_known, c_far, g_known, pf, af, lf, sems) = refs[:-10], refs[-10:]
    panel, order = own.shape[1:]
    count, known = own.shape[0] // 2, 2 * panel
    steps = means.shape[0]
    e = lax.axis_index("state") % 2
    start, copies = starter(sems)
    for k in range(2 * count):
        target, top = (pf, k * known) if k < count else (lf.at[k - count], 0)
        start(own.at[k], target.at[pl.ds(pl.multiple_of(top + e * panel, panel), panel), :])
        for piece, at, row, size in spans(near, k, panel):
            to = pl.multiple_of(top + (1 - e) * panel + row, 8)
            start(near[piece].at[pl.ds(at, size), :], target.at[pl.ds(to, size), :])
    for j in range(order // known):
        mine, theirs = (joined.at[j - 1], joined_near.at[j - 1]) if j else (trans, trans_near)
        start(mine, af.at[rows(e ^ (2 * j), panel), :])
        start(theirs, af.at[rows(e ^ (2 * j) ^ 1, panel), :])
    pf[count * known :, :] = jnp.concatenate([means[...], jnp.zeros((16 - steps, order), F32)], axis=0)
    for copy in copies:
        copy.wait()
    product = dot3(pf[...], af[...], NT)
    info[:8] = pf[count * known : count * known + 8, :]
    info[8:] = product[count * known : count * known + 8]
    for half, x in enumerate(split(af[:, known:].T)):
        a_far[half] = x
    across = jnp.concatenate([pf[k * known : (k + 1) * known, known:].T for k in range(count)], axis=0)
    rest = dot3(across, af[:, :known], NT)
    for k in range(count):
        part = product[k * known : (k + 1) * known]
        for half, x in enumerate(split(lf[k])):
            l_known[k, half] = x
        partial = dot3(part[:, :known], lf[k], NN)
        g_known[k, :, :known] = partial[:, :known] + dot3(part[:, known:], lf[k, :, known:], NT)
        g_known[k, :, known:] = partial[:, known:]
        c_known[k] = part[:, known:]
        c_far[k] = rest[k * (order - known) : (k + 1) * (order - known)]


def steps_of(info, count):
    a = base(lax.axis_index("state"), count)
    return [info[pl.ds(a + shift, 1), :] for shift in (0, 1, 8, 9)]


def far_row(j, panel):
    return pl.ds(pl.multiple_of(j * panel, panel), panel)


def middle_kernel(a_far, l_known, c_known, c_far, g_known, *refs):
    far, (ga_ref, gb_ref, col_ref, h_ref, ff) = refs[:-5], refs[-5:]
    count, known, order = g_known.shape
    panel = known // 2
    e = lax.axis_index("state") % 2
    i, j = e, 1 - e
    for k in range(2 * count):
        if len(far) > 1:
            for off, piece in enumerate(far, 2):
                ff[k, rows((e ^ off) - 2, panel), :] = piece[k]
            continue
        beside, folded = far[0][k, :panel], far[0][k, panel:]
        ff[k, rows(i, panel), rows(i, panel)] = unfold(folded)
        ff[k, rows(j, panel), rows(j, panel)] = jnp.zeros((panel, panel), F32)
        ff[k, rows(i, panel), rows(j, panel)] = beside
        ff[k, rows(j, panel), rows(i, panel)] = beside.T

    for k, out in enumerate((ga_ref, gb_ref)):
        c = c_far[k] + dot3(ff[k], a_far, NN)
        known_rows = (l_known.at[k, 0], l_known.at[k, 1])
        known_far = [x[:, known:] for x in known_rows]
        l_far = split(ff[count + k])
        column = jnp.concatenate([c_known[k], c[:, known:]], axis=0)
        share = dot3(column, l_far, NN)
        low = dot3(c[:, :known], known_rows, NN)
        out[:known, :known] = g_known[k, :, :known]
        out[:known, known:] = g_known[k, :, known:] + share[:known]
        out[known:, :known] = low[:, :known] + dot3(c[:, known:], known_far, NT)
        out[known:, known:] = low[:, known:] + share[known:]
        if len(far) == 1:
            col_ref[k] = jnp.where(j == 0, column[:, :panel], column[:, panel:])
            halves = a_far[0, far_row(j, panel), :], a_far[1, far_row(j, panel), :]
            head, tail = [x[:, :known] for x in halves], [x[:, known:] for x in halves]
            h = dot3(head, known_rows, NN)
            h_ref[k, :, :known] = h[:, :known] + dot3(tail, known_far, NT)
            h_ref[k, :, known:] = h[:, known:] + dot3(tail, l_far, NN)


def steps_of(info, count):
    a = base(lax.axis_index("state"), count)
    return [info[pl.ds(a + shift, 1), :] for shift in (0, 1, 8, 9)]


def late_kernel(first, info, a_far, ga, gb, col, h, *refs):
    far, (ga_ref, gb_ref, mean_ref) = refs[:-3], refs[-3:]
    count, panel, order = h.shape
    j = 1 - lax.axis_index("state") % 2
    for k, (gain, out) in enumerate(((ga, ga_ref), (gb, gb_ref))):
        if far:
            at = far_row(2 + j, panel)
            p_last, l_last = unfold(far[0][k]), unfold(far[0][count + k])
            corner = [a_far[half, far_row(j, panel), at] for half in range(2)]
            out[at, :] = gain[at, :] + dot3(p_last, h[k], NN)
            out[:, at] += dot3(col[k], l_last, NN)
            out[at, at] += dot3(dot3(p_last, corner, NN), l_last, NN)
    mean_a, mean_b, pred_a, pred_b = steps_of(info, count)
    mean_ref[...] = mean_a + matvec(ga_ref[...], mean_b + matvec(gb_ref[...], first[...] - pred_b) - pred_a)


def two_kernel(x, info, ga, gb, out_ref):
    mean_a, mean_b, pred_a, pred_b = steps_of(info, 2)
    out_ref[...] = mean_a + matvec(ga[...], mean_b + matvec(gb[...], x[...] - pred_b) - pred_a)


def pair_kernel(info, ga, gb, map_ref):
    order = ga.shape[1]
    mean_a, mean_b, pred_a, pred_b = steps_of(info, 2)
    map_ref[order:, :] = jnp.concatenate(
        [mean_a + matvec(ga[...], mean_b - pred_a), mean_b, pred_b, jnp.zeros((5, order), F32)], axis=0
    )
    map_ref[:order, :] = dot3(ga[...], gb[...], NN)


def block_kernel(late, early, m_ref, vec_ref):
    order = late.shape[1]
    shift = early[order : order + 1, :] + matvec(
        early[:order, :], late[order : order + 1, :] - early[order + 2 : order + 3, :]
    )
    vec_ref[...] = jnp.concatenate([late[order + 2 : order + 3, :], shift, jnp.zeros((6, order), F32)], axis=0)
    m_ref[...] = dot3(early[:order, :], late[:order, :], NN)


def pair_hop_kernel(x, late, early, out_ref):
    order = x.shape[1]
    y = late[order : order + 1, :] + matvec(late[:order, :], x[...] - late[order + 2 : order + 3, :])
    out_ref[...] = early[order : order + 1, :] + matvec(early[:order, :], y - early[order + 2 : order + 3, :])


def hop_kernel(x, m, vec, out_ref):
    out_ref[...] = vec[1:2, :] + matvec(m[...], x[...] - vec[0:1, :])


def last_kernel(devices, *refs):
    blocks = len(refs) - 7 - devices
    incoming, (m, vec, late, g3, early, g1), outs, cut = refs[:blocks], refs[blocks : blocks + 6], refs[blocks + 6 : -1], refs[-1]
    order, panel = m.shape[1], outs[0].shape[1]
    b, s = lax.axis_index("tm"), lax.axis_index("state")
    x = incoming[0][...]
    for k, ref in enumerate(incoming[1:], 1):
        x = jnp.where(lax.axis_size("tm") - 1 - b == k, ref[...], x)
    gap = x - vec[0:1, :]
    x3 = late[order + 1 : order + 2, :] + matvec(g3[...], gap)
    x2 = late[order : order + 1, :] + matvec(late[:order, :], gap)
    x0 = vec[1:2, :] + matvec(m[...], gap)
    x1 = early[order + 1 : order + 2, :] + matvec(g1[...], x2 - early[order + 2 : order + 3, :])
    full = jnp.concatenate([x0, x1, x2, x3], axis=0)
    for i in range(devices):
        cut[i] = full[:, i * panel : (i + 1) * panel]
    for off, out in enumerate(outs):
        out[...] = cut[s ^ off]


def out_kernel(*refs):
    given, out_ref = [refs[0], *refs[-2:0:-1]], refs[-1]
    off = lax.axis_index("state") ^ 1
    x = given[0][...]
    for k, ref in enumerate(given[1:], 1):
        x = jnp.where(off == k, ref[...], x)
    out_ref[...] = x


def params(mebibytes):
    return pltpu.CompilerParams(vmem_limit_bytes=mebibytes * 2**20)


def local(filtered_covariance, pred_prec, transition, filt_means, terminal_mean):
    steps, panel, order = filtered_covariance.shape
    devices, blocks = lax.axis_size("state"), lax.axis_size("tm")
    count = steps // 2

    def swap(x, off, block_off=0):
        pairs = [(i, i ^ (block_off * devices + off)) for i in range(blocks * devices)]
        return lax.ppermute(x, ("tm", "state"), pairs)

    def shape(*dims):
        return jax.ShapeDtypeStruct(dims, F32)

    def call(kernel, name, mebibytes, outs, in_specs, scratch, args, aliases={}):
        return pl.pallas_call(
            kernel,
            out_shape=outs,
            in_specs=in_specs,
            out_specs=[VMEM] * len(outs),
            scratch_shapes=scratch,
            input_output_aliases=aliases,
            compiler_params=params(mebibytes),
            name=name,
        )(*args)

    cov, prec, trans, means, terminal = (
        pltpu.with_memory_space_constraint(x, pltpu.HBM)
        for x in (filtered_covariance, pred_prec, transition, filt_means, terminal_mean[None])
    )
    semaphores = pltpu.SemaphoreType.DMA((8 * devices,))
    square = shape(order, order)

    far = [shape(*far_shape(devices, count, panel, order, off)) for off in range(2, devices)]
    *far, trans_half, first = call(
        functools.partial(pack_kernel, devices),
        "pack",
        6,
        far + [shape(panel // 2, order), shape(1, order)],
        [HBM] * 4,
        [pltpu.VMEM((1, order), F32), pltpu.VMEM((2, steps, panel, panel), F32), semaphores],
        (cov, prec, trans, terminal),
    )
    across = [swap(trans_half, off) for off in range(2, devices, 2)]
    far = [swap(x, off) for off, x in enumerate(far, 2)]
    moved = [y for x in across for y in (x, swap(x, 0, 1))]
    near = call(
        near_kernel,
        "near",
        4,
        [shape(count * panel, order)] * 2,
        [HBM] * 2 + [ANY],
        [semaphores],
        (cov, prec, first),
    )
    near = [swap(x, 1) for x in near]
    own, own_trans, own_means = call(
        own_kernel,
        "own",
        4,
        [shape(2 * count, panel, order), shape(panel, order), shape(steps, order)],
        [HBM] * 4 + [ANY],
        [semaphores],
        (cov, prec, trans, means, across[0]),
    )
    (joined,) = call(
        join_kernel,
        "join",
        4,
        [shape(devices // 2 - 1, panel, order)],
        [ANY] * (1 + len(moved)),
        [semaphores],
        (own_trans, *moved),
    )
    joined_near = swap(joined, 1)
    trans_near = swap(transition, 1)

    known = 2 * panel
    parts = call(
        early_kernel,
        "early",
        24,
        [
            shape(16, order),
            jax.ShapeDtypeStruct((2, order - known, order), BF16),
            jax.ShapeDtypeStruct((count, 2, known, order), BF16),
            shape(count, known, order - known),
            shape(count, order - known, order),
            shape(count, known, order),
        ],
        [ANY, VMEM] + [ANY] * 2 + [ANY] * 4,
        [
            pltpu.VMEM((count * known + 16, order), F32),
            pltpu.VMEM((order, order), F32),
            pltpu.VMEM((count, known, order), F32),
            semaphores,
        ],
        (own, own_means, own_trans, trans_near, joined, joined_near, *near),
    )
    info, a_far = parts[:2]
    last = far[1:] if trimmed(devices, panel) else []
    ga, gb, col, h = call(
        middle_kernel,
        "middle",
        24,
        [square, square, shape(count, order, panel), shape(count, panel, order)],
        [VMEM] * (5 + len(far) - len(last)),
        [pltpu.VMEM((2 * count, order - known, order - known), F32)],
        (*parts[1:], *far[: len(far) - len(last)]),
    )
    ga, gb, mean = call(
        late_kernel,
        "late",
        12,
        [square, square, shape(1, order)],
        [VMEM] * (7 + len(last)),
        [],
        (first, info, a_far, ga, gb, col, h, *last),
        {3: 0, 4: 1},
    )
    mean = swap(mean, 1)
    (early_map,) = call(pair_kernel, "pair", 12, [shape(order + 8, order)], [VMEM] * 3, [], (info, ga, gb))
    late_map = swap(lax.optimization_barrier((early_map, mean))[0], 1)
    (mean,) = call(two_kernel, "two", 6, [shape(1, order)], [VMEM] * 4, [], (mean, info, ga, gb))

    incoming = [first, swap(mean, 0, 1)]
    (x,) = call(pair_hop_kernel, "pair_hop", 4, [shape(1, order)], [VMEM] * 3, [], (incoming[-1], late_map, early_map))
    m, vec = call(block_kernel, "block", 12, [square, shape(8, order)], [VMEM] * 2, [], (late_map, early_map))
    for block in range(blocks - 2, 0, -1):
        if block < blocks - 2:
            (x,) = call(hop_kernel, "hop", 4, [shape(1, order)], [VMEM] * 3, [], (incoming[-1], m, vec))
        target = {i: i ^ 1 for i in range(blocks * devices)}
        for at, to in ((block, block - 1), (block - 1, block)):
            target[at * devices + 1] = to * devices + 1
            target.update({at * devices + i: at * devices + j for i, j in ((0, 2), (2, 3), (3, 0))})
        x = lax.ppermute(x, ("tm", "state"), list(target.items()))
        incoming.append(x)
    g3 = swap(lax.optimization_barrier((gb, incoming[3]))[0], 1)

    given = list(call(
        functools.partial(last_kernel, devices),
        "last",
        8,
        [shape(steps, panel)] * devices,
        [VMEM] * (blocks + 6),
        [pltpu.VMEM((devices, steps, panel), F32)],
        (*incoming, m, vec, late_map, g3, early_map, gb),
    ))
    for off in range(devices - 1, 0, -1):
        given[off] = swap(given[off], off)
    given = [given[0], *given[:0:-1]]
    (out,) = call(out_kernel, "out", 4, [shape(steps, panel)], [VMEM] * devices, [], given)
    return out


def solution(mesh):
    return jax.shard_map(
        local,
        mesh=mesh,
        in_specs=(
            P("tm", "state", None),
            P("tm", "state", None),
            P("state", None),
            P("tm", None),
            P(),
        ),
        out_specs=P("tm", "state"),
        check_vma=False,
    )
```

```python
import functools

import jax
import jax.numpy as jnp
from jax import lax
from jax.experimental import pallas as pl
from jax.experimental.pallas import tpu as pltpu
from jax.sharding import PartitionSpec as P

F32, BF16 = jnp.float32, jnp.bfloat16
NN = (((1,), (0,)), ((), ()))
NT = (((1,), (1,)), ((), ()))
ANY = pl.BlockSpec(memory_space=pl.ANY)
HBM = pl.BlockSpec(memory_space=pltpu.HBM)
VMEM = pl.BlockSpec(memory_space=pltpu.VMEM)


def split(x):
    high = x.astype(BF16)
    return high, (x - high.astype(F32)).astype(BF16)


def dot3(a, b, dims):
    (ah, al), (bh, bl) = (split(x) if getattr(x, "dtype", None) == F32 else (x[0][...], x[1][...]) for x in (a, b))
    dot = functools.partial(lax.dot_general, dimension_numbers=dims, preferred_element_type=F32)
    return dot(ah, bh) + (dot(ah, bl) + dot(al, bh))


def matvec(matrix, row):
    order = matrix.shape[1]
    total = matrix[:, :128] * row[:, :128]
    for j in range(128, order, 128):
        total += matrix[:, j : j + 128] * row[:, j : j + 128]
    return jnp.sum(total.T, axis=0, keepdims=True)


def rows(i, panel):
    return pl.ds(pl.multiple_of(i * panel, panel), panel)


def starter(sems):
    copies = []

    def start(source, target):
        copy = pltpu.make_async_copy(source, target, sems.at[len(copies)])
        copy.start()
        copies.append(copy)

    return start, copies


def trimmed(devices, panel):
    return devices == 4 and panel == 128


def far_shape(devices, count, panel, order, off):
    if trimmed(devices, panel):
        return (2 * count, panel * 9 // 16 + (panel if off == 2 else 0), panel)
    return (2 * count, panel, order - 2 * panel)


def lanes(rows):
    return lax.broadcasted_iota(jnp.int32, (rows, 128), 1)


def fold(block):
    lower = ((112, 16), (96, 32), (80, 48))
    filled = [
        jnp.where(lanes(16) < width, pltpu.roll(block[row : row + 16], width, 1), block[width : width + 16])
        for row, width in lower
    ]
    rest = jnp.where(lanes(8) < 64, pltpu.roll(block[64:72], 64, 1), block[72:80])
    return jnp.concatenate([block[:16], *filled, rest], axis=0)


def unfold(folded):
    rest = folded[64:]
    moved = [pltpu.roll(folded[width : width + 16], 128 - width, 1) for width in (48, 32, 16)]
    upper = jnp.concatenate([folded[:64], pltpu.roll(rest, 64, 1), rest, *moved], axis=0)
    row = lax.broadcasted_iota(jnp.int32, (128, 128), 0)
    return jnp.where(row // 16 <= lanes(128) // 16, upper, upper.T)


def base(device, count):
    return (1 - device % 2) * count


def pack_kernel(devices, cov, prec, trans, terminal, *refs):
    far, (trans_half, first, vector, diagonal, sems) = refs[: devices - 2], refs[devices - 2 :]
    count, panel, order = cov.shape[0] // 2, *cov.shape[1:]
    b, s = lax.axis_index("tm"), lax.axis_index("state")
    start, copies = starter(sems)
    start(terminal, vector)
    start(trans.at[pl.ds(pl.multiple_of((b % 2) * (panel // 2), panel // 2), panel // 2), :], trans_half)
    trim = trimmed(devices, panel)
    if trim:
        for k, matrix in enumerate((cov, prec)):
            start(matrix.at[:, :, rows(s, panel)], diagonal.at[k])
    for off, piece in enumerate(far, 2):
        theirs = pl.ds(base(s ^ off, count), count)
        for k, matrix in enumerate((cov, prec)):
            target = piece.at[pl.ds(k * count, count)]
            if not trim:
                start(matrix.at[theirs, :, 2 * panel :], target)
            elif off == 2:
                start(matrix.at[theirs, :, rows(s ^ 1, panel)], target.at[:, :panel])
    copies[0].wait()
    first[...] = jnp.where(b == lax.axis_size("tm") - 1, vector[...], 0.0)
    for copy in copies[1:]:
        copy.wait()
    if trim:
        for off, piece in enumerate(far, 2):
            for k in range(2 * count):
                block = diagonal[k // count, base(s ^ off, count) + k % count]
                piece[k, piece.shape[1] - panel * 9 // 16 :, :] = fold(block)


def near_kernel(cov, prec, trans, after, near_cov, near_prec, near_trans, sems):
    count = cov.shape[0] // 2
    theirs = pl.ds((1 - lax.axis_index("state") % 2) * count, count)
    start, copies = starter(sems)
    start(cov.at[theirs], near_cov)
    start(prec.at[theirs], near_prec)
    start(trans, near_trans)
    for copy in copies:
        copy.wait()


def near_kernel(cov, prec, after, *refs):
    pieces, sems = refs[:-1], refs[-1]
    count, panel = cov.shape[0] // 2, cov.shape[1]
    first = base(lax.axis_index("state") ^ 1, count)
    start, copies = starter(sems)
    for k in range(2 * count):
        matrix = (cov, prec)[k // count]
        for piece, at, source, size in spans(pieces, k, panel):
            start(matrix.at[first + k % count, pl.ds(source, size), :], pieces[piece].at[pl.ds(at, size), :])
    for copy in copies:
        copy.wait()


def spans(pieces, k, panel):
    found, at = [], 0
    for i, piece in enumerate(pieces):
        low, high = max(at, k * panel), min(at + piece.shape[0], (k + 1) * panel)
        if low < high:
            found.append((i, low - at, low - k * panel, high - low))
        at += piece.shape[0]
    return found


def own_kernel(cov, prec, trans, means, after, own, own_trans, own_means, sems):
    count = cov.shape[0] // 2
    mine = pl.ds(base(lax.axis_index("state"), count), count)
    start, copies = starter(sems)
    start(cov.at[mine], own.at[pl.ds(0, count)])
    start(prec.at[mine], own.at[pl.ds(count, count)])
    start(trans, own_trans)
    start(means, own_means)
    for copy in copies:
        copy.wait()


def join_kernel(after, *refs):
    moved, (joined, sems) = refs[:-2], refs[-2:]
    half = moved[0].shape[0]
    b = lax.axis_index("tm")
    start, copies = starter(sems)
    for k, piece in enumerate(moved):
        at = (b % 2 if k % 2 == 0 else 1 - b % 2) * half
        start(piece, joined.at[k // 2, pl.ds(pl.multiple_of(at, half), half), :])
    for copy in copies:
        copy.wait()


def early_kernel(own, means, trans, trans_near, joined, joined_near, *refs):
    near, (info, a_far, l_known, c_known, c_far, g_known, pf, af, lf, sems) = refs[:-10], refs[-10:]
    panel, order = own.shape[1:]
    count, known = own.shape[0] // 2, 2 * panel
    steps = means.shape[0]
    e = lax.axis_index("state") % 2
    start, copies = starter(sems)
    for k in range(2 * count):
        target, top = (pf, k * known) if k < count else (lf.at[k - count], 0)
        start(own.at[k], target.at[pl.ds(pl.multiple_of(top + e * panel, panel), panel), :])
        for piece, at, row, size in spans(near, k, panel):
            to = pl.multiple_of(top + (1 - e) * panel + row, 8)
            start(near[piece].at[pl.ds(at, size), :], target.at[pl.ds(to, size), :])
    start(trans, af.at[rows(e, panel), :])
    start(trans_near, af.at[rows(1 - e, panel), :])
    size = panel // 2
    for j in range(1, order // known):
        for half in range(2):
            mine = e ^ (2 * j) ^ ((lax.axis_index("tm") + half) % 2)
            for i, piece in ((mine, joined), (mine ^ 1, joined_near)):
                at = pl.multiple_of(i * panel + half * size, size)
                start(piece.at[j - 1, pl.ds(half * size, size), :], af.at[pl.ds(at, size), :])
    pf[count * known :, :] = jnp.concatenate([means[...], jnp.zeros((16 - steps, order), F32)], axis=0)
    for copy in copies:
        copy.wait()
    product = dot3(pf[...], af[...], NT)
    info[:8] = pf[count * known : count * known + 8, :]
    info[8:] = product[count * known : count * known + 8]
    for half, x in enumerate(split(af[:, known:].T)):
        a_far[half] = x
    across = jnp.concatenate([pf[k * known : (k + 1) * known, known:].T for k in range(count)], axis=0)
    rest = dot3(across, af[:, :known], NT)
    for k in range(count):
        part = product[k * known : (k + 1) * known]
        for half, x in enumerate(split(lf[k])):
            l_known[k, half] = x
        partial = dot3(part[:, :known], lf[k], NN)
        g_known[k, :, :known] = partial[:, :known] + dot3(part[:, known:], lf[k, :, known:], NT)
        g_known[k, :, known:] = partial[:, known:]
        c_known[k] = part[:, known:]
        c_far[k] = rest[k * (order - known) : (k + 1) * (order - known)]


def steps_of(info, count):
    a = base(lax.axis_index("state"), count)
    return [info[pl.ds(a + shift, 1), :] for shift in (0, 1, 8, 9)]


def far_row(j, panel):
    return pl.ds(pl.multiple_of(j * panel, panel), panel)


def middle_kernel(a_far, l_known, c_known, c_far, g_known, *refs):
    far, (ga_ref, gb_ref, col_ref, h_ref, ff) = refs[:-5], refs[-5:]
    count, known, order = g_known.shape
    panel = known // 2
    e = lax.axis_index("state") % 2
    i, j = e, 1 - e
    for k in range(2 * count):
        if len(far) > 1:
            for off, piece in enumerate(far, 2):
                ff[k, rows((e ^ off) - 2, panel), :] = piece[k]
            continue
        beside, folded = far[0][k, :panel], far[0][k, panel:]
        ff[k, rows(i, panel), rows(i, panel)] = unfold(folded)
        ff[k, rows(j, panel), rows(j, panel)] = jnp.zeros((panel, panel), F32)
        ff[k, rows(i, panel), rows(j, panel)] = beside
        ff[k, rows(j, panel), rows(i, panel)] = beside.T

    for k, out in enumerate((ga_ref, gb_ref)):
        c = c_far[k] + dot3(ff[k], a_far, NN)
        known_rows = (l_known.at[k, 0], l_known.at[k, 1])
        known_far = [x[:, known:] for x in known_rows]
        l_far = split(ff[count + k])
        column = jnp.concatenate([c_known[k], c[:, known:]], axis=0)
        share = dot3(column, l_far, NN)
        low = dot3(c[:, :known], known_rows, NN)
        out[:known, :known] = g_known[k, :, :known]
        out[:known, known:] = g_known[k, :, known:] + share[:known]
        out[known:, :known] = low[:, :known] + dot3(c[:, known:], known_far, NT)
        out[known:, known:] = low[:, known:] + share[known:]
        if len(far) == 1:
            col_ref[k] = jnp.where(j == 0, column[:, :panel], column[:, panel:])
            halves = a_far[0, far_row(j, panel), :], a_far[1, far_row(j, panel), :]
            head, tail = [x[:, :known] for x in halves], [x[:, known:] for x in halves]
            h = dot3(head, known_rows, NN)
            h_ref[k, :, :known] = h[:, :known] + dot3(tail, known_far, NT)
            h_ref[k, :, known:] = h[:, known:] + dot3(tail, l_far, NN)


def steps_of(info, count):
    a = base(lax.axis_index("state"), count)
    return [info[pl.ds(a + shift, 1), :] for shift in (0, 1, 8, 9)]


def late_kernel(first, info, a_far, ga, gb, col, h, *refs):
    far, (ga_ref, gb_ref, mean_ref) = refs[:-3], refs[-3:]
    count, panel, order = h.shape
    j = 1 - lax.axis_index("state") % 2
    for k, (gain, out) in enumerate(((ga, ga_ref), (gb, gb_ref))):
        if far:
            at = far_row(2 + j, panel)
            p_last, l_last = unfold(far[0][k]), unfold(far[0][count + k])
            corner = [a_far[half, far_row(j, panel), at] for half in range(2)]
            out[at, :] = gain[at, :] + dot3(p_last, h[k], NN)
            out[:, at] += dot3(col[k], l_last, NN)
            out[at, at] += dot3(dot3(p_last, corner, NN), l_last, NN)
    mean_a, mean_b, pred_a, pred_b = steps_of(info, count)
    mean_ref[...] = mean_a + matvec(ga_ref[...], mean_b + matvec(gb_ref[...], first[...] - pred_b) - pred_a)


def two_kernel(x, info, ga, gb, out_ref):
    mean_a, mean_b, pred_a, pred_b = steps_of(info, 2)
    out_ref[...] = mean_a + matvec(ga[...], mean_b + matvec(gb[...], x[...] - pred_b) - pred_a)


def pair_kernel(info, ga, gb, map_ref):
    order = ga.shape[1]
    mean_a, mean_b, pred_a, pred_b = steps_of(info, 2)
    map_ref[order:, :] = jnp.concatenate(
        [mean_a + matvec(ga[...], mean_b - pred_a), mean_b, pred_b, jnp.zeros((5, order), F32)], axis=0
    )
    map_ref[:order, :] = dot3(ga[...], gb[...], NN)


def block_kernel(late, early, m_ref, vec_ref):
    order = late.shape[1]
    shift = early[order : order + 1, :] + matvec(
        early[:order, :], late[order : order + 1, :] - early[order + 2 : order + 3, :]
    )
    vec_ref[...] = jnp.concatenate([late[order + 2 : order + 3, :], shift, jnp.zeros((6, order), F32)], axis=0)
    m_ref[...] = dot3(early[:order, :], late[:order, :], NN)


def pair_hop_kernel(x, late, early, out_ref):
    order = x.shape[1]
    y = late[order : order + 1, :] + matvec(late[:order, :], x[...] - late[order + 2 : order + 3, :])
    out_ref[...] = early[order : order + 1, :] + matvec(early[:order, :], y - early[order + 2 : order + 3, :])


def hop_kernel(x, m, vec, out_ref):
    out_ref[...] = vec[1:2, :] + matvec(m[...], x[...] - vec[0:1, :])


def last_kernel(devices, *refs):
    blocks = len(refs) - 7 - devices
    incoming, (m, vec, late, g3, early, g1), outs, cut = refs[:blocks], refs[blocks : blocks + 6], refs[blocks + 6 : -1], refs[-1]
    order, panel = m.shape[1], outs[0].shape[1]
    b, s = lax.axis_index("tm"), lax.axis_index("state")
    x = incoming[0][...]
    for k, ref in enumerate(incoming[1:], 1):
        x = jnp.where(lax.axis_size("tm") - 1 - b == k, ref[...], x)
    gap = x - vec[0:1, :]
    x3 = late[order + 1 : order + 2, :] + matvec(g3[...], gap)
    x2 = late[order : order + 1, :] + matvec(late[:order, :], gap)
    x0 = vec[1:2, :] + matvec(m[...], gap)
    x1 = early[order + 1 : order + 2, :] + matvec(g1[...], x2 - early[order + 2 : order + 3, :])
    full = jnp.concatenate([x0, x1, x2, x3], axis=0)
    for i in range(devices):
        cut[i] = full[:, i * panel : (i + 1) * panel]
    for off, out in enumerate(outs):
        out[...] = cut[s ^ off]


def out_kernel(*refs):
    given, out_ref = [refs[0], *refs[-2:0:-1]], refs[-1]
    off = lax.axis_index("state") ^ 1
    x = given[0][...]
    for k, ref in enumerate(given[1:], 1):
        x = jnp.where(off == k, ref[...], x)
    out_ref[...] = x


def params(mebibytes):
    return pltpu.CompilerParams(vmem_limit_bytes=mebibytes * 2**20)


def local(filtered_covariance, pred_prec, transition, filt_means, terminal_mean):
    steps, panel, order = filtered_covariance.shape
    devices, blocks = lax.axis_size("state"), lax.axis_size("tm")
    count = steps // 2

    def swap(x, off, block_off=0):
        pairs = [(i, i ^ (block_off * devices + off)) for i in range(blocks * devices)]
        return lax.ppermute(x, ("tm", "state"), pairs)

    def shape(*dims):
        return jax.ShapeDtypeStruct(dims, F32)

    def call(kernel, name, mebibytes, outs, in_specs, scratch, args, aliases={}):
        return pl.pallas_call(
            kernel,
            out_shape=outs,
            in_specs=in_specs,
            out_specs=[VMEM] * len(outs),
            scratch_shapes=scratch,
            input_output_aliases=aliases,
            compiler_params=params(mebibytes),
            name=name,
        )(*args)

    cov, prec, trans, means, terminal = (
        pltpu.with_memory_space_constraint(x, pltpu.HBM)
        for x in (filtered_covariance, pred_prec, transition, filt_means, terminal_mean[None])
    )
    semaphores = pltpu.SemaphoreType.DMA((8 * devices,))
    square = shape(order, order)

    far = [shape(*far_shape(devices, count, panel, order, off)) for off in range(2, devices)]
    *far, trans_half, first = call(
        functools.partial(pack_kernel, devices),
        "pack",
        6,
        far + [shape(panel // 2, order), shape(1, order)],
        [HBM] * 4,
        [pltpu.VMEM((1, order), F32), pltpu.VMEM((2, steps, panel, panel), F32), semaphores],
        (cov, prec, trans, terminal),
    )
    across = [swap(trans_half, off) for off in range(2, devices, 2)]
    far = [swap(x, off) for off, x in enumerate(far, 2)]
    moved = [y for x in across for y in (x, swap(x, 1, 1))]
    near = call(
        near_kernel,
        "near",
        4,
        [shape(count * panel, order)] * 2,
        [HBM] * 2 + [ANY],
        [semaphores],
        (cov, prec, first),
    )
    near = [swap(x, 1) for x in near]
    own, own_trans, own_means = call(
        own_kernel,
        "own",
        4,
        [shape(2 * count, panel, order), shape(panel, order), shape(steps, order)],
        [HBM] * 4 + [ANY],
        [semaphores],
        (cov, prec, trans, means, across[0]),
    )
    (joined,) = call(
        join_kernel,
        "join",
        4,
        [shape(devices // 2 - 1, panel, order)],
        [ANY] * (1 + len(moved)),
        [semaphores],
        (own_trans, *moved),
    )
    joined_near = swap(joined, 1)
    trans_near = swap(transition, 1)

    known = 2 * panel
    parts = call(
        early_kernel,
        "early",
        24,
        [
            shape(16, order),
            jax.ShapeDtypeStruct((2, order - known, order), BF16),
            jax.ShapeDtypeStruct((count, 2, known, order), BF16),
            shape(count, known, order - known),
            shape(count, order - known, order),
            shape(count, known, order),
        ],
        [ANY, VMEM] + [ANY] * 2 + [ANY] * 4,
        [
            pltpu.VMEM((count * known + 16, order), F32),
            pltpu.VMEM((order, order), F32),
            pltpu.VMEM((count, known, order), F32),
            semaphores,
        ],
        (own, own_means, own_trans, trans_near, joined, joined_near, *near),
    )
    info, a_far = parts[:2]
    last = far[1:] if trimmed(devices, panel) else []
    ga, gb, col, h = call(
        middle_kernel,
        "middle",
        24,
        [square, square, shape(count, order, panel), shape(count, panel, order)],
        [VMEM] * (5 + len(far) - len(last)),
        [pltpu.VMEM((2 * count, order - known, order - known), F32)],
        (*parts[1:], *far[: len(far) - len(last)]),
    )
    ga, gb, mean = call(
        late_kernel,
        "late",
        12,
        [square, square, shape(1, order)],
        [VMEM] * (7 + len(last)),
        [],
        (first, info, a_far, ga, gb, col, h, *last),
        {3: 0, 4: 1},
    )
    mean = swap(mean, 1)
    (early_map,) = call(pair_kernel, "pair", 12, [shape(order + 8, order)], [VMEM] * 3, [], (info, ga, gb))
    late_map = swap(lax.optimization_barrier((early_map, mean))[0], 1)
    (mean,) = call(two_kernel, "two", 6, [shape(1, order)], [VMEM] * 4, [], (mean, info, ga, gb))

    def hop(x, block):
        target = {i: i ^ 1 for i in range(blocks * devices)}
        for at, to in ((block, block - 1), (block - 1, block)):
            target[at * devices + 1] = to * devices + 1
            target.update({at * devices + i: at * devices + j for i, j in ((0, 2), (2, 3), (3, 0))})
        return lax.ppermute(x, ("tm", "state"), list(target.items()))

    incoming = [first, hop(mean, blocks - 1)]
    (x,) = call(pair_hop_kernel, "pair_hop", 4, [shape(1, order)], [VMEM] * 3, [], (incoming[-1], late_map, early_map))
    m, vec = call(block_kernel, "block", 12, [square, shape(8, order)], [VMEM] * 2, [], (late_map, early_map))
    for block in range(blocks - 2, 0, -1):
        if block < blocks - 2:
            (x,) = call(hop_kernel, "hop", 4, [shape(1, order)], [VMEM] * 3, [], (incoming[-1], m, vec))
        incoming.append(hop(x, block))
    g3 = swap(lax.optimization_barrier((gb, incoming[3]))[0], 1)

    given = list(call(
        functools.partial(last_kernel, devices),
        "last",
        8,
        [shape(steps, panel)] * devices,
        [VMEM] * (blocks + 6),
        [pltpu.VMEM((devices, steps, panel), F32)],
        (*incoming, m, vec, late_map, g3, early_map, gb),
    ))
    for off in range(devices - 1, 0, -1):
        given[off] = swap(given[off], off)
    given = [given[0], *given[:0:-1]]
    (out,) = call(out_kernel, "out", 4, [shape(steps, panel)], [VMEM] * devices, [], given)
    return out


def solution(mesh):
    return jax.shard_map(
        local,
        mesh=mesh,
        in_specs=(
            P("tm", "state", None),
            P("tm", "state", None),
            P("state", None),
            P("tm", None),
            P(),
        ),
        out_specs=P("tm", "state"),
        check_vma=False,
    )
```

```python
import functools

import jax
import jax.numpy as jnp
from jax import lax
from jax.experimental import pallas as pl
from jax.experimental.pallas import tpu as pltpu
from jax.sharding import PartitionSpec as P

F32, BF16 = jnp.float32, jnp.bfloat16
NN = (((1,), (0,)), ((), ()))
NT = (((1,), (1,)), ((), ()))
ANY = pl.BlockSpec(memory_space=pl.ANY)
HBM = pl.BlockSpec(memory_space=pltpu.HBM)
VMEM = pl.BlockSpec(memory_space=pltpu.VMEM)


def split(x):
    high = x.astype(BF16)
    return high, (x - high.astype(F32)).astype(BF16)


def dot3(a, b, dims):
    (ah, al), (bh, bl) = (split(x) if getattr(x, "dtype", None) == F32 else (x[0][...], x[1][...]) for x in (a, b))
    dot = functools.partial(lax.dot_general, dimension_numbers=dims, preferred_element_type=F32)
    return dot(ah, bh) + (dot(ah, bl) + dot(al, bh))


def matvec(matrix, row):
    order = matrix.shape[1]
    total = matrix[:, :128] * row[:, :128]
    for j in range(128, order, 128):
        total += matrix[:, j : j + 128] * row[:, j : j + 128]
    return jnp.sum(total.T, axis=0, keepdims=True)


def rows(i, panel):
    return pl.ds(pl.multiple_of(i * panel, panel), panel)


def starter(sems):
    copies = []

    def start(source, target):
        copy = pltpu.make_async_copy(source, target, sems.at[len(copies)])
        copy.start()
        copies.append(copy)

    return start, copies


def trimmed(devices, panel):
    return devices == 4 and panel == 128


def far_shape(devices, count, panel, order, off):
    if trimmed(devices, panel):
        return (2 * count, panel * 9 // 16 + (panel if off == 2 else 0), panel)
    return (2 * count, panel, order - 2 * panel)


def lanes(rows):
    return lax.broadcasted_iota(jnp.int32, (rows, 128), 1)


def fold(block):
    lower = ((112, 16), (96, 32), (80, 48))
    filled = [
        jnp.where(lanes(16) < width, pltpu.roll(block[row : row + 16], width, 1), block[width : width + 16])
        for row, width in lower
    ]
    rest = jnp.where(lanes(8) < 64, pltpu.roll(block[64:72], 64, 1), block[72:80])
    return jnp.concatenate([block[:16], *filled, rest], axis=0)


def unfold(folded):
    rest = folded[64:]
    moved = [pltpu.roll(folded[width : width + 16], 128 - width, 1) for width in (48, 32, 16)]
    upper = jnp.concatenate([folded[:64], pltpu.roll(rest, 64, 1), rest, *moved], axis=0)
    row = lax.broadcasted_iota(jnp.int32, (128, 128), 0)
    return jnp.where(row // 16 <= lanes(128) // 16, upper, upper.T)


def base(device, count):
    return (1 - device % 2) * count


def pack_kernel(devices, cov, prec, trans, terminal, *refs):
    far, (trans_half, first, vector, diagonal, sems) = refs[: devices - 2], refs[devices - 2 :]
    count, panel, order = cov.shape[0] // 2, *cov.shape[1:]
    b, s = lax.axis_index("tm"), lax.axis_index("state")
    start, copies = starter(sems)
    start(terminal, vector)
    start(trans.at[pl.ds(pl.multiple_of((b % 2) * (panel // 2), panel // 2), panel // 2), :], trans_half)
    trim = trimmed(devices, panel)
    if trim:
        for k, matrix in enumerate((cov, prec)):
            start(matrix.at[:, :, rows(s, panel)], diagonal.at[k])
    for off, piece in enumerate(far, 2):
        theirs = pl.ds(base(s ^ off, count), count)
        for k, matrix in enumerate((cov, prec)):
            target = piece.at[pl.ds(k * count, count)]
            if not trim:
                start(matrix.at[theirs, :, 2 * panel :], target)
            elif off == 2:
                start(matrix.at[theirs, :, rows(s ^ 1, panel)], target.at[:, :panel])
    copies[0].wait()
    first[...] = jnp.where(b == lax.axis_size("tm") - 1, vector[...], 0.0)
    for copy in copies[1:]:
        copy.wait()
    if trim:
        for off, piece in enumerate(far, 2):
            for k in range(2 * count):
                block = diagonal[k // count, base(s ^ off, count) + k % count]
                piece[k, piece.shape[1] - panel * 9 // 16 :, :] = fold(block)


def near_kernel(cov, prec, trans, after, near_cov, near_prec, near_trans, sems):
    count = cov.shape[0] // 2
    theirs = pl.ds((1 - lax.axis_index("state") % 2) * count, count)
    start, copies = starter(sems)
    start(cov.at[theirs], near_cov)
    start(prec.at[theirs], near_prec)
    start(trans, near_trans)
    for copy in copies:
        copy.wait()


def near_kernel(cov, prec, after, *refs):
    pieces, sems = refs[:-1], refs[-1]
    count, panel = cov.shape[0] // 2, cov.shape[1]
    first = base(lax.axis_index("state") ^ 1, count)
    start, copies = starter(sems)
    for k in range(2 * count):
        matrix = (cov, prec)[k // count]
        for piece, at, source, size in spans(pieces, k, panel):
            start(matrix.at[first + k % count, pl.ds(source, size), :], pieces[piece].at[pl.ds(at, size), :])
    for copy in copies:
        copy.wait()


def spans(pieces, k, panel):
    found, at = [], 0
    for i, piece in enumerate(pieces):
        low, high = max(at, k * panel), min(at + piece.shape[0], (k + 1) * panel)
        if low < high:
            found.append((i, low - at, low - k * panel, high - low))
        at += piece.shape[0]
    return found


def own_kernel(cov, prec, trans, means, after, own, own_trans, own_means, sems):
    count = cov.shape[0] // 2
    mine = pl.ds(base(lax.axis_index("state"), count), count)
    start, copies = starter(sems)
    start(cov.at[mine], own.at[pl.ds(0, count)])
    start(prec.at[mine], own.at[pl.ds(count, count)])
    start(trans, own_trans)
    start(means, own_means)
    for copy in copies:
        copy.wait()


def join_kernel(after, *refs):
    moved, (joined, sems) = refs[:-2], refs[-2:]
    half = moved[0].shape[0]
    b = lax.axis_index("tm")
    start, copies = starter(sems)
    for k, piece in enumerate(moved):
        at = (b % 2 if k % 2 == 0 else 1 - b % 2) * half
        start(piece, joined.at[k // 2, pl.ds(pl.multiple_of(at, half), half), :])
    for copy in copies:
        copy.wait()


def early_kernel(own, means, trans, trans_near, joined, joined_near, *refs):
    near, (info, a_far, l_known, c_known, c_far, g_known, pf, af, lf, sems) = refs[:-10], refs[-10:]
    panel, order = own.shape[1:]
    count, known = own.shape[0] // 2, 2 * panel
    steps = means.shape[0]
    e = lax.axis_index("state") % 2
    start, copies = starter(sems)
    for k in range(2 * count):
        target, top = (pf, k * known) if k < count else (lf.at[k - count], 0)
        start(own.at[k], target.at[pl.ds(pl.multiple_of(top + e * panel, panel), panel), :])
        for piece, at, row, size in spans(near, k, panel):
            to = pl.multiple_of(top + (1 - e) * panel + row, 8)
            start(near[piece].at[pl.ds(at, size), :], target.at[pl.ds(to, size), :])
    for j in range(order // known):
        mine, theirs = (joined.at[j - 1], joined_near.at[j - 1]) if j else (trans, trans_near)
        start(mine, af.at[rows(e ^ (2 * j), panel), :])
        start(theirs, af.at[rows(e ^ (2 * j) ^ 1, panel), :])
    pf[count * known :, :] = jnp.concatenate([means[...], jnp.zeros((16 - steps, order), F32)], axis=0)
    for copy in copies:
        copy.wait()
    product = dot3(pf[...], af[...], NT)
    info[:8] = pf[count * known : count * known + 8, :]
    info[8:] = product[count * known : count * known + 8]
    for half, x in enumerate(split(af[:, known:].T)):
        a_far[half] = x
    across = jnp.concatenate([pf[k * known : (k + 1) * known, known:].T for k in range(count)], axis=0)
    rest = dot3(across, af[:, :known], NT)
    for k in range(count):
        part = product[k * known : (k + 1) * known]
        for half, x in enumerate(split(lf[k])):
            l_known[k, half] = x
        partial = dot3(part[:, :known], lf[k], NN)
        g_known[k, :, :known] = partial[:, :known] + dot3(part[:, known:], lf[k, :, known:], NT)
        g_known[k, :, known:] = partial[:, known:]
        c_known[k] = part[:, known:]
        c_far[k] = rest[k * (order - known) : (k + 1) * (order - known)]


def steps_of(info, count):
    a = base(lax.axis_index("state"), count)
    return [info[pl.ds(a + shift, 1), :] for shift in (0, 1, 8, 9)]


def far_row(j, panel):
    return pl.ds(pl.multiple_of(j * panel, panel), panel)


def middle_kernel(a_far, l_known, c_known, c_far, g_known, *refs):
    far, (ga_ref, gb_ref, col_ref, h_ref, ff) = refs[:-5], refs[-5:]
    count, known, order = g_known.shape
    panel = known // 2
    e = lax.axis_index("state") % 2
    i, j = e, 1 - e
    for k in range(2 * count):
        if len(far) > 1:
            for off, piece in enumerate(far, 2):
                ff[k, rows((e ^ off) - 2, panel), :] = piece[k]
            continue
        beside, folded = far[0][k, :panel], far[0][k, panel:]
        ff[k, rows(i, panel), rows(i, panel)] = unfold(folded)
        ff[k, rows(j, panel), rows(j, panel)] = jnp.zeros((panel, panel), F32)
        ff[k, rows(i, panel), rows(j, panel)] = beside
        ff[k, rows(j, panel), rows(i, panel)] = beside.T

    for k, out in enumerate((ga_ref, gb_ref)):
        c = c_far[k] + dot3(ff[k], a_far, NN)
        known_rows = (l_known.at[k, 0], l_known.at[k, 1])
        known_far = [x[:, known:] for x in known_rows]
        l_far = split(ff[count + k])
        column = jnp.concatenate([c_known[k], c[:, known:]], axis=0)
        share = dot3(column, l_far, NN)
        low = dot3(c[:, :known], known_rows, NN)
        out[:known, :known] = g_known[k, :, :known]
        out[:known, known:] = g_known[k, :, known:] + share[:known]
        out[known:, :known] = low[:, :known] + dot3(c[:, known:], known_far, NT)
        out[known:, known:] = low[:, known:] + share[known:]
        if len(far) == 1:
            col_ref[k] = jnp.where(j == 0, column[:, :panel], column[:, panel:])
            halves = a_far[0, far_row(j, panel), :], a_far[1, far_row(j, panel), :]
            head, tail = [x[:, :known] for x in halves], [x[:, known:] for x in halves]
            h = dot3(head, known_rows, NN)
            h_ref[k, :, :known] = h[:, :known] + dot3(tail, known_far, NT)
            h_ref[k, :, known:] = h[:, known:] + dot3(tail, l_far, NN)


def steps_of(info, count):
    a = base(lax.axis_index("state"), count)
    return [info[pl.ds(a + shift, 1), :] for shift in (0, 1, 8, 9)]


def late_kernel(first, info, a_far, ga, gb, col, h, *refs):
    far, (ga_ref, gb_ref, mean_ref) = refs[:-3], refs[-3:]
    count, panel, order = h.shape
    j = 1 - lax.axis_index("state") % 2
    for k, (gain, out) in enumerate(((ga, ga_ref), (gb, gb_ref))):
        if far:
            at = far_row(2 + j, panel)
            p_last, l_last = unfold(far[0][k]), unfold(far[0][count + k])
            corner = [a_far[half, far_row(j, panel), at] for half in range(2)]
            out[at, :] = gain[at, :] + dot3(p_last, h[k], NN)
            out[:, at] += dot3(col[k], l_last, NN)
            out[at, at] += dot3(dot3(p_last, corner, NN), l_last, NN)
    mean_a, mean_b, pred_a, pred_b = steps_of(info, count)
    mean_ref[...] = mean_a + matvec(ga_ref[...], mean_b + matvec(gb_ref[...], first[...] - pred_b) - pred_a)


def two_kernel(x, info, ga, gb, out_ref):
    mean_a, mean_b, pred_a, pred_b = steps_of(info, 2)
    out_ref[...] = mean_a + matvec(ga[...], mean_b + matvec(gb[...], x[...] - pred_b) - pred_a)


def pair_kernel(info, ga, gb, map_ref):
    order = ga.shape[1]
    mean_a, mean_b, pred_a, pred_b = steps_of(info, 2)
    map_ref[order:, :] = jnp.concatenate(
        [mean_a + matvec(ga[...], mean_b - pred_a), mean_b, pred_b, jnp.zeros((5, order), F32)], axis=0
    )
    map_ref[:order, :] = dot3(ga[...], gb[...], NN)


def block_kernel(late, early, m_ref, vec_ref):
    order = late.shape[1]
    shift = early[order : order + 1, :] + matvec(
        early[:order, :], late[order : order + 1, :] - early[order + 2 : order + 3, :]
    )
    vec_ref[...] = jnp.concatenate([late[order + 2 : order + 3, :], shift, jnp.zeros((6, order), F32)], axis=0)
    m_ref[...] = dot3(early[:order, :], late[:order, :], NN)


def pair_hop_kernel(x, late, early, out_ref):
    order = x.shape[1]
    y = late[order : order + 1, :] + matvec(late[:order, :], x[...] - late[order + 2 : order + 3, :])
    out_ref[...] = early[order : order + 1, :] + matvec(early[:order, :], y - early[order + 2 : order + 3, :])


def hop_kernel(x, m, vec, out_ref):
    out_ref[...] = vec[1:2, :] + matvec(m[...], x[...] - vec[0:1, :])


def last_kernel(devices, *refs):
    blocks = len(refs) - 7 - devices
    incoming, (m, vec, late, g3, early, g1), outs, cut = refs[:blocks], refs[blocks : blocks + 6], refs[blocks + 6 : -1], refs[-1]
    order, panel = m.shape[1], outs[0].shape[1]
    b, s = lax.axis_index("tm"), lax.axis_index("state")
    x = incoming[0][...]
    for k, ref in enumerate(incoming[1:], 1):
        x = jnp.where(lax.axis_size("tm") - 1 - b == k, ref[...], x)
    gap = x - vec[0:1, :]
    x3 = late[order + 1 : order + 2, :] + matvec(g3[...], gap)
    x2 = late[order : order + 1, :] + matvec(late[:order, :], gap)
    x0 = vec[1:2, :] + matvec(m[...], gap)
    x1 = early[order + 1 : order + 2, :] + matvec(g1[...], x2 - early[order + 2 : order + 3, :])
    full = jnp.concatenate([x0, x1, x2, x3], axis=0)
    for i in range(devices):
        cut[i] = full[:, i * panel : (i + 1) * panel]
    for off, out in enumerate(outs):
        out[...] = cut[s ^ off]


def out_kernel(*refs):
    given, out_ref = [refs[0], *refs[-2:0:-1]], refs[-1]
    off = lax.axis_index("state") ^ 1
    x = given[0][...]
    for k, ref in enumerate(given[1:], 1):
        x = jnp.where(off == k, ref[...], x)
    out_ref[...] = x


def params(mebibytes):
    return pltpu.CompilerParams(vmem_limit_bytes=mebibytes * 2**20)


def local(filtered_covariance, pred_prec, transition, filt_means, terminal_mean):
    steps, panel, order = filtered_covariance.shape
    devices, blocks = lax.axis_size("state"), lax.axis_size("tm")
    count = steps // 2

    def swap(x, off, block_off=0):
        pairs = [(i, i ^ (block_off * devices + off)) for i in range(blocks * devices)]
        return lax.ppermute(x, ("tm", "state"), pairs)

    def shape(*dims):
        return jax.ShapeDtypeStruct(dims, F32)

    def call(kernel, name, mebibytes, outs, in_specs, scratch, args, aliases={}):
        return pl.pallas_call(
            kernel,
            out_shape=outs,
            in_specs=in_specs,
            out_specs=[VMEM] * len(outs),
            scratch_shapes=scratch,
            input_output_aliases=aliases,
            compiler_params=params(mebibytes),
            name=name,
        )(*args)

    cov, prec, trans, means, terminal = (
        pltpu.with_memory_space_constraint(x, pltpu.HBM)
        for x in (filtered_covariance, pred_prec, transition, filt_means, terminal_mean[None])
    )
    semaphores = pltpu.SemaphoreType.DMA((8 * devices,))
    square = shape(order, order)

    far = [shape(*far_shape(devices, count, panel, order, off)) for off in range(2, devices)]
    *far, trans_half, first = call(
        functools.partial(pack_kernel, devices),
        "pack",
        6,
        far + [shape(panel // 2, order), shape(1, order)],
        [HBM] * 4,
        [pltpu.VMEM((1, order), F32), pltpu.VMEM((2, steps, panel, panel), F32), semaphores],
        (cov, prec, trans, terminal),
    )
    across = [swap(trans_half, off) for off in range(2, devices, 2)]
    far = [swap(x, off) for off, x in enumerate(far, 2)]
    moved = [y for x in across for y in (x, swap(x, 0, 1))]
    near = call(
        near_kernel,
        "near",
        4,
        [shape(count * panel, order)] * 2,
        [HBM] * 2 + [ANY],
        [semaphores],
        (cov, prec, first),
    )
    near = [swap(x, 1) for x in near]
    own, own_trans, own_means = call(
        own_kernel,
        "own",
        4,
        [shape(2 * count, panel, order), shape(panel, order), shape(steps, order)],
        [HBM] * 4 + [ANY],
        [semaphores],
        (cov, prec, trans, means, across[0]),
    )
    (joined,) = call(
        join_kernel,
        "join",
        4,
        [shape(devices // 2 - 1, panel, order)],
        [ANY] * (1 + len(moved)),
        [semaphores],
        (own_trans, *moved),
    )
    joined_near = swap(joined, 1)
    trans_near = swap(transition, 1)

    known = 2 * panel
    parts = call(
        early_kernel,
        "early",
        24,
        [
            shape(16, order),
            jax.ShapeDtypeStruct((2, order - known, order), BF16),
            jax.ShapeDtypeStruct((count, 2, known, order), BF16),
            shape(count, known, order - known),
            shape(count, order - known, order),
            shape(count, known, order),
        ],
        [ANY, VMEM] + [ANY] * 2 + [ANY] * 4,
        [
            pltpu.VMEM((count * known + 16, order), F32),
            pltpu.VMEM((order, order), F32),
            pltpu.VMEM((count, known, order), F32),
            semaphores,
        ],
        (own, own_means, own_trans, trans_near, joined, joined_near, *near),
    )
    info, a_far = parts[:2]
    last = far[1:] if trimmed(devices, panel) else []
    ga, gb, col, h = call(
        middle_kernel,
        "middle",
        24,
        [square, square, shape(count, order, panel), shape(count, panel, order)],
        [VMEM] * (5 + len(far) - len(last)),
        [pltpu.VMEM((2 * count, order - known, order - known), F32)],
        (*parts[1:], *far[: len(far) - len(last)]),
    )
    ga, gb, mean = call(
        late_kernel,
        "late",
        12,
        [square, square, shape(1, order)],
        [VMEM] * (7 + len(last)),
        [],
        (first, info, a_far, ga, gb, col, h, *last),
        {3: 0, 4: 1},
    )
    mean = swap(mean, 1)
    (early_map,) = call(pair_kernel, "pair", 12, [shape(order + 8, order)], [VMEM] * 3, [], (info, ga, gb))
    late_map = swap(lax.optimization_barrier((early_map, mean))[0], 1)
    (mean,) = call(two_kernel, "two", 6, [shape(1, order)], [VMEM] * 4, [], (mean, info, ga, gb))

    def hop(x, block):
        target = {i: i ^ 1 for i in range(blocks * devices)}
        for at, to in ((block, block - 1), (block - 1, block)):
            target[at * devices + 1] = to * devices + 1
            target.update({at * devices + i: at * devices + j for i, j in ((0, 2), (2, 3), (3, 0))})
        return lax.ppermute(x, ("tm", "state"), list(target.items()))

    incoming = [first, hop(mean, blocks - 1)]
    (x,) = call(pair_hop_kernel, "pair_hop", 4, [shape(1, order)], [VMEM] * 3, [], (incoming[-1], late_map, early_map))
    m, vec = call(block_kernel, "block", 12, [square, shape(8, order)], [VMEM] * 2, [], (late_map, early_map))
    for block in range(blocks - 2, 0, -1):
        if block < blocks - 2:
            (x,) = call(hop_kernel, "hop", 4, [shape(1, order)], [VMEM] * 3, [], (incoming[-1], m, vec))
        incoming.append(hop(x, block))
    g3 = swap(lax.optimization_barrier((gb, incoming[3]))[0], 1)

    given = list(call(
        functools.partial(last_kernel, devices),
        "last",
        8,
        [shape(steps, panel)] * devices,
        [VMEM] * (blocks + 6),
        [pltpu.VMEM((devices, steps, panel), F32)],
        (*incoming, m, vec, late_map, g3, early_map, gb),
    ))
    for off in range(devices - 1, 0, -1):
        given[off] = swap(given[off], off)
    given = [given[0], *given[:0:-1]]
    (out,) = call(out_kernel, "out", 4, [shape(steps, panel)], [VMEM] * devices, [], given)
    return out


def solution(mesh):
    return jax.shard_map(
        local,
        mesh=mesh,
        in_specs=(
            P("tm", "state", None),
            P("tm", "state", None),
            P("state", None),
            P("tm", None),
            P(),
        ),
        out_specs=P("tm", "state"),
        check_vma=False,
    )
```

```python
import functools

import jax
import jax.numpy as jnp
from jax import lax
from jax.experimental import pallas as pl
from jax.experimental.pallas import tpu as pltpu
from jax.sharding import PartitionSpec as P

F32, BF16 = jnp.float32, jnp.bfloat16
NN = (((1,), (0,)), ((), ()))
NT = (((1,), (1,)), ((), ()))
ANY = pl.BlockSpec(memory_space=pl.ANY)
HBM = pl.BlockSpec(memory_space=pltpu.HBM)
VMEM = pl.BlockSpec(memory_space=pltpu.VMEM)


def split(x):
    high = x.astype(BF16)
    return high, (x - high.astype(F32)).astype(BF16)


def dot3(a, b, dims):
    (ah, al), (bh, bl) = (split(x) if getattr(x, "dtype", None) == F32 else (x[0][...], x[1][...]) for x in (a, b))
    dot = functools.partial(lax.dot_general, dimension_numbers=dims, preferred_element_type=F32)
    return dot(ah, bh) + (dot(ah, bl) + dot(al, bh))


def matvec(matrix, row):
    order = matrix.shape[1]
    total = matrix[:, :128] * row[:, :128]
    for j in range(128, order, 128):
        total += matrix[:, j : j + 128] * row[:, j : j + 128]
    return jnp.sum(total.T, axis=0, keepdims=True)


def rows(i, panel):
    return pl.ds(pl.multiple_of(i * panel, panel), panel)


def starter(sems):
    copies = []

    def start(source, target):
        copy = pltpu.make_async_copy(source, target, sems.at[len(copies)])
        copy.start()
        copies.append(copy)

    return start, copies


def trimmed(devices, panel):
    return devices == 4 and panel == 128


def far_shape(devices, count, panel, order, off):
    if trimmed(devices, panel):
        return (2 * count, panel * 9 // 16 + (panel if off == 2 else 0), panel)
    return (2 * count, panel, order - 2 * panel)


def lanes(rows):
    return lax.broadcasted_iota(jnp.int32, (rows, 128), 1)


def fold(block):
    lower = ((112, 16), (96, 32), (80, 48))
    filled = [
        jnp.where(lanes(16) < width, pltpu.roll(block[row : row + 16], width, 1), block[width : width + 16])
        for row, width in lower
    ]
    rest = jnp.where(lanes(8) < 64, pltpu.roll(block[64:72], 64, 1), block[72:80])
    return jnp.concatenate([block[:16], *filled, rest], axis=0)


def unfold(folded):
    rest = folded[64:]
    moved = [pltpu.roll(folded[width : width + 16], 128 - width, 1) for width in (48, 32, 16)]
    upper = jnp.concatenate([folded[:64], pltpu.roll(rest, 64, 1), rest, *moved], axis=0)
    row = lax.broadcasted_iota(jnp.int32, (128, 128), 0)
    return jnp.where(row // 16 <= lanes(128) // 16, upper, upper.T)


def base(device, count):
    return (1 - device % 2) * count


def pack_kernel(devices, cov, prec, trans, terminal, *refs):
    far, (trans_half, first, vector, diagonal, sems) = refs[: devices - 2], refs[devices - 2 :]
    count, panel, order = cov.shape[0] // 2, *cov.shape[1:]
    b, s = lax.axis_index("tm"), lax.axis_index("state")
    start, copies = starter(sems)
    start(terminal, vector)
    start(trans.at[pl.ds(pl.multiple_of((b % 2) * (panel // 2), panel // 2), panel // 2), :], trans_half)
    trim = trimmed(devices, panel)
    if trim:
        for k, matrix in enumerate((cov, prec)):
            start(matrix.at[:, :, rows(s, panel)], diagonal.at[k])
    for off, piece in enumerate(far, 2):
        theirs = pl.ds(base(s ^ off, count), count)
        for k, matrix in enumerate((cov, prec)):
            target = piece.at[pl.ds(k * count, count)]
            if not trim:
                start(matrix.at[theirs, :, 2 * panel :], target)
            elif off == 2:
                start(matrix.at[theirs, :, rows(s ^ 1, panel)], target.at[:, :panel])
    copies[0].wait()
    first[...] = jnp.where(b == lax.axis_size("tm") - 1, vector[...], 0.0)
    for copy in copies[1:]:
        copy.wait()
    if trim:
        for off, piece in enumerate(far, 2):
            for k in range(2 * count):
                block = diagonal[k // count, base(s ^ off, count) + k % count]
                piece[k, piece.shape[1] - panel * 9 // 16 :, :] = fold(block)


def near_kernel(cov, prec, trans, after, near_cov, near_prec, near_trans, sems):
    count = cov.shape[0] // 2
    theirs = pl.ds((1 - lax.axis_index("state") % 2) * count, count)
    start, copies = starter(sems)
    start(cov.at[theirs], near_cov)
    start(prec.at[theirs], near_prec)
    start(trans, near_trans)
    for copy in copies:
        copy.wait()


def near_kernel(cov, prec, after, *refs):
    pieces, sems = refs[:-1], refs[-1]
    count, panel = cov.shape[0] // 2, cov.shape[1]
    first = base(lax.axis_index("state") ^ 1, count)
    start, copies = starter(sems)
    for k in range(2 * count):
        matrix = (cov, prec)[k // count]
        for piece, at, source, size in spans(pieces, k, panel):
            start(matrix.at[first + k % count, pl.ds(source, size), :], pieces[piece].at[pl.ds(at, size), :])
    for copy in copies:
        copy.wait()


def spans(pieces, k, panel):
    found, at = [], 0
    for i, piece in enumerate(pieces):
        low, high = max(at, k * panel), min(at + piece.shape[0], (k + 1) * panel)
        if low < high:
            found.append((i, low - at, low - k * panel, high - low))
        at += piece.shape[0]
    return found


def own_kernel(cov, prec, trans, means, after, own, own_trans, own_means, sems):
    count = cov.shape[0] // 2
    mine = pl.ds(base(lax.axis_index("state"), count), count)
    start, copies = starter(sems)
    start(cov.at[mine], own.at[pl.ds(0, count)])
    start(prec.at[mine], own.at[pl.ds(count, count)])
    start(trans, own_trans)
    start(means, own_means)
    for copy in copies:
        copy.wait()


def join_kernel(after, *refs):
    moved, (joined, sems) = refs[:-2], refs[-2:]
    half = moved[0].shape[0]
    b = lax.axis_index("tm")
    start, copies = starter(sems)
    for k, piece in enumerate(moved):
        at = (b % 2 if k % 2 == 0 else 1 - b % 2) * half
        start(piece, joined.at[k // 2, pl.ds(pl.multiple_of(at, half), half), :])
    for copy in copies:
        copy.wait()


def early_kernel(own, means, trans, trans_near, joined, joined_near, *refs):
    near, (info, a_far, l_known, c_known, c_far, g_known, pf, af, lf, sems) = refs[:-10], refs[-10:]
    panel, order = own.shape[1:]
    count, known = own.shape[0] // 2, 2 * panel
    steps = means.shape[0]
    e = lax.axis_index("state") % 2
    start, copies = starter(sems)
    for k in range(2 * count):
        target, top = (pf, k * known) if k < count else (lf.at[k - count], 0)
        start(own.at[k], target.at[pl.ds(pl.multiple_of(top + e * panel, panel), panel), :])
        for piece, at, row, size in spans(near, k, panel):
            to = pl.multiple_of(top + (1 - e) * panel + row, 8)
            start(near[piece].at[pl.ds(at, size), :], target.at[pl.ds(to, size), :])
    for j in range(order // known):
        mine, theirs = (joined.at[j - 1], joined_near.at[j - 1]) if j else (trans, trans_near)
        start(mine, af.at[rows(e ^ (2 * j), panel), :])
        start(theirs, af.at[rows(e ^ (2 * j) ^ 1, panel), :])
    pf[count * known :, :] = jnp.concatenate([means[...], jnp.zeros((16 - steps, order), F32)], axis=0)
    for copy in copies:
        copy.wait()
    product = dot3(pf[...], af[...], NT)
    info[:8] = pf[count * known : count * known + 8, :]
    info[8:] = product[count * known : count * known + 8]
    for half, x in enumerate(split(af[:, known:].T)):
        a_far[half] = x
    across = jnp.concatenate([pf[k * known : (k + 1) * known, known:].T for k in range(count)], axis=0)
    rest = dot3(across, af[:, :known], NT)
    for k in range(count):
        part = product[k * known : (k + 1) * known]
        for half, x in enumerate(split(lf[k])):
            l_known[k, half] = x
        partial = dot3(part[:, :known], lf[k], NN)
        g_known[k, :, :known] = partial[:, :known] + dot3(part[:, known:], lf[k, :, known:], NT)
        g_known[k, :, known:] = partial[:, known:]
        c_known[k] = part[:, known:]
        c_far[k] = rest[k * (order - known) : (k + 1) * (order - known)]


def steps_of(info, count):
    a = base(lax.axis_index("state"), count)
    return [info[pl.ds(a + shift, 1), :] for shift in (0, 1, 8, 9)]


def far_row(j, panel):
    return pl.ds(pl.multiple_of(j * panel, panel), panel)


def middle_kernel(a_far, l_known, c_known, c_far, g_known, *refs):
    far, (ga_ref, gb_ref, col_ref, h_ref, ff) = refs[:-5], refs[-5:]
    count, known, order = g_known.shape
    panel = known // 2
    e = lax.axis_index("state") % 2
    i, j = e, 1 - e
    for k in range(2 * count):
        if len(far) > 1:
            for off, piece in enumerate(far, 2):
                ff[k, rows((e ^ off) - 2, panel), :] = piece[k]
            continue
        beside, folded = far[0][k, :panel], far[0][k, panel:]
        ff[k, rows(i, panel), rows(i, panel)] = unfold(folded)
        ff[k, rows(j, panel), rows(j, panel)] = jnp.zeros((panel, panel), F32)
        ff[k, rows(i, panel), rows(j, panel)] = beside
        ff[k, rows(j, panel), rows(i, panel)] = beside.T

    for k, out in enumerate((ga_ref, gb_ref)):
        c = c_far[k] + dot3(ff[k], a_far, NN)
        known_rows = (l_known.at[k, 0], l_known.at[k, 1])
        known_far = [x[:, known:] for x in known_rows]
        column = jnp.concatenate([c_known[k], c[:, known:]], axis=0)
        low_rows, share_rows = split(c), split(column)
        if len(far) == 1:
            halves = a_far[0, far_row(j, panel), :], a_far[1, far_row(j, panel), :]
            low_rows = [jnp.concatenate([x, y], axis=0) for x, y in zip(low_rows, halves)]
            share_rows = [jnp.concatenate([x, y[:, known:]], axis=0) for x, y in zip(share_rows, halves)]
        share = dot3(share_rows, split(ff[count + k]), NN)
        low = dot3([x[:, :known] for x in low_rows], known_rows, NN)
        left = low[:, :known] + dot3([x[:, known:] for x in low_rows], known_far, NT)
        right = low[:, known:] + share[known:]
        size = order - known
        out[:known, :known] = g_known[k, :, :known]
        out[:known, known:] = g_known[k, :, known:] + share[:known]
        out[known:, :known] = left[:size]
        out[known:, known:] = right[:size]
        if len(far) == 1:
            col_ref[k] = jnp.where(j == 0, column[:, :panel], column[:, panel:])
            h_ref[k, :, :known] = left[size:]
            h_ref[k, :, known:] = right[size:]


def steps_of(info, count):
    a = base(lax.axis_index("state"), count)
    return [info[pl.ds(a + shift, 1), :] for shift in (0, 1, 8, 9)]


def far_row(j, panel):
    return pl.ds(pl.multiple_of(j * panel, panel), panel)


def middle_kernel(a_far, l_known, c_known, c_far, g_known, *refs):
    far, (ga_ref, gb_ref, col_ref, h_ref, ff) = refs[:-5], refs[-5:]
    count, known, order = g_known.shape
    panel = known // 2
    e = lax.axis_index("state") % 2
    i, j = e, 1 - e
    for k in range(2 * count):
        if len(far) > 1:
            for off, piece in enumerate(far, 2):
                ff[k, rows((e ^ off) - 2, panel), :] = piece[k]
            continue
        beside, folded = far[0][k, :panel], far[0][k, panel:]
        ff[k, rows(i, panel), rows(i, panel)] = unfold(folded)
        ff[k, rows(j, panel), rows(j, panel)] = jnp.zeros((panel, panel), F32)
        ff[k, rows(i, panel), rows(j, panel)] = beside
        ff[k, rows(j, panel), rows(i, panel)] = beside.T

    for k, out in enumerate((ga_ref, gb_ref)):
        c = c_far[k] + dot3(ff[k], a_far, NN)
        known_rows = (l_known.at[k, 0], l_known.at[k, 1])
        known_far = [x[:, known:] for x in known_rows]
        l_far = split(ff[count + k])
        column = jnp.concatenate([c_known[k], c[:, known:]], axis=0)
        share = dot3(column, l_far, NN)
        low = dot3(c[:, :known], known_rows, NN)
        out[:known, :known] = g_known[k, :, :known]
        out[:known, known:] = g_known[k, :, known:] + share[:known]
        out[known:, :known] = low[:, :known] + dot3(c[:, known:], known_far, NT)
        out[known:, known:] = low[:, known:] + share[known:]
        if len(far) == 1:
            col_ref[k] = jnp.where(j == 0, column[:, :panel], column[:, panel:])
            halves = a_far[0, far_row(j, panel), :], a_far[1, far_row(j, panel), :]
            head, tail = [x[:, :known] for x in halves], [x[:, known:] for x in halves]
            h = dot3(head, known_rows, NN)
            h_ref[k, :, :known] = h[:, :known] + dot3(tail, known_far, NT)
            h_ref[k, :, known:] = h[:, known:] + dot3(tail, l_far, NN)


def steps_of(info, count):
    a = base(lax.axis_index("state"), count)
    return [info[pl.ds(a + shift, 1), :] for shift in (0, 1, 8, 9)]


def late_kernel(first, info, a_far, ga, gb, col, h, *refs):
    far, (ga_ref, gb_ref, mean_ref) = refs[:-3], refs[-3:]
    count, panel, order = h.shape
    j = 1 - lax.axis_index("state") % 2
    for k, (gain, out) in enumerate(((ga, ga_ref), (gb, gb_ref))):
        if far:
            at = far_row(2 + j, panel)
            p_last, l_last = unfold(far[0][k]), unfold(far[0][count + k])
            corner = sum(a_far[half, far_row(j, panel), at].astype(F32) for half in range(2))
            wide = dot3(p_last, jnp.concatenate([h[k], corner], axis=1), NN)
            tall = dot3(jnp.concatenate([col[k], wide[:, order:]], axis=0), l_last, NN)
            out[at, :] = gain[at, :] + wide[:, :order]
            out[:, at] += tall[:order]
            out[at, at] += tall[order:]
    mean_a, mean_b, pred_a, pred_b = steps_of(info, count)
    mean_ref[...] = mean_a + matvec(ga_ref[...], mean_b + matvec(gb_ref[...], first[...] - pred_b) - pred_a)


def two_kernel(x, info, ga, gb, out_ref):
    mean_a, mean_b, pred_a, pred_b = steps_of(info, 2)
    out_ref[...] = mean_a + matvec(ga[...], mean_b + matvec(gb[...], x[...] - pred_b) - pred_a)


def pair_kernel(info, ga, gb, map_ref):
    order = ga.shape[1]
    mean_a, mean_b, pred_a, pred_b = steps_of(info, 2)
    map_ref[order:, :] = jnp.concatenate(
        [mean_a + matvec(ga[...], mean_b - pred_a), mean_b, pred_b, jnp.zeros((5, order), F32)], axis=0
    )
    map_ref[:order, :] = dot3(ga[...], gb[...], NN)


def block_kernel(late, early, m_ref, vec_ref):
    order = late.shape[1]
    shift = early[order : order + 1, :] + matvec(
        early[:order, :], late[order : order + 1, :] - early[order + 2 : order + 3, :]
    )
    vec_ref[...] = jnp.concatenate([late[order + 2 : order + 3, :], shift, jnp.zeros((6, order), F32)], axis=0)
    m_ref[...] = dot3(early[:order, :], late[:order, :], NN)


def pair_hop_kernel(x, late, early, out_ref):
    order = x.shape[1]
    y = late[order : order + 1, :] + matvec(late[:order, :], x[...] - late[order + 2 : order + 3, :])
    out_ref[...] = early[order : order + 1, :] + matvec(early[:order, :], y - early[order + 2 : order + 3, :])


def hop_kernel(x, m, vec, out_ref):
    out_ref[...] = vec[1:2, :] + matvec(m[...], x[...] - vec[0:1, :])


def last_kernel(devices, *refs):
    blocks = len(refs) - 7 - devices
    incoming, (m, vec, late, g3, early, g1), outs, cut = refs[:blocks], refs[blocks : blocks + 6], refs[blocks + 6 : -1], refs[-1]
    order, panel = m.shape[1], outs[0].shape[1]
    b, s = lax.axis_index("tm"), lax.axis_index("state")
    x = incoming[0][...]
    for k, ref in enumerate(incoming[1:], 1):
        x = jnp.where(lax.axis_size("tm") - 1 - b == k, ref[...], x)
    gap = x - vec[0:1, :]
    x3 = late[order + 1 : order + 2, :] + matvec(g3[...], gap)
    x2 = late[order : order + 1, :] + matvec(late[:order, :], gap)
    x0 = vec[1:2, :] + matvec(m[...], gap)
    x1 = early[order + 1 : order + 2, :] + matvec(g1[...], x2 - early[order + 2 : order + 3, :])
    full = jnp.concatenate([x0, x1, x2, x3], axis=0)
    for i in range(devices):
        cut[i] = full[:, i * panel : (i + 1) * panel]
    for off, out in enumerate(outs):
        out[...] = cut[s ^ off]


def out_kernel(*refs):
    given, out_ref = [refs[0], *refs[-2:0:-1]], refs[-1]
    off = lax.axis_index("state") ^ 1
    x = given[0][...]
    for k, ref in enumerate(given[1:], 1):
        x = jnp.where(off == k, ref[...], x)
    out_ref[...] = x


def params(mebibytes):
    return pltpu.CompilerParams(vmem_limit_bytes=mebibytes * 2**20)


def local(filtered_covariance, pred_prec, transition, filt_means, terminal_mean):
    steps, panel, order = filtered_covariance.shape
    devices, blocks = lax.axis_size("state"), lax.axis_size("tm")
    count = steps // 2

    def swap(x, off, block_off=0):
        pairs = [(i, i ^ (block_off * devices + off)) for i in range(blocks * devices)]
        return lax.ppermute(x, ("tm", "state"), pairs)

    def shape(*dims):
        return jax.ShapeDtypeStruct(dims, F32)

    def call(kernel, name, mebibytes, outs, in_specs, scratch, args, aliases={}):
        return pl.pallas_call(
            kernel,
            out_shape=outs,
            in_specs=in_specs,
            out_specs=[VMEM] * len(outs),
            scratch_shapes=scratch,
            input_output_aliases=aliases,
            compiler_params=params(mebibytes),
            name=name,
        )(*args)

    cov, prec, trans, means, terminal = (
        pltpu.with_memory_space_constraint(x, pltpu.HBM)
        for x in (filtered_covariance, pred_prec, transition, filt_means, terminal_mean[None])
    )
    semaphores = pltpu.SemaphoreType.DMA((8 * devices,))
    square = shape(order, order)

    far = [shape(*far_shape(devices, count, panel, order, off)) for off in range(2, devices)]
    *far, trans_half, first = call(
        functools.partial(pack_kernel, devices),
        "pack",
        6,
        far + [shape(panel // 2, order), shape(1, order)],
        [HBM] * 4,
        [pltpu.VMEM((1, order), F32), pltpu.VMEM((2, steps, panel, panel), F32), semaphores],
        (cov, prec, trans, terminal),
    )
    across = [swap(trans_half, off) for off in range(2, devices, 2)]
    far = [swap(x, off) for off, x in enumerate(far, 2)]
    moved = [y for x in across for y in (x, swap(x, 0, 1))]
    near = call(
        near_kernel,
        "near",
        4,
        [shape(count * panel, order)] * 2,
        [HBM] * 2 + [ANY],
        [semaphores],
        (cov, prec, first),
    )
    near = [swap(x, 1) for x in near]
    own, own_trans, own_means = call(
        own_kernel,
        "own",
        4,
        [shape(2 * count, panel, order), shape(panel, order), shape(steps, order)],
        [HBM] * 4 + [ANY],
        [semaphores],
        (cov, prec, trans, means, across[0]),
    )
    (joined,) = call(
        join_kernel,
        "join",
        4,
        [shape(devices // 2 - 1, panel, order)],
        [ANY] * (1 + len(moved)),
        [semaphores],
        (own_trans, *moved),
    )
    joined_near = swap(joined, 1)
    trans_near = swap(transition, 1)

    known = 2 * panel
    parts = call(
        early_kernel,
        "early",
        24,
        [
            shape(16, order),
            jax.ShapeDtypeStruct((2, order - known, order), BF16),
            jax.ShapeDtypeStruct((count, 2, known, order), BF16),
            shape(count, known, order - known),
            shape(count, order - known, order),
            shape(count, known, order),
        ],
        [ANY, VMEM] + [ANY] * 2 + [ANY] * 4,
        [
            pltpu.VMEM((count * known + 16, order), F32),
            pltpu.VMEM((order, order), F32),
            pltpu.VMEM((count, known, order), F32),
            semaphores,
        ],
        (own, own_means, own_trans, trans_near, joined, joined_near, *near),
    )
    info, a_far = parts[:2]
    last = far[1:] if trimmed(devices, panel) else []
    ga, gb, col, h = call(
        middle_kernel,
        "middle",
        24,
        [square, square, shape(count, order, panel), shape(count, panel, order)],
        [VMEM] * (5 + len(far) - len(last)),
        [pltpu.VMEM((2 * count, order - known, order - known), F32)],
        (*parts[1:], *far[: len(far) - len(last)]),
    )
    ga, gb, mean = call(
        late_kernel,
        "late",
        12,
        [square, square, shape(1, order)],
        [VMEM] * (7 + len(last)),
        [],
        (first, info, a_far, ga, gb, col, h, *last),
        {3: 0, 4: 1},
    )
    mean = swap(mean, 1)
    (early_map,) = call(pair_kernel, "pair", 12, [shape(order + 8, order)], [VMEM] * 3, [], (info, ga, gb))
    late_map = swap(lax.optimization_barrier((early_map, mean))[0], 1)
    (mean,) = call(two_kernel, "two", 6, [shape(1, order)], [VMEM] * 4, [], (mean, info, ga, gb))

    def hop(x, block):
        target = {i: i ^ 1 for i in range(blocks * devices)}
        for at, to in ((block, block - 1), (block - 1, block)):
            target[at * devices + 1] = to * devices + 1
            target.update({at * devices + i: at * devices + j for i, j in ((0, 2), (2, 3), (3, 0))})
        return lax.ppermute(x, ("tm", "state"), list(target.items()))

    incoming = [first, hop(mean, blocks - 1)]
    (x,) = call(pair_hop_kernel, "pair_hop", 4, [shape(1, order)], [VMEM] * 3, [], (incoming[-1], late_map, early_map))
    m, vec = call(block_kernel, "block", 12, [square, shape(8, order)], [VMEM] * 2, [], (late_map, early_map))
    for block in range(blocks - 2, 0, -1):
        if block < blocks - 2:
            (x,) = call(hop_kernel, "hop", 4, [shape(1, order)], [VMEM] * 3, [], (incoming[-1], m, vec))
        incoming.append(hop(x, block))
    g3 = swap(lax.optimization_barrier((gb, incoming[3]))[0], 1)

    given = list(call(
        functools.partial(last_kernel, devices),
        "last",
        8,
        [shape(steps, panel)] * devices,
        [VMEM] * (blocks + 6),
        [pltpu.VMEM((devices, steps, panel), F32)],
        (*incoming, m, vec, late_map, g3, early_map, gb),
    ))
    for off in range(devices - 1, 0, -1):
        given[off] = swap(given[off], off)
    given = [given[0], *given[:0:-1]]
    (out,) = call(out_kernel, "out", 4, [shape(steps, panel)], [VMEM] * devices, [], given)
    return out


def solution(mesh):
    return jax.shard_map(
        local,
        mesh=mesh,
        in_specs=(
            P("tm", "state", None),
            P("tm", "state", None),
            P("state", None),
            P("tm", None),
            P(),
        ),
        out_specs=P("tm", "state"),
        check_vma=False,
    )
```

```python
import functools

import jax
import jax.numpy as jnp
from jax import lax
from jax.experimental import pallas as pl
from jax.experimental.pallas import tpu as pltpu
from jax.sharding import PartitionSpec as P

F32, BF16 = jnp.float32, jnp.bfloat16
NN = (((1,), (0,)), ((), ()))
NT = (((1,), (1,)), ((), ()))
ANY = pl.BlockSpec(memory_space=pl.ANY)
HBM = pl.BlockSpec(memory_space=pltpu.HBM)
VMEM = pl.BlockSpec(memory_space=pltpu.VMEM)


def split(x):
    high = x.astype(BF16)
    return high, (x - high.astype(F32)).astype(BF16)


def dot3(a, b, dims):
    (ah, al), (bh, bl) = (split(x) if getattr(x, "dtype", None) == F32 else (x[0][...], x[1][...]) for x in (a, b))
    dot = functools.partial(lax.dot_general, dimension_numbers=dims, preferred_element_type=F32)
    return dot(ah, bh) + (dot(ah, bl) + dot(al, bh))


def matvec(matrix, row):
    order = matrix.shape[1]
    total = matrix[:, :128] * row[:, :128]
    for j in range(128, order, 128):
        total += matrix[:, j : j + 128] * row[:, j : j + 128]
    return jnp.sum(total.T, axis=0, keepdims=True)


def rows(i, panel):
    return pl.ds(pl.multiple_of(i * panel, panel), panel)


def starter(sems):
    copies = []

    def start(source, target):
        copy = pltpu.make_async_copy(source, target, sems.at[len(copies)])
        copy.start()
        copies.append(copy)

    return start, copies


def trimmed(devices, panel):
    return devices == 4 and panel == 128


def far_shape(devices, count, panel, order, off):
    if trimmed(devices, panel):
        return (2 * count, panel * 9 // 16 + (panel if off == 2 else 0), panel)
    return (2 * count, panel, order - 2 * panel)


def lanes(rows):
    return lax.broadcasted_iota(jnp.int32, (rows, 128), 1)


def fold(block):
    lower = ((112, 16), (96, 32), (80, 48))
    filled = [
        jnp.where(lanes(16) < width, pltpu.roll(block[row : row + 16], width, 1), block[width : width + 16])
        for row, width in lower
    ]
    rest = jnp.where(lanes(8) < 64, pltpu.roll(block[64:72], 64, 1), block[72:80])
    return jnp.concatenate([block[:16], *filled, rest], axis=0)


def unfold(folded):
    rest = folded[64:]
    moved = [pltpu.roll(folded[width : width + 16], 128 - width, 1) for width in (48, 32, 16)]
    upper = jnp.concatenate([folded[:64], pltpu.roll(rest, 64, 1), rest, *moved], axis=0)
    row = lax.broadcasted_iota(jnp.int32, (128, 128), 0)
    return jnp.where(row // 16 <= lanes(128) // 16, upper, upper.T)


def base(device, count):
    return (1 - device % 2) * count


def pack_kernel(devices, cov, prec, trans, terminal, *refs):
    far, (trans_half, first, vector, diagonal, sems) = refs[: devices - 2], refs[devices - 2 :]
    count, panel, order = cov.shape[0] // 2, *cov.shape[1:]
    b, s = lax.axis_index("tm"), lax.axis_index("state")
    start, copies = starter(sems)
    start(terminal, vector)
    start(trans.at[pl.ds(pl.multiple_of((b % 2) * (panel // 2), panel // 2), panel // 2), :], trans_half)
    trim = trimmed(devices, panel)
    if trim:
        for k, matrix in enumerate((cov, prec)):
            start(matrix.at[:, :, rows(s, panel)], diagonal.at[k])
    for off, piece in enumerate(far, 2):
        theirs = pl.ds(base(s ^ off, count), count)
        for k, matrix in enumerate((cov, prec)):
            target = piece.at[pl.ds(k * count, count)]
            if not trim:
                start(matrix.at[theirs, :, 2 * panel :], target)
            elif off == 2:
                start(matrix.at[theirs, :, rows(s ^ 1, panel)], target.at[:, :panel])
    copies[0].wait()
    first[...] = jnp.where(b == lax.axis_size("tm") - 1, vector[...], 0.0)
    for copy in copies[1:]:
        copy.wait()
    if trim:
        for off, piece in enumerate(far, 2):
            for k in range(2 * count):
                block = diagonal[k // count, base(s ^ off, count) + k % count]
                piece[k, piece.shape[1] - panel * 9 // 16 :, :] = fold(block)


def near_kernel(cov, prec, trans, after, near_cov, near_prec, near_trans, sems):
    count = cov.shape[0] // 2
    theirs = pl.ds((1 - lax.axis_index("state") % 2) * count, count)
    start, copies = starter(sems)
    start(cov.at[theirs], near_cov)
    start(prec.at[theirs], near_prec)
    start(trans, near_trans)
    for copy in copies:
        copy.wait()


def near_kernel(cov, prec, after, *refs):
    pieces, sems = refs[:-1], refs[-1]
    count, panel = cov.shape[0] // 2, cov.shape[1]
    first = base(lax.axis_index("state") ^ 1, count)
    start, copies = starter(sems)
    for k in range(2 * count):
        matrix = (cov, prec)[k // count]
        for piece, at, source, size in spans(pieces, k, panel):
            start(matrix.at[first + k % count, pl.ds(source, size), :], pieces[piece].at[pl.ds(at, size), :])
    for copy in copies:
        copy.wait()


def spans(pieces, k, panel):
    found, at = [], 0
    for i, piece in enumerate(pieces):
        low, high = max(at, k * panel), min(at + piece.shape[0], (k + 1) * panel)
        if low < high:
            found.append((i, low - at, low - k * panel, high - low))
        at += piece.shape[0]
    return found


def own_kernel(cov, prec, trans, means, after, own, own_trans, own_means, sems):
    count = cov.shape[0] // 2
    mine = pl.ds(base(lax.axis_index("state"), count), count)
    start, copies = starter(sems)
    start(cov.at[mine], own.at[pl.ds(0, count)])
    start(prec.at[mine], own.at[pl.ds(count, count)])
    start(trans, own_trans)
    start(means, own_means)
    for copy in copies:
        copy.wait()


def join_kernel(after, *refs):
    moved, (joined, sems) = refs[:-2], refs[-2:]
    half = moved[0].shape[0]
    b = lax.axis_index("tm")
    start, copies = starter(sems)
    for k, piece in enumerate(moved):
        at = (b % 2 if k % 2 == 0 else 1 - b % 2) * half
        start(piece, joined.at[k // 2, pl.ds(pl.multiple_of(at, half), half), :])
    for copy in copies:
        copy.wait()


def early_kernel(own, means, trans, trans_near, joined, joined_near, *refs):
    near, (info, a_far, l_known, c_known, c_far, g_known, pf, af, lf, sems) = refs[:-10], refs[-10:]
    panel, order = own.shape[1:]
    count, known = own.shape[0] // 2, 2 * panel
    steps = means.shape[0]
    e = lax.axis_index("state") % 2
    start, copies = starter(sems)
    for k in range(2 * count):
        target, top = (pf, k * known) if k < count else (lf.at[k - count], 0)
        start(own.at[k], target.at[pl.ds(pl.multiple_of(top + e * panel, panel), panel), :])
        for piece, at, row, size in spans(near, k, panel):
            to = pl.multiple_of(top + (1 - e) * panel + row, 8)
            start(near[piece].at[pl.ds(at, size), :], target.at[pl.ds(to, size), :])
    for j in range(order // known):
        mine, theirs = (joined.at[j - 1], joined_near.at[j - 1]) if j else (trans, trans_near)
        start(mine, af.at[rows(e ^ (2 * j), panel), :])
        start(theirs, af.at[rows(e ^ (2 * j) ^ 1, panel), :])
    pf[count * known :, :] = jnp.concatenate([means[...], jnp.zeros((16 - steps, order), F32)], axis=0)
    for copy in copies:
        copy.wait()
    product = dot3(pf[...], af[...], NT)
    info[:8] = pf[count * known : count * known + 8, :]
    info[8:] = product[count * known : count * known + 8]
    for half, x in enumerate(split(af[:, known:].T)):
        a_far[half] = x
    across = jnp.concatenate([pf[k * known : (k + 1) * known, known:].T for k in range(count)], axis=0)
    rest = dot3(across, af[:, :known], NT)
    for k in range(count):
        part = product[k * known : (k + 1) * known]
        for half, x in enumerate(split(lf[k])):
            l_known[k, half] = x
        partial = dot3(part[:, :known], lf[k], NN)
        g_known[k, :, :known] = partial[:, :known] + dot3(part[:, known:], lf[k, :, known:], NT)
        g_known[k, :, known:] = partial[:, known:]
        c_known[k] = part[:, known:]
        c_far[k] = rest[k * (order - known) : (k + 1) * (order - known)]


def steps_of(info, count):
    a = base(lax.axis_index("state"), count)
    return [info[pl.ds(a + shift, 1), :] for shift in (0, 1, 8, 9)]


def far_row(j, panel):
    return pl.ds(pl.multiple_of(j * panel, panel), panel)


def middle_kernel(a_far, l_known, c_known, c_far, g_known, *refs):
    far, (ga_ref, gb_ref, col_ref, h_ref, ff) = refs[:-5], refs[-5:]
    count, known, order = g_known.shape
    panel = known // 2
    e = lax.axis_index("state") % 2
    i, j = e, 1 - e
    for k in range(2 * count):
        if len(far) > 1:
            for off, piece in enumerate(far, 2):
                ff[k, rows((e ^ off) - 2, panel), :] = piece[k]
            continue
        beside, folded = far[0][k, :panel], far[0][k, panel:]
        ff[k, rows(i, panel), rows(i, panel)] = unfold(folded)
        ff[k, rows(j, panel), rows(j, panel)] = jnp.zeros((panel, panel), F32)
        ff[k, rows(i, panel), rows(j, panel)] = beside
        ff[k, rows(j, panel), rows(i, panel)] = beside.T

    for k, out in enumerate((ga_ref, gb_ref)):
        c = c_far[k] + dot3(ff[k], a_far, NN)
        known_rows = (l_known.at[k, 0], l_known.at[k, 1])
        known_far = [x[:, known:] for x in known_rows]
        l_far = split(ff[count + k])
        column = jnp.concatenate([c_known[k], c[:, known:]], axis=0)
        share = dot3(column, l_far, NN)
        low = dot3(c[:, :known], known_rows, NN)
        out[:known, :known] = g_known[k, :, :known]
        out[:known, known:] = g_known[k, :, known:] + share[:known]
        out[known:, :known] = low[:, :known] + dot3(c[:, known:], known_far, NT)
        out[known:, known:] = low[:, known:] + share[known:]
        if len(far) == 1:
            col_ref[k] = jnp.where(j == 0, column[:, :panel], column[:, panel:])
            halves = a_far[0, far_row(j, panel), :], a_far[1, far_row(j, panel), :]
            head, tail = [x[:, :known] for x in halves], [x[:, known:] for x in halves]
            h = dot3(head, known_rows, NN)
            h_ref[k, :, :known] = h[:, :known] + dot3(tail, known_far, NT)
            h_ref[k, :, known:] = h[:, known:] + dot3(tail, l_far, NN)


def steps_of(info, count):
    a = base(lax.axis_index("state"), count)
    return [info[pl.ds(a + shift, 1), :] for shift in (0, 1, 8, 9)]


def late_kernel(first, info, a_far, ga, gb, col, h, *refs):
    far, (ga_ref, gb_ref, mean_ref) = refs[:-3], refs[-3:]
    count, panel, order = h.shape
    j = 1 - lax.axis_index("state") % 2
    mean_a, mean_b, pred_a, pred_b = steps_of(info, count)
    row = first[...]
    for k, gain, out, mean, pred in ((1, gb, gb_ref, mean_b, pred_b), (0, ga, ga_ref, mean_a, pred_a)):
        if far:
            at = far_row(2 + j, panel)
            p_last, l_last = unfold(far[0][k]), unfold(far[0][count + k])
            corner = [a_far[half, far_row(j, panel), at] for half in range(2)]
            out[at, :] = gain[at, :] + dot3(p_last, h[k], NN)
            out[:, at] += dot3(col[k], l_last, NN)
            out[at, at] += dot3(dot3(p_last, corner, NN), l_last, NN)
        row = mean + matvec(out[...], row - pred)
    mean_ref[...] = row


def two_kernel(x, info, ga, gb, out_ref):
    mean_a, mean_b, pred_a, pred_b = steps_of(info, 2)
    out_ref[...] = mean_a + matvec(ga[...], mean_b + matvec(gb[...], x[...] - pred_b) - pred_a)


def pair_kernel(info, ga, gb, map_ref):
    order = ga.shape[1]
    mean_a, mean_b, pred_a, pred_b = steps_of(info, 2)
    map_ref[order:, :] = jnp.concatenate(
        [mean_a + matvec(ga[...], mean_b - pred_a), mean_b, pred_b, jnp.zeros((5, order), F32)], axis=0
    )
    map_ref[:order, :] = dot3(ga[...], gb[...], NN)


def block_kernel(late, early, m_ref, vec_ref):
    order = late.shape[1]
    shift = early[order : order + 1, :] + matvec(
        early[:order, :], late[order : order + 1, :] - early[order + 2 : order + 3, :]
    )
    vec_ref[...] = jnp.concatenate([late[order + 2 : order + 3, :], shift, jnp.zeros((6, order), F32)], axis=0)
    m_ref[...] = dot3(early[:order, :], late[:order, :], NN)


def pair_hop_kernel(x, late, early, out_ref):
    order = x.shape[1]
    y = late[order : order + 1, :] + matvec(late[:order, :], x[...] - late[order + 2 : order + 3, :])
    out_ref[...] = early[order : order + 1, :] + matvec(early[:order, :], y - early[order + 2 : order + 3, :])


def hop_kernel(x, m, vec, out_ref):
    out_ref[...] = vec[1:2, :] + matvec(m[...], x[...] - vec[0:1, :])


def last_kernel(devices, *refs):
    blocks = len(refs) - 7 - devices
    incoming, (m, vec, late, g3, early, g1), outs, cut = refs[:blocks], refs[blocks : blocks + 6], refs[blocks + 6 : -1], refs[-1]
    order, panel = m.shape[1], outs[0].shape[1]
    b, s = lax.axis_index("tm"), lax.axis_index("state")
    x = incoming[0][...]
    for k, ref in enumerate(incoming[1:], 1):
        x = jnp.where(lax.axis_size("tm") - 1 - b == k, ref[...], x)
    gap = x - vec[0:1, :]
    x3 = late[order + 1 : order + 2, :] + matvec(g3[...], gap)
    x2 = late[order : order + 1, :] + matvec(late[:order, :], gap)
    x0 = vec[1:2, :] + matvec(m[...], gap)
    x1 = early[order + 1 : order + 2, :] + matvec(g1[...], x2 - early[order + 2 : order + 3, :])
    full = jnp.concatenate([x0, x1, x2, x3], axis=0)
    for i in range(devices):
        cut[i] = full[:, i * panel : (i + 1) * panel]
    for off, out in enumerate(outs):
        out[...] = cut[s ^ off]


def out_kernel(*refs):
    given, out_ref = [refs[0], refs[-2], *refs[1:-2]], refs[-1]
    off = lax.axis_index("state") ^ 1
    x = given[0][...]
    for k, ref in enumerate(given[1:], 1):
        x = jnp.where(off == k, ref[...], x)
    out_ref[...] = x


def params(mebibytes):
    return pltpu.CompilerParams(vmem_limit_bytes=mebibytes * 2**20)


def local(filtered_covariance, pred_prec, transition, filt_means, terminal_mean):
    steps, panel, order = filtered_covariance.shape
    devices, blocks = lax.axis_size("state"), lax.axis_size("tm")
    count = steps // 2

    def swap(x, off, block_off=0):
        pairs = [(i, i ^ (block_off * devices + off)) for i in range(blocks * devices)]
        return lax.ppermute(x, ("tm", "state"), pairs)

    def shape(*dims):
        return jax.ShapeDtypeStruct(dims, F32)

    def call(kernel, name, mebibytes, outs, in_specs, scratch, args, aliases={}):
        return pl.pallas_call(
            kernel,
            out_shape=outs,
            in_specs=in_specs,
            out_specs=[VMEM] * len(outs),
            scratch_shapes=scratch,
            input_output_aliases=aliases,
            compiler_params=params(mebibytes),
            name=name,
        )(*args)

    cov, prec, trans, means, terminal = (
        pltpu.with_memory_space_constraint(x, pltpu.HBM)
        for x in (filtered_covariance, pred_prec, transition, filt_means, terminal_mean[None])
    )
    semaphores = pltpu.SemaphoreType.DMA((8 * devices,))
    square = shape(order, order)

    far = [shape(*far_shape(devices, count, panel, order, off)) for off in range(2, devices)]
    *far, trans_half, first = call(
        functools.partial(pack_kernel, devices),
        "pack",
        6,
        far + [shape(panel // 2, order), shape(1, order)],
        [HBM] * 4,
        [pltpu.VMEM((1, order), F32), pltpu.VMEM((2, steps, panel, panel), F32), semaphores],
        (cov, prec, trans, terminal),
    )
    across = [swap(trans_half, off) for off in range(2, devices, 2)]
    far = [swap(x, off) for off, x in enumerate(far, 2)]
    moved = [y for x in across for y in (x, swap(x, 0, 1))]
    near = call(
        near_kernel,
        "near",
        4,
        [shape(count * panel, order)] * 2,
        [HBM] * 2 + [ANY],
        [semaphores],
        (cov, prec, first),
    )
    near = [swap(x, 1) for x in near]
    own, own_trans, own_means = call(
        own_kernel,
        "own",
        4,
        [shape(2 * count, panel, order), shape(panel, order), shape(steps, order)],
        [HBM] * 4 + [ANY],
        [semaphores],
        (cov, prec, trans, means, across[0]),
    )
    (joined,) = call(
        join_kernel,
        "join",
        4,
        [shape(devices // 2 - 1, panel, order)],
        [ANY] * (1 + len(moved)),
        [semaphores],
        (own_trans, *moved),
    )
    joined_near = swap(joined, 1)
    trans_near = swap(transition, 1)

    known = 2 * panel
    parts = call(
        early_kernel,
        "early",
        24,
        [
            shape(16, order),
            jax.ShapeDtypeStruct((2, order - known, order), BF16),
            jax.ShapeDtypeStruct((count, 2, known, order), BF16),
            shape(count, known, order - known),
            shape(count, order - known, order),
            shape(count, known, order),
        ],
        [ANY, VMEM] + [ANY] * 2 + [ANY] * 4,
        [
            pltpu.VMEM((count * known + 16, order), F32),
            pltpu.VMEM((order, order), F32),
            pltpu.VMEM((count, known, order), F32),
            semaphores,
        ],
        (own, own_means, own_trans, trans_near, joined, joined_near, *near),
    )
    info, a_far = parts[:2]
    last = far[1:] if trimmed(devices, panel) else []
    ga, gb, col, h = call(
        middle_kernel,
        "middle",
        24,
        [square, square, shape(count, order, panel), shape(count, panel, order)],
        [VMEM] * (5 + len(far) - len(last)),
        [pltpu.VMEM((2 * count, order - known, order - known), F32)],
        (*parts[1:], *far[: len(far) - len(last)]),
    )
    ga, gb, mean = call(
        late_kernel,
        "late",
        12,
        [square, square, shape(1, order)],
        [VMEM] * (7 + len(last)),
        [],
        (first, info, a_far, ga, gb, col, h, *last),
        {3: 0, 4: 1},
    )
    mean = swap(mean, 1)
    (early_map,) = call(pair_kernel, "pair", 12, [shape(order + 8, order)], [VMEM] * 3, [], (info, ga, gb))
    late_map = swap(lax.optimization_barrier((early_map, mean))[0], 1)
    (mean,) = call(two_kernel, "two", 6, [shape(1, order)], [VMEM] * 4, [], (mean, info, ga, gb))

    def hop(x, block):
        target = {i: i ^ 1 for i in range(blocks * devices)}
        for at, to in ((block, block - 1), (block - 1, block)):
            target[at * devices + 1] = to * devices + 1
            target.update({at * devices + i: at * devices + j for i, j in ((0, 2), (2, 3), (3, 0))})
        return lax.ppermute(x, ("tm", "state"), list(target.items()))

    incoming = [first, hop(mean, blocks - 1)]
    (x,) = call(pair_hop_kernel, "pair_hop", 4, [shape(1, order)], [VMEM] * 3, [], (incoming[-1], late_map, early_map))
    m, vec = call(block_kernel, "block", 12, [square, shape(8, order)], [VMEM] * 2, [], (late_map, early_map))
    for block in range(blocks - 2, 0, -1):
        if block < blocks - 2:
            (x,) = call(hop_kernel, "hop", 4, [shape(1, order)], [VMEM] * 3, [], (incoming[-1], m, vec))
        incoming.append(hop(x, block))
    g3 = swap(lax.optimization_barrier((gb, incoming[3]))[0], 1)

    given = list(call(
        functools.partial(last_kernel, devices),
        "last",
        8,
        [shape(steps, panel)] * devices,
        [VMEM] * (blocks + 6),
        [pltpu.VMEM((devices, steps, panel), F32)],
        (*incoming, m, vec, late_map, g3, early_map, gb),
    ))
    order_of = (*range(2, devices), 1)
    ring = {1: 2, 2: 0, 0: 3, 3: 1}
    for off in order_of:
        if off == 3:
            pairs = [(i, ring.get(i, i ^ 3)) for i in range(devices)]
            given[off] = lax.ppermute(given[off], "state", pairs)
        else:
            given[off] = swap(given[off], off)
    given = [given[0], *(given[off] for off in order_of)]
    (out,) = call(out_kernel, "out", 4, [shape(steps, panel)], [VMEM] * devices, [], given)
    return out


def solution(mesh):
    return jax.shard_map(
        local,
        mesh=mesh,
        in_specs=(
            P("tm", "state", None),
            P("tm", "state", None),
            P("state", None),
            P("tm", None),
            P(),
        ),
        out_specs=P("tm", "state"),
        check_vma=False,
    )
```

```python
import functools

import jax
import jax.numpy as jnp
from jax import lax
from jax.experimental import pallas as pl
from jax.experimental.pallas import tpu as pltpu
from jax.sharding import PartitionSpec as P

F32, BF16 = jnp.float32, jnp.bfloat16
NN = (((1,), (0,)), ((), ()))
NT = (((1,), (1,)), ((), ()))
ANY = pl.BlockSpec(memory_space=pl.ANY)
HBM = pl.BlockSpec(memory_space=pltpu.HBM)
VMEM = pl.BlockSpec(memory_space=pltpu.VMEM)


def split(x):
    high = x.astype(BF16)
    return high, (x - high.astype(F32)).astype(BF16)


def dot3(a, b, dims):
    (ah, al), (bh, bl) = (split(x) if getattr(x, "dtype", None) == F32 else (x[0][...], x[1][...]) for x in (a, b))
    dot = functools.partial(lax.dot_general, dimension_numbers=dims, preferred_element_type=F32)
    return dot(ah, bh) + (dot(ah, bl) + dot(al, bh))


def matvec(matrix, row):
    order = matrix.shape[1]
    total = matrix[:, :128] * row[:, :128]
    for j in range(128, order, 128):
        total += matrix[:, j : j + 128] * row[:, j : j + 128]
    return jnp.sum(total.T, axis=0, keepdims=True)


def rows(i, panel):
    return pl.ds(pl.multiple_of(i * panel, panel), panel)


def starter(sems):
    copies = []

    def start(source, target):
        copy = pltpu.make_async_copy(source, target, sems.at[len(copies)])
        copy.start()
        copies.append(copy)

    return start, copies


def trimmed(devices, panel):
    return devices == 4 and panel == 128


def far_shape(devices, count, panel, order, off):
    if trimmed(devices, panel):
        return (2 * count, panel * 9 // 16 + (panel if off == 2 else 0), panel)
    return (2 * count, panel, order - 2 * panel)


def lanes(rows):
    return lax.broadcasted_iota(jnp.int32, (rows, 128), 1)


def fold(block):
    lower = ((112, 16), (96, 32), (80, 48))
    filled = [
        jnp.where(lanes(16) < width, pltpu.roll(block[row : row + 16], width, 1), block[width : width + 16])
        for row, width in lower
    ]
    rest = jnp.where(lanes(8) < 64, pltpu.roll(block[64:72], 64, 1), block[72:80])
    return jnp.concatenate([block[:16], *filled, rest], axis=0)


def unfold(folded):
    rest = folded[64:]
    moved = [pltpu.roll(folded[width : width + 16], 128 - width, 1) for width in (48, 32, 16)]
    upper = jnp.concatenate([folded[:64], pltpu.roll(rest, 64, 1), rest, *moved], axis=0)
    row = lax.broadcasted_iota(jnp.int32, (128, 128), 0)
    return jnp.where(row // 16 <= lanes(128) // 16, upper, upper.T)


def base(device, count):
    return (1 - device % 2) * count


def pack_kernel(devices, cov, prec, trans, terminal, *refs):
    far, (trans_half, first, vector, diagonal, sems) = refs[: devices - 2], refs[devices - 2 :]
    count, panel, order = cov.shape[0] // 2, *cov.shape[1:]
    b, s = lax.axis_index("tm"), lax.axis_index("state")
    start, copies = starter(sems)
    start(terminal, vector)
    start(trans.at[pl.ds(pl.multiple_of((b % 2) * (panel // 2), panel // 2), panel // 2), :], trans_half)
    trim = trimmed(devices, panel)
    if trim:
        for k, matrix in enumerate((cov, prec)):
            start(matrix.at[:, :, rows(s, panel)], diagonal.at[k])
    for off, piece in enumerate(far, 2):
        theirs = pl.ds(base(s ^ off, count), count)
        for k, matrix in enumerate((cov, prec)):
            target = piece.at[pl.ds(k * count, count)]
            if not trim:
                start(matrix.at[theirs, :, 2 * panel :], target)
            elif off == 2:
                start(matrix.at[theirs, :, rows(s ^ 1, panel)], target.at[:, :panel])
    copies[0].wait()
    first[...] = jnp.where(b == lax.axis_size("tm") - 1, vector[...], 0.0)
    for copy in copies[1:]:
        copy.wait()
    if trim:
        for off, piece in enumerate(far, 2):
            for k in range(2 * count):
                block = diagonal[k // count, base(s ^ off, count) + k % count]
                piece[k, piece.shape[1] - panel * 9 // 16 :, :] = fold(block)


def near_kernel(cov, prec, trans, after, near_cov, near_prec, near_trans, sems):
    count = cov.shape[0] // 2
    theirs = pl.ds((1 - lax.axis_index("state") % 2) * count, count)
    start, copies = starter(sems)
    start(cov.at[theirs], near_cov)
    start(prec.at[theirs], near_prec)
    start(trans, near_trans)
    for copy in copies:
        copy.wait()


def near_kernel(cov, prec, after, *refs):
    pieces, sems = refs[:-1], refs[-1]
    count, panel = cov.shape[0] // 2, cov.shape[1]
    first = base(lax.axis_index("state") ^ 1, count)
    start, copies = starter(sems)
    for k in range(2 * count):
        matrix = (cov, prec)[k // count]
        for piece, at, source, size in spans(pieces, k, panel):
            start(matrix.at[first + k % count, pl.ds(source, size), :], pieces[piece].at[pl.ds(at, size), :])
    for copy in copies:
        copy.wait()


def spans(pieces, k, panel):
    found, at = [], 0
    for i, piece in enumerate(pieces):
        low, high = max(at, k * panel), min(at + piece.shape[0], (k + 1) * panel)
        if low < high:
            found.append((i, low - at, low - k * panel, high - low))
        at += piece.shape[0]
    return found


def own_kernel(cov, prec, trans, means, after, own, own_trans, own_means, sems):
    count = cov.shape[0] // 2
    mine = pl.ds(base(lax.axis_index("state"), count), count)
    start, copies = starter(sems)
    start(cov.at[mine], own.at[pl.ds(0, count)])
    start(prec.at[mine], own.at[pl.ds(count, count)])
    start(trans, own_trans)
    start(means, own_means)
    for copy in copies:
        copy.wait()


def join_kernel(after, *refs):
    moved, (joined, sems) = refs[:-2], refs[-2:]
    half = moved[0].shape[0]
    b = lax.axis_index("tm")
    start, copies = starter(sems)
    for k, piece in enumerate(moved):
        at = (b % 2 if k % 2 == 0 else 1 - b % 2) * half
        start(piece, joined.at[k // 2, pl.ds(pl.multiple_of(at, half), half), :])
    for copy in copies:
        copy.wait()


def early_kernel(own, means, trans, trans_near, joined, joined_near, *refs):
    near, (info, a_far, l_known, c_known, c_far, g_known, pf, af, lf, sems) = refs[:-10], refs[-10:]
    panel, order = own.shape[1:]
    count, known = own.shape[0] // 2, 2 * panel
    steps = means.shape[0]
    e = lax.axis_index("state") % 2
    start, copies = starter(sems)
    for k in range(2 * count):
        target, top = (pf, k * known) if k < count else (lf.at[k - count], 0)
        start(own.at[k], target.at[pl.ds(pl.multiple_of(top + e * panel, panel), panel), :])
        for piece, at, row, size in spans(near, k, panel):
            to = pl.multiple_of(top + (1 - e) * panel + row, 8)
            start(near[piece].at[pl.ds(at, size), :], target.at[pl.ds(to, size), :])
    for j in range(order // known):
        mine, theirs = (joined.at[j - 1], joined_near.at[j - 1]) if j else (trans, trans_near)
        start(mine, af.at[rows(e ^ (2 * j), panel), :])
        start(theirs, af.at[rows(e ^ (2 * j) ^ 1, panel), :])
    pf[count * known :, :] = jnp.concatenate([means[...], jnp.zeros((16 - steps, order), F32)], axis=0)
    for copy in copies:
        copy.wait()
    product = dot3(pf[...], af[...], NT)
    info[:8] = pf[count * known : count * known + 8, :]
    info[8:] = product[count * known : count * known + 8]
    for half, x in enumerate(split(af[:, known:].T)):
        a_far[half] = x
    across = jnp.concatenate([pf[k * known : (k + 1) * known, known:].T for k in range(count)], axis=0)
    rest = dot3(across, af[:, :known], NT)
    for k in range(count):
        part = product[k * known : (k + 1) * known]
        for half, x in enumerate(split(lf[k])):
            l_known[k, half] = x
        partial = dot3(part[:, :known], lf[k], NN)
        g_known[k, :, :known] = partial[:, :known] + dot3(part[:, known:], lf[k, :, known:], NT)
        g_known[k, :, known:] = partial[:, known:]
        c_known[k] = part[:, known:]
        c_far[k] = rest[k * (order - known) : (k + 1) * (order - known)]


def steps_of(info, count):
    a = base(lax.axis_index("state"), count)
    return [info[pl.ds(a + shift, 1), :] for shift in (0, 1, 8, 9)]


def far_row(j, panel):
    return pl.ds(pl.multiple_of(j * panel, panel), panel)


def middle_kernel(a_far, l_known, c_known, c_far, g_known, *refs):
    far, (ga_ref, gb_ref, col_ref, h_ref, ff) = refs[:-5], refs[-5:]
    count, known, order = g_known.shape
    panel = known // 2
    e = lax.axis_index("state") % 2
    i, j = e, 1 - e
    for k in range(2 * count):
        if len(far) > 1:
            for off, piece in enumerate(far, 2):
                ff[k, rows((e ^ off) - 2, panel), :] = piece[k]
            continue
        beside, folded = far[0][k, :panel], far[0][k, panel:]
        ff[k, rows(i, panel), rows(i, panel)] = unfold(folded)
        ff[k, rows(j, panel), rows(j, panel)] = jnp.zeros((panel, panel), F32)
        ff[k, rows(i, panel), rows(j, panel)] = beside
        ff[k, rows(j, panel), rows(i, panel)] = beside.T

    for k, out in enumerate((ga_ref, gb_ref)):
        c = c_far[k] + dot3(ff[k], a_far, NN)
        known_rows = (l_known.at[k, 0], l_known.at[k, 1])
        known_far = [x[:, known:] for x in known_rows]
        l_far = split(ff[count + k])
        column = jnp.concatenate([c_known[k], c[:, known:]], axis=0)
        share = dot3(column, l_far, NN)
        low = dot3(c[:, :known], known_rows, NN)
        out[:known, :known] = g_known[k, :, :known]
        out[:known, known:] = g_known[k, :, known:] + share[:known]
        out[known:, :known] = low[:, :known] + dot3(c[:, known:], known_far, NT)
        out[known:, known:] = low[:, known:] + share[known:]
        if len(far) == 1:
            col_ref[k] = jnp.where(j == 0, column[:, :panel], column[:, panel:])
            halves = a_far[0, far_row(j, panel), :], a_far[1, far_row(j, panel), :]
            head, tail = [x[:, :known] for x in halves], [x[:, known:] for x in halves]
            h = dot3(head, known_rows, NN)
            h_ref[k, :, :known] = h[:, :known] + dot3(tail, known_far, NT)
            h_ref[k, :, known:] = h[:, known:] + dot3(tail, l_far, NN)


def steps_of(info, count):
    a = base(lax.axis_index("state"), count)
    return [info[pl.ds(a + shift, 1), :] for shift in (0, 1, 8, 9)]


def late_kernel(first, info, a_far, ga, gb, col, h, *refs):
    far, (ga_ref, gb_ref, mean_ref) = refs[:-3], refs[-3:]
    count, panel, order = h.shape
    j = 1 - lax.axis_index("state") % 2
    mean_a, mean_b, pred_a, pred_b = steps_of(info, count)
    row = first[...]
    for k, gain, out, mean, pred in ((1, gb, gb_ref, mean_b, pred_b), (0, ga, ga_ref, mean_a, pred_a)):
        if far:
            at = far_row(2 + j, panel)
            p_last, l_last = unfold(far[0][k]), unfold(far[0][count + k])
            corner = [a_far[half, far_row(j, panel), at] for half in range(2)]
            out[at, :] = gain[at, :] + dot3(p_last, h[k], NN)
            out[:, at] += dot3(col[k], l_last, NN)
            out[at, at] += dot3(dot3(p_last, corner, NN), l_last, NN)
        row = mean + matvec(out[...], row - pred)
    mean_ref[...] = row


def two_kernel(x, info, ga, gb, out_ref):
    mean_a, mean_b, pred_a, pred_b = steps_of(info, 2)
    out_ref[...] = mean_a + matvec(ga[...], mean_b + matvec(gb[...], x[...] - pred_b) - pred_a)


def pair_kernel(info, ga, gb, map_ref):
    order = ga.shape[1]
    left = split(ga[...])
    for at in range(0, order, order // 2):
        columns = slice(at, at + order // 2)
        map_ref[:order, columns] = dot3(left, gb[:, columns], NN)
    mean_a, mean_b, pred_a, pred_b = steps_of(info, 2)
    map_ref[order:, :] = jnp.concatenate(
        [mean_a + matvec(ga[...], mean_b - pred_a), mean_b, pred_b, jnp.zeros((5, order), F32)], axis=0
    )


def block_kernel(late, early, m_ref, vec_ref):
    order = late.shape[1]
    shift = early[order : order + 1, :] + matvec(
        early[:order, :], late[order : order + 1, :] - early[order + 2 : order + 3, :]
    )
    vec_ref[...] = jnp.concatenate([late[order + 2 : order + 3, :], shift, jnp.zeros((6, order), F32)], axis=0)
    m_ref[...] = dot3(early[:order, :], late[:order, :], NN)


def pair_hop_kernel(x, late, early, out_ref):
    order = x.shape[1]
    y = late[order : order + 1, :] + matvec(late[:order, :], x[...] - late[order + 2 : order + 3, :])
    out_ref[...] = early[order : order + 1, :] + matvec(early[:order, :], y - early[order + 2 : order + 3, :])


def hop_kernel(x, m, vec, out_ref):
    out_ref[...] = vec[1:2, :] + matvec(m[...], x[...] - vec[0:1, :])


def last_kernel(devices, *refs):
    blocks = len(refs) - 7 - devices
    incoming, (m, vec, late, g3, early, g1), outs, cut = refs[:blocks], refs[blocks : blocks + 6], refs[blocks + 6 : -1], refs[-1]
    order, panel = m.shape[1], outs[0].shape[1]
    b, s = lax.axis_index("tm"), lax.axis_index("state")
    x = incoming[0][...]
    for k, ref in enumerate(incoming[1:], 1):
        x = jnp.where(lax.axis_size("tm") - 1 - b == k, ref[...], x)
    gap = x - vec[0:1, :]
    x3 = late[order + 1 : order + 2, :] + matvec(g3[...], gap)
    x2 = late[order : order + 1, :] + matvec(late[:order, :], gap)
    x0 = vec[1:2, :] + matvec(m[...], gap)
    x1 = early[order + 1 : order + 2, :] + matvec(g1[...], x2 - early[order + 2 : order + 3, :])
    full = jnp.concatenate([x0, x1, x2, x3], axis=0)
    for i in range(devices):
        cut[i] = full[:, i * panel : (i + 1) * panel]
    for off, out in enumerate(outs):
        out[...] = cut[s ^ off]


def out_kernel(*refs):
    given, out_ref = [refs[0], refs[-2], *refs[1:-2]], refs[-1]
    off = lax.axis_index("state") ^ 1
    x = given[0][...]
    for k, ref in enumerate(given[1:], 1):
        x = jnp.where(off == k, ref[...], x)
    out_ref[...] = x


def params(mebibytes):
    return pltpu.CompilerParams(vmem_limit_bytes=mebibytes * 2**20)


def local(filtered_covariance, pred_prec, transition, filt_means, terminal_mean):
    steps, panel, order = filtered_covariance.shape
    devices, blocks = lax.axis_size("state"), lax.axis_size("tm")
    count = steps // 2

    def swap(x, off, block_off=0):
        pairs = [(i, i ^ (block_off * devices + off)) for i in range(blocks * devices)]
        return lax.ppermute(x, ("tm", "state"), pairs)

    def shape(*dims):
        return jax.ShapeDtypeStruct(dims, F32)

    def call(kernel, name, mebibytes, outs, in_specs, scratch, args, aliases={}):
        return pl.pallas_call(
            kernel,
            out_shape=outs,
            in_specs=in_specs,
            out_specs=[VMEM] * len(outs),
            scratch_shapes=scratch,
            input_output_aliases=aliases,
            compiler_params=params(mebibytes),
            name=name,
        )(*args)

    cov, prec, trans, means, terminal = (
        pltpu.with_memory_space_constraint(x, pltpu.HBM)
        for x in (filtered_covariance, pred_prec, transition, filt_means, terminal_mean[None])
    )
    semaphores = pltpu.SemaphoreType.DMA((8 * devices,))
    square = shape(order, order)

    far = [shape(*far_shape(devices, count, panel, order, off)) for off in range(2, devices)]
    *far, trans_half, first = call(
        functools.partial(pack_kernel, devices),
        "pack",
        6,
        far + [shape(panel // 2, order), shape(1, order)],
        [HBM] * 4,
        [pltpu.VMEM((1, order), F32), pltpu.VMEM((2, steps, panel, panel), F32), semaphores],
        (cov, prec, trans, terminal),
    )
    across = [swap(trans_half, off) for off in range(2, devices, 2)]
    far = [swap(x, off) for off, x in enumerate(far, 2)]
    moved = [y for x in across for y in (x, swap(x, 0, 1))]
    near = call(
        near_kernel,
        "near",
        4,
        [shape(count * panel, order)] * 2,
        [HBM] * 2 + [ANY],
        [semaphores],
        (cov, prec, first),
    )
    near = [swap(x, 1) for x in near]
    own, own_trans, own_means = call(
        own_kernel,
        "own",
        4,
        [shape(2 * count, panel, order), shape(panel, order), shape(steps, order)],
        [HBM] * 4 + [ANY],
        [semaphores],
        (cov, prec, trans, means, across[0]),
    )
    (joined,) = call(
        join_kernel,
        "join",
        4,
        [shape(devices // 2 - 1, panel, order)],
        [ANY] * (1 + len(moved)),
        [semaphores],
        (own_trans, *moved),
    )
    joined_near = swap(joined, 1)
    trans_near = swap(transition, 1)

    known = 2 * panel
    parts = call(
        early_kernel,
        "early",
        24,
        [
            shape(16, order),
            jax.ShapeDtypeStruct((2, order - known, order), BF16),
            jax.ShapeDtypeStruct((count, 2, known, order), BF16),
            shape(count, known, order - known),
            shape(count, order - known, order),
            shape(count, known, order),
        ],
        [ANY, VMEM] + [ANY] * 2 + [ANY] * 4,
        [
            pltpu.VMEM((count * known + 16, order), F32),
            pltpu.VMEM((order, order), F32),
            pltpu.VMEM((count, known, order), F32),
            semaphores,
        ],
        (own, own_means, own_trans, trans_near, joined, joined_near, *near),
    )
    info, a_far = parts[:2]
    last = far[1:] if trimmed(devices, panel) else []
    ga, gb, col, h = call(
        middle_kernel,
        "middle",
        24,
        [square, square, shape(count, order, panel), shape(count, panel, order)],
        [VMEM] * (5 + len(far) - len(last)),
        [pltpu.VMEM((2 * count, order - known, order - known), F32)],
        (*parts[1:], *far[: len(far) - len(last)]),
    )
    ga, gb, mean = call(
        late_kernel,
        "late",
        12,
        [square, square, shape(1, order)],
        [VMEM] * (7 + len(last)),
        [],
        (first, info, a_far, ga, gb, col, h, *last),
        {3: 0, 4: 1},
    )
    mean = swap(mean, 1)
    (early_map,) = call(pair_kernel, "pair", 12, [shape(order + 8, order)], [VMEM] * 3, [], (info, ga, gb))
    late_map = swap(lax.optimization_barrier((early_map, mean))[0], 1)
    (mean,) = call(two_kernel, "two", 6, [shape(1, order)], [VMEM] * 4, [], (mean, info, ga, gb))

    def hop(x, block):
        target = {i: i ^ 1 for i in range(blocks * devices)}
        for at, to in ((block, block - 1), (block - 1, block)):
            target[at * devices + 1] = to * devices + 1
            target.update({at * devices + i: at * devices + j for i, j in ((0, 2), (2, 3), (3, 0))})
        return lax.ppermute(x, ("tm", "state"), list(target.items()))

    incoming = [first, hop(mean, blocks - 1)]
    (x,) = call(pair_hop_kernel, "pair_hop", 4, [shape(1, order)], [VMEM] * 3, [], (incoming[-1], late_map, early_map))
    m, vec = call(block_kernel, "block", 12, [square, shape(8, order)], [VMEM] * 2, [], (late_map, early_map))
    for block in range(blocks - 2, 0, -1):
        if block < blocks - 2:
            (x,) = call(hop_kernel, "hop", 4, [shape(1, order)], [VMEM] * 3, [], (incoming[-1], m, vec))
        incoming.append(hop(x, block))
    g3 = swap(lax.optimization_barrier((gb, incoming[3]))[0], 1)

    given = list(call(
        functools.partial(last_kernel, devices),
        "last",
        8,
        [shape(steps, panel)] * devices,
        [VMEM] * (blocks + 6),
        [pltpu.VMEM((devices, steps, panel), F32)],
        (*incoming, m, vec, late_map, g3, early_map, gb),
    ))
    order_of = (*range(2, devices), 1)
    ring = {1: 2, 2: 0, 0: 3, 3: 1}
    for off in order_of:
        if off == 3:
            pairs = [(i, ring.get(i, i ^ 3)) for i in range(devices)]
            given[off] = lax.ppermute(given[off], "state", pairs)
        else:
            given[off] = swap(given[off], off)
    given = [given[0], *(given[off] for off in order_of)]
    (out,) = call(out_kernel, "out", 4, [shape(steps, panel)], [VMEM] * devices, [], given)
    return out


def solution(mesh):
    return jax.shard_map(
        local,
        mesh=mesh,
        in_specs=(
            P("tm", "state", None),
            P("tm", "state", None),
            P("state", None),
            P("tm", None),
            P(),
        ),
        out_specs=P("tm", "state"),
        check_vma=False,
    )
```
